128 devices in a mesh: gx: 16 (over z, y), gy: 8 (over x, core).
Axes of the slice: x: 4, y: 4, z: 4, core: 2. Of those that a mesh axis runs over, the one named last changes fastest.
Arguments:
- fractions: float32 [16384, 3, 128], P(('gx', 'gy')), may hold values from 0 to 1
- normals: float32 [16384, 3, 128], P(('gx', 'gy')), may hold values from -6 to 6
- point_cells: int32 [16384, 128], P(('gx', 'gy')), may hold values from 0 to 1574
- block_owner: int32 [16384, 1], P(('gx', 'gy')), may hold values from 0 to 127; in each aligned block of 128 rows (0 to 127, 128 to 255, ...) at most 2 rows name the same one
- block_tile: int32 [16384], P(('gx', 'gy')), may hold values from 0 to 127
- block_count: int32 [16384], P(('gx', 'gy')), may hold values from 1 to 128
Outputs:
- solution_field: float32 [16, 1024, 2048], P(None, 'gx', 'gy')
- residual: float32 [16, 1024, 2048], P(None, 'gx', 'gy')
The draws below stay inside these ranges and needn't reach their ends.
Inputs may be any that keep to these rules, and one draw needn't show every extreme that they name: `block_owner`: among the blocks of one device, no owner is named by more than 2 blocks.
All inputs are finite; a program needn't handle non-finite values.
Results may differ from the reference program's by a relative error of at most 0.0003.
Values sent between devices are 32-bit elements; how exact they have to be, the bound alone decides.
A program may use at most 128 MiB of HBM per device.

```python
import math
import jax
import jax.numpy as jnp
import numpy as np
from jax import lax

CX = 64
CY = 256
CZ = 16
TX = 8
TY = 16
BLOCK = 128
BLK_DEV = 128
ITERS = 3
NX = 1024
NY = 2048
BLOCKS = 16384
TILES_DEV = 128
CAP = 2
N_GX = 16
N_GY = 8
DEVICES = 128


def set_ends(entries, stream_key, low, largest):
    extent = entries.shape
    spot = [jax.random.randint(jax.random.fold_in(stream_key, axis), (), 0, extent[axis]) for axis in range(len(extent))]
    entries = entries.at[tuple(spot)].set(low)
    longest = extent.index(max(extent))
    spot[longest] = (spot[longest] + 1) % extent[longest]
    return entries.at[tuple(spot)].set(largest)


def block_scale(stream_key, extent, shards, low, high):
    def one(axis_at, shards_of):
        draws = jax.random.uniform(jax.random.fold_in(jax.random.fold_in(stream_key, 6), axis_at), (shards_of,), jnp.float32, low / len(shards), high / len(shards))
        return jnp.repeat(jnp.exp(draws), extent[axis_at] // shards_of).reshape((-1,) + (1,) * (len(extent) - axis_at - 1))

    level = one(*shards[0])
    for cut in shards[1:]:
        level = level * one(*cut)
    return level


def deal_out(own_key, own, number, rows, count, top, bound, lean):
    ranking = jax.random.permutation(own_key, count)
    packed, usual = portions_of(count, rows * top, bound, lean, True), portions_of(count, rows * top, bound, lean, False)
    places = jnp.arange(count)

    def named(lengths, turn):
        used = int((lengths > 0).sum())
        fixed = max(1, used // 4)
        passed = fixed + (places - fixed + turn * (used - fixed)) % max(1, count - fixed)
        return jnp.zeros((count,), jnp.int32).at[ranking[jnp.where(places < fixed, places, passed)]].set(jnp.asarray(lengths, jnp.int32))

    lengths = jnp.where(number % 4 == 0, named(packed, number // 4), named(usual, number - number // 4 - 1))
    mixed = jax.random.permutation(jax.random.fold_in(own, 3), count)
    donor, receiver = mixed[0:count // 2 * 2:2], mixed[1:count // 2 * 2:2]
    margin = jnp.minimum(lengths[donor] - 1, bound - lengths[receiver]) // 2
    margin = jnp.where((donor == ranking[0]) | (receiver == ranking[0]) | (lengths[receiver] == 0), 0, jnp.maximum(margin, 0))
    passed = jax.random.randint(jax.random.fold_in(own, 4), (count // 2,), 0, 1 << 20) % (margin + 1)
    lengths = lengths.at[donor].add(-passed).at[receiver].add(passed)
    items = jnp.searchsorted(jnp.cumsum(lengths), jnp.arange(rows * top), side="right").astype(jnp.int32)
    listing = items.reshape(top, rows).T
    listing = listing[jax.random.permutation(jax.random.fold_in(own, 1), rows)]
    turn = jax.random.randint(jax.random.fold_in(own, 2), (rows, 1), 0, top)
    return jnp.take_along_axis(listing, (jnp.arange(top)[None, :] + turn) % top, axis=1)


def portions_of(count, total, bound, skew, full):
    weights = [(1 << 20) // math.isqrt(rank ** skew) + 1 for rank in range(1, count + 1)]
    largest = bound if full else min(bound, max(-(-total // count), total * weights[0] // sum(weights)))
    least = 1 if total - largest >= count - 1 else 0
    counts, spare = [largest] + [least] * (count - 1), total - largest - least * (count - 1)
    while spare > 0:
        free = [i for i in range(1, count) if counts[i] < largest] or [i for i in range(1, count) if counts[i] < bound]
        pool, remaining = sum([weights[i] for i in free]), spare
        for i in free:
            extra = min(bound - counts[i], max(1, remaining * weights[i] // pool), spare)
            counts[i] = counts[i] + extra
            spare = spare - extra
    return np.array(counts)


def bell_draw(own_key, dims, width, most, split=(), kind=jnp.bfloat16):
    values = width * jax.random.normal(own_key, dims, jnp.float32)
    if split:
        values = values * block_scale(own_key, dims, split, -0.22, 0.18)
    return jnp.clip(values, -most, most).astype(kind)


def setup_inputs(seed: int = 0) -> dict:
    key_of = jax.random.split(jax.random.key(seed), 7)
    fractions = jnp.clip(1.0 * jax.random.uniform(key_of[0], (BLOCKS, 3, BLOCK), jnp.float32) ** block_scale(key_of[0], (BLOCKS, 3, BLOCK), ((0, 128),), -0.2, 0.2), 0.0, 1.0)
    normals = bell_draw(key_of[1], (BLOCKS, 3, BLOCK), 1.0, 6.0, ((0, 128),), jnp.float32)
    point_cells = set_ends(jax.random.randint(key_of[2], (BLOCKS, BLOCK), 0, (TX - 1) * (TY - 1) * (CZ - 1)), jax.random.fold_in(key_of[2], 1), 0, ((TX - 1) * (TY - 1) * (CZ - 1)) - 1).astype(jnp.int32)
    block_owner_keys = jax.random.split(jax.random.fold_in(key_of[3], 1), BLOCKS // BLK_DEV)
    block_owner_turns = jax.random.permutation(jax.random.fold_in(key_of[3], 3), BLOCKS // BLK_DEV)
    block_owner = jax.vmap(lambda own, number: deal_out(jax.random.fold_in(key_of[3], 2), own, number, BLK_DEV, DEVICES, 1, CAP, 2))(block_owner_keys, block_owner_turns).reshape((BLOCKS, 1))
    block_tile = set_ends(jax.random.randint(key_of[4], (BLOCKS,), 0, TILES_DEV), jax.random.fold_in(key_of[4], 1), 0, TILES_DEV - 1).astype(jnp.int32)
    block_count = set_ends(jax.random.randint(key_of[5], (BLOCKS,), 1, BLOCK + 1), jax.random.fold_in(key_of[5], 1), 1, BLOCK).astype(jnp.int32)
    return dict(fractions=fractions, normals=normals, point_cells=point_cells, block_owner=block_owner, block_tile=block_tile, block_count=block_count)


screen_weight = 4.0


def spline_taps(anchor, offsets, length):
    places = jnp.arange(length, dtype=jnp.int32)
    lower = (places[None, :] == anchor[:, None]).astype(jnp.float32)
    upper = (places[None, :] == anchor[:, None] + 1).astype(jnp.float32)
    return lower * (1.0 - offsets[:, None]) + upper * offsets[:, None], upper - lower


def splat_block(fractions, normals, cells, count):
    points = cells.shape[0]
    valid = (jnp.arange(points, dtype=jnp.int32) < count).astype(jnp.float32)
    plane = cells % (CZ - 1)
    remains = cells // (CZ - 1)
    column = remains % (TY - 1)
    row_index = remains // (TY - 1)
    weight_x, slope_x = spline_taps(row_index, fractions[0], TX)
    weight_y, slope_y = spline_taps(column, fractions[1], TY)
    weight_z, slope_z = spline_taps(plane, fractions[2], CZ)

    def outer_pair(first, second):
        return (first[:, :, None] * second[:, None, :]).reshape(points, CZ * TX)

    shared = outer_pair(weight_z, weight_x)
    left = jnp.concatenate([
        (normals[0] * valid)[:, None] * outer_pair(weight_z, slope_x),
        (normals[1] * valid)[:, None] * shared,
        (normals[2] * valid)[:, None] * outer_pair(slope_z, weight_x)], axis=0)
    right = jnp.concatenate([weight_y, slope_y, weight_y], axis=0)
    source = jnp.dot(left.T, right, precision=lax.Precision.HIGHEST, preferred_element_type=jnp.float32)
    density = jnp.dot((valid[:, None] * shared).T, weight_y, precision=lax.Precision.HIGHEST, preferred_element_type=jnp.float32)
    return jnp.stack([source, density])


def box_sum(padded):
    total = padded[:-2] + padded[1:-1] + padded[2:]
    total = total[:, :-2] + total[:, 1:-1] + total[:, 2:]
    return total[:, :, :-2] + total[:, :, 1:-1] + total[:, :, 2:]


def reference(fractions, normals, point_cells, block_owner, block_tile, block_count):
    tiles = lax.map(lambda items: splat_block(*items), (fractions, normals, point_cells, block_count), batch_size=64)
    owner = block_owner[:, 0]
    across_x = owner // N_GY
    across_y = owner % N_GY
    tiles_x = CX // TX
    tiles_y = CY // TY
    global_tile = ((across_x * tiles_x + block_tile // tiles_y) * (N_GY * tiles_y)
                   + across_y * tiles_y + block_tile % tiles_y).astype(jnp.int32)
    summed = jax.ops.segment_sum(tiles, global_tile, num_segments=N_GX * tiles_x * N_GY * tiles_y)
    fields = summed.reshape(N_GX * tiles_x, N_GY * tiles_y, 2, CZ, TX, TY)
    fields = fields.transpose(2, 3, 0, 4, 1, 5).reshape(2, CZ, NX, NY)
    source = fields[0]
    diagonal = 6.5 + screen_weight * fields[1]

    def operate(field):
        return diagonal * field - 0.25 * (box_sum(jnp.pad(field, 1)) - field)

    solution_field = jnp.zeros_like(source)
    residual = source
    direction = source
    norm_now = jnp.sum(residual * residual)
    for turn in range(ITERS):
        image = operate(direction)
        alpha = norm_now / jnp.sum(direction * image)
        solution_field = solution_field + alpha * direction
        residual = residual - alpha * image
        norm_next = jnp.sum(residual * residual)
        direction = residual + (norm_next / norm_now) * direction
        norm_now = norm_next
    return solution_field, residual
```

```python
import jax
import jax.numpy as jnp
from jax import lax
from jax.experimental import pallas as pl
from jax.experimental.pallas import tpu as pltpu
from jax.sharding import PartitionSpec as P

CX = 64
CY = 256
CZ = 16
TX = 8
TY = 16
POINTS = 128
ITERS = 3
LANES = 128
GROUP = 4

screen_weight = 4.0
MESH = pl.DeviceIdType.MESH


def arrange_kernel(slot_ref, tile_ref, count_ref, frac_ref, norm_ref, cell_ref, out_ref):
    blocks = frac_ref.shape[0]
    lane = lax.broadcasted_iota(jnp.int32, (1, LANES), 1)
    out_ref[...] = jnp.zeros_like(out_ref)

    def place(k, carry):
        slot = slot_ref[k]
        out_ref[slot, 0:3, :] = frac_ref[k]
        out_ref[slot, 3:6, :] = norm_ref[k]
        out_ref[slot, 6:7, :] = cell_ref[pl.ds(k, 1), :].astype(jnp.float32)
        header = jnp.where(lane == 0, tile_ref[k], jnp.where(lane == 1, count_ref[k], 0))
        out_ref[slot, 7:8, :] = header.astype(jnp.float32)
        return carry

    lax.fori_loop(0, blocks, place, 0)


def arrange(slot, tile, count, fractions, normals, cells, slots):
    smem = pl.BlockSpec(memory_space=pltpu.SMEM)
    vmem = pl.BlockSpec(memory_space=pltpu.VMEM)
    return pl.pallas_call(
        arrange_kernel,
        out_shape=jax.ShapeDtypeStruct((slots, 8, LANES), jnp.float32),
        in_specs=[smem, smem, smem, vmem, vmem, vmem],
        out_specs=vmem,
        compiler_params=pltpu.CompilerParams(vmem_limit_bytes=16 << 20),
    )(slot, tile, count, fractions, normals, cells)


def split(value):
    high = value.astype(jnp.bfloat16)
    return high, (value - high.astype(jnp.float32)).astype(jnp.bfloat16)


def taps(anchor, offset, length):
    place = lax.broadcasted_iota(jnp.int32, (length, POINTS), 0).astype(jnp.float32)
    lower = place == anchor
    upper = place == anchor + 1.0
    weight = jnp.where(lower, 1.0 - offset, jnp.where(upper, offset, 0.0))
    slope = jnp.where(lower, -1.0, jnp.where(upper, 1.0, 0.0))
    return weight, slope


def splat_tile(block, count):
    lane = lax.broadcasted_iota(jnp.int32, (1, POINTS), 1)
    valid = lane < count
    cell = block[6:7]
    remains = jnp.floor((cell + 0.5) * (1.0 / (CZ - 1)))
    plane = cell - remains * (CZ - 1)
    row = jnp.floor((remains + 0.5) * (1.0 / (TY - 1)))
    column = remains - row * (TY - 1)
    row = jnp.where(valid, row, -4.0)
    wx, sx = taps(row, block[0:1], TX)
    wy, sy = taps(column, block[1:2], TY)
    wz, sz = taps(plane, block[2:3], CZ)
    sx = sx * block[3:4]
    sy = sy * block[4:5]
    tx = wx * block[5:6]
    first = jnp.concatenate(
        [wz[z : z + 1] * sx + sz[z : z + 1] * tx for z in range(CZ)], axis=0
    )
    second = jnp.concatenate([wz[z : z + 1] * wx for z in range(CZ)], axis=0)
    big = jnp.concatenate([first, second], axis=1)
    top = jnp.concatenate([wy, sy], axis=1)
    low = jnp.concatenate([jnp.zeros_like(wy), wy], axis=1)
    small = jnp.concatenate([top, low], axis=0)
    big_high, big_low = split(big)
    small_high, small_low = split(small)
    dims = (((1,), (1,)), ((), ()))
    both = lax.dot_general(
        jnp.concatenate([small_high, small_low], axis=0),
        big_high,
        dims,
        preferred_element_type=jnp.float32,
    )
    rest = lax.dot_general(small_high, big_low, dims, preferred_element_type=jnp.float32)
    return both[: 2 * TY] + both[2 * TY :] + rest


def splat_kernel(tile_ref, count_ref, blocks_ref, acc_ref, order):
    slots = blocks_ref.shape[0]
    acc_ref[...] = jnp.zeros_like(acc_ref)

    def gather(i, carry):
        used, empty = carry
        some = count_ref[i] > 0

        @pl.when(some)
        def _():
            order[used] = i

        return used + some.astype(jnp.int32), jnp.where(some, empty, i)

    used, empty = lax.fori_loop(0, slots, gather, (jnp.int32(0), jnp.int32(0)))
    for extra in range(GROUP):
        order[used + extra] = empty

    def work(j, carry):
        made = []
        for u in range(GROUP):
            slot = order[j * GROUP + u]
            made.append((tile_ref[slot], splat_tile(blocks_ref[slot], count_ref[slot])))
        tiles_y = CY // TY
        for tile, values in made:
            x = tile // tiles_y
            y = pl.multiple_of((tile % tiles_y) * TY, TY)
            acc_ref[x, 0, pl.ds(y, TY), :] += values[:TY]
            acc_ref[x, 1, pl.ds(y, TY), :] += values[TY:]
        return carry

    lax.fori_loop(0, (used + GROUP - 1) // GROUP, work, 0)


def splat(tile, count, blocks):
    slots = blocks.shape[0]
    smem = pl.BlockSpec(memory_space=pltpu.SMEM)
    vmem = pl.BlockSpec(memory_space=pltpu.VMEM)
    return pl.pallas_call(
        splat_kernel,
        out_shape=jax.ShapeDtypeStruct((CX // TX, 2, CY, CZ * TX), jnp.float32),
        in_specs=[smem, smem, vmem],
        out_specs=vmem,
        scratch_shapes=[pltpu.SMEM((slots + GROUP,), jnp.int32)],
        compiler_params=pltpu.CompilerParams(vmem_limit_bytes=24 << 20),
    )(tile, count, blocks)


def fold(value):
    total = value[0:8]
    for k in range(1, value.shape[0] // 8):
        total = total + value[8 * k : 8 * k + 8]
    return total


def solve_kernel(
    count_x, count_y,
    acc_ref, x_ref, r_ref,
    rp, dg, p, s, w, rim,
    row_out, row_in, col_out, col_in, part_y, part_x, got_y, got_x,
    row_s, row_r, col_s, col_r, y_s, y_r, x_s, x_r,
):
    me_x, me_y = lax.axis_index("gx"), lax.axis_index("gy")

    def at(dx, dy):
        return (lax.rem(me_x + dx + count_x, count_x), lax.rem(me_y + dy + count_y, count_y))

    barrier = pltpu.get_barrier_semaphore()

    def greet_y(d, carry):
        pl.semaphore_signal(barrier, inc=1, device_id=at(0, d), device_id_type=MESH)
        return carry

    def greet_x(d, carry):
        pl.semaphore_signal(barrier, inc=1, device_id=at(d, 0), device_id_type=MESH)
        return carry

    lax.fori_loop(1, count_y, greet_y, 0)
    lax.fori_loop(1, count_x, greet_x, 0)
    for dx in (-1, 1):
        for dy in (-1, 1):
            pl.semaphore_signal(barrier, inc=1, device_id=at(dx, dy), device_id_type=MESH)

    sub8 = lax.broadcasted_iota(jnp.int32, (8, LANES), 0)
    lane8 = lax.broadcasted_iota(jnp.int32, (8, LANES), 1)
    lane_half = lax.broadcasted_iota(jnp.int32, (CX, LANES), 1)
    row_half = lax.broadcasted_iota(jnp.int32, (CX, LANES), 0)

    rp[0] = jnp.zeros((CX, CY), jnp.float32)
    rp[CZ + 1] = jnp.zeros((CX, CY), jnp.float32)

    def unfold(t, carry):
        rows = pl.ds(pl.multiple_of(t * TX, TX), TX)
        source = acc_ref[t, 0].T.reshape(CZ, TX, CY)
        density = acc_ref[t, 1].T.reshape(CZ, TX, CY)
        rp[1 : CZ + 1, rows, :] = source
        dg[:, rows, :] = 6.75 + screen_weight * density
        return carry

    lax.fori_loop(0, CX // TX, unfold, 0)

    def clear(z, carry):
        zero = jnp.zeros((CX, CY), jnp.float32)
        p[z] = zero
        s[z] = zero
        x_ref[z] = zero
        return carry

    lax.fori_loop(0, CZ, clear, 0)
    pl.semaphore_wait(barrier, (count_y - 1) + (count_x - 1) + 4)

    def pack(z, carry):
        west, east = carry
        for t in range(CX // TX):
            here = rp[z + 1, 8 * t : 8 * t + 8, :]
            shift = z + CZ * t
            mine = lane8 == shift
            west = jnp.where(mine, pltpu.roll(here[:, :LANES], shift, 1), west)
            turned = pltpu.roll(here[:, LANES:], lax.rem(shift + 1, LANES), 1)
            east = jnp.where(mine, turned, east)
        return west, east

    def ask(count, target, src, dst, send, recv):
        pltpu.make_async_remote_copy(
            src_ref=src, dst_ref=dst, send_sem=send, recv_sem=recv,
            device_id=target, device_id_type=MESH,
        ).start()

    def wait_for(ref, sem):
        pltpu.make_async_copy(ref, ref, sem).wait()

    zero8 = jnp.zeros((8, LANES), jnp.float32)

    def total_of(parts):
        total = parts[0]
        for k in range(1, parts.shape[0]):
            total = total + parts[k]
        return total

    def turn(it, carry):
        gamma_old, curve_old = carry
        row_out[it, 0] = rp[1 : CZ + 1, 0, :]
        row_out[it, 1] = rp[1 : CZ + 1, CX - 1, :]
        ask(0, at(-1, 0), row_out.at[it, 0], row_in.at[it, 1], row_s.at[it], row_r.at[it])
        ask(0, at(1, 0), row_out.at[it, 1], row_in.at[it, 0], row_s.at[it], row_r.at[it])
        west, east = lax.fori_loop(0, CZ, pack, (zero8, zero8))
        col_out[it, 0] = west
        col_out[it, 1] = east
        for dx in (-1, 0, 1):
            ask(0, at(dx, -1), col_out.at[it, 0], col_in.at[it, 1, 1 - dx], col_s.at[it], col_r.at[it])
            ask(0, at(dx, 1), col_out.at[it, 1], col_in.at[it, 0, 1 - dx], col_s.at[it], col_r.at[it])

        wait_for(row_in.at[it], row_r.at[it])
        zrow = lax.broadcasted_iota(jnp.int32, (CZ, CY), 0)
        for side, there in ((0, me_x > 0), (1, me_x < count_x - 1)):
            near = row_in[it, side]
            near = (
                near
                + jnp.where(zrow > 0, pltpu.roll(near, 1, 0), 0.0)
                + jnp.where(zrow < CZ - 1, pltpu.roll(near, CZ - 1, 0), 0.0)
            )
            near = jnp.where(there, near, 0.0)
            rim[side, 0] = near[:, :LANES]
            rim[side, 1] = near[:, LANES:]
        wait_for(col_in.at[it], col_r.at[it])

        plane8 = lax.rem(lane8, CZ)

        def column(side, there):
            def summed(k, ok):
                col = col_in[it, side, k]
                col = (
                    col
                    + jnp.where(plane8 > 0, pltpu.roll(col, 1, 1), 0.0)
                    + jnp.where(plane8 < CZ - 1, pltpu.roll(col, LANES - 1, 1), 0.0)
                )
                return jnp.where(ok, col, 0.0)

            mid = summed(1, there)
            low = summed(0, jnp.logical_and(there, me_x > 0))
            high = summed(2, jnp.logical_and(there, me_x < count_x - 1))

            def down(v):
                return pltpu.roll(v, 1, 0)

            def up(v):
                return pltpu.roll(v, 7, 0)

            before = jnp.where(lane8 < CZ, pltpu.roll(down(low), CZ, 1), pltpu.roll(down(mid), CZ, 1))
            before = jnp.where(sub8 == 0, before, down(mid))
            after = jnp.where(
                lane8 >= LANES - CZ,
                pltpu.roll(up(high), LANES - CZ, 1),
                pltpu.roll(up(mid), LANES - CZ, 1),
            )
            after = jnp.where(sub8 == 7, after, up(mid))
            return before + mid + after

        west_in = column(0, me_y > 0)
        east_in = column(1, me_y < count_y - 1)

        def apply(z, sums):
            gamma, delta, eta = sums
            halves = []
            for h in range(2):
                cols = slice(h * LANES, (h + 1) * LANES)
                u = rp[z, :, cols] + rp[z + 1, :, cols] + rp[z + 2, :, cols]
                above = rim[0, h, pl.ds(z, 1), :]
                below = rim[1, h, pl.ds(z, 1), :]
                t = (
                    u
                    + jnp.where(row_half == 0, above, pltpu.roll(u, 1, 0))
                    + jnp.where(row_half == CX - 1, below, pltpu.roll(u, CX - 1, 0))
                )
                halves.append(t)
            left, right = halves
            back = lax.rem(2 * LANES - z, LANES)
            west_col = jnp.concatenate(
                [pltpu.roll(west_in, lax.rem(back + LANES - CZ * t, LANES), 1) for t in range(CX // TX)],
                axis=0,
            )
            east_col = jnp.concatenate(
                [pltpu.roll(east_in, lax.rem(back + 2 * LANES - 1 - CZ * t, LANES), 1) for t in range(CX // TX)],
                axis=0,
            )
            lr, rr = pltpu.roll(left, 1, 1), pltpu.roll(right, 1, 1)
            ll, rl = pltpu.roll(left, LANES - 1, 1), pltpu.roll(right, LANES - 1, 1)
            first, last = lane_half == 0, lane_half == LANES - 1
            box_left = left + jnp.where(first, west_col, lr) + jnp.where(last, rl, ll)
            box_right = right + jnp.where(first, lr, rr) + jnp.where(last, east_col, rl)
            for h, box in ((0, box_left), (1, box_right)):
                cols = slice(h * LANES, (h + 1) * LANES)
                v = rp[z + 1, :, cols]
                image = dg[z, :, cols] * v - 0.25 * box
                w[z, :, cols] = image
                gamma = gamma + fold(v * v)
                delta = delta + fold(v * image)
                eta = eta + fold(v * s[z, :, cols])
            return gamma, delta, eta

        gamma, delta, eta = lax.fori_loop(0, CZ, apply, (zero8, zero8, zero8))
        gamma = jnp.sum(gamma, axis=0, keepdims=True)
        delta = jnp.sum(delta, axis=0, keepdims=True)
        eta = jnp.sum(eta, axis=0, keepdims=True)
        mine = jnp.where(sub8 == 0, gamma, jnp.where(sub8 == 1, delta, jnp.where(sub8 == 2, eta, 0.0)))
        part_y[it] = mine
        got_y[it, me_y] = mine

        def send_y(d, c):
            ask(0, at(0, d), part_y.at[it], got_y.at[it, me_y], y_s.at[it], y_r.at[it])
            return c

        lax.fori_loop(1, count_y, send_y, 0)
        wait_for(got_y.at[it, pl.ds(0, count_y - 1)], y_r.at[it])
        mine = total_of(got_y.at[it])
        part_x[it] = mine
        got_x[it, me_x] = mine

        def send_x(d, c):
            ask(0, at(d, 0), part_x.at[it], got_x.at[it, me_x], x_s.at[it], x_r.at[it])
            return c

        lax.fori_loop(1, count_x, send_x, 0)
        wait_for(got_x.at[it, pl.ds(0, count_x - 1)], x_r.at[it])
        total = jnp.sum(total_of(got_x.at[it]), axis=1, keepdims=True)
        gamma, delta, eta = total[0:1], total[1:2], total[2:3]
        beta = jnp.where(it == 0, 0.0, gamma / gamma_old)
        curve = delta + 2.0 * beta * eta + beta * beta * curve_old
        alpha = gamma / curve

        def update(z, c):
            r = rp[z + 1]
            pn = r + beta * p[z]
            sn = w[z] + beta * s[z]
            p[z] = pn
            s[z] = sn
            x_ref[z] = x_ref[z] + alpha * pn
            r = r - alpha * sn
            rp[z + 1] = r
            r_ref[z] = r
            return c

        lax.fori_loop(0, CZ, update, 0)
        return gamma, curve

    one = jnp.ones((1, 1), jnp.float32)
    lax.fori_loop(0, ITERS, turn, (one, 0.0 * one))

    def finish(it, c):
        wait_for(row_out.at[it], row_s.at[it])
        wait_for(col_in.at[it], col_s.at[it])
        wait_for(got_y.at[it, pl.ds(0, count_y - 1)], y_s.at[it])
        wait_for(got_x.at[it, pl.ds(0, count_x - 1)], x_s.at[it])
        return c

    lax.fori_loop(0, ITERS, finish, 0)


def solve(acc, count_x, count_y):
    vmem = pl.BlockSpec(memory_space=pltpu.VMEM)
    field = jax.ShapeDtypeStruct((CZ, CX, CY), jnp.float32)
    cells = (CZ, CX, CY)

    def kernel(*refs):
        solve_kernel(count_x, count_y, *refs)

    return pl.pallas_call(
        kernel,
        out_shape=(field, field),
        in_specs=[vmem],
        out_specs=(vmem, vmem),
        scratch_shapes=[
            pltpu.VMEM((CZ + 2, CX, CY), jnp.float32),
            pltpu.VMEM(cells, jnp.float32),
            pltpu.VMEM(cells, jnp.float32),
            pltpu.VMEM(cells, jnp.float32),
            pltpu.VMEM(cells, jnp.float32),
            pltpu.VMEM((2, 2, CZ, LANES), jnp.float32),
            pltpu.VMEM((ITERS, 2, CZ, CY), jnp.float32),
            pltpu.VMEM((ITERS, 2, CZ, CY), jnp.float32),
            pltpu.VMEM((ITERS, 2, 8, LANES), jnp.float32),
            pltpu.VMEM((ITERS, 2, 3, 8, LANES), jnp.float32),
            pltpu.VMEM((ITERS, 8, LANES), jnp.float32),
            pltpu.VMEM((ITERS, 8, LANES), jnp.float32),
            pltpu.VMEM((ITERS, count_y, 8, LANES), jnp.float32),
            pltpu.VMEM((ITERS, count_x, 8, LANES), jnp.float32),
        ]
        + [pltpu.SemaphoreType.DMA((ITERS,))] * 8,
        compiler_params=pltpu.CompilerParams(
            collective_id=0, has_side_effects=True, vmem_limit_bytes=32 << 20
        ),
    )(acc)


def local(fractions, normals, point_cells, block_owner, block_tile, block_count):
    count_x, count_y = lax.axis_size("gx"), lax.axis_size("gy")
    devices = count_x * count_y
    blocks = fractions.shape[0]
    capacity = 2 * blocks // devices
    owner = block_owner[:, 0]
    index = jnp.arange(blocks, dtype=jnp.int32)
    earlier = (owner[:, None] == owner[None, :]) & (index[None, :] < index[:, None])
    slot = owner * capacity + jnp.sum(earlier.astype(jnp.int32), axis=1)
    packed = arrange(
        slot, block_tile, block_count, fractions, normals, point_cells, devices * capacity
    )
    packed = packed.reshape(devices, capacity, 8, POINTS)
    got = lax.all_to_all(packed, ("gx", "gy"), split_axis=0, concat_axis=0, tiled=True)
    got = got.reshape(devices * capacity, 8, POINTS)
    header = got[:, 7, :2].astype(jnp.int32)
    acc = splat(header[:, 0], header[:, 1], got)
    return solve(acc, count_x, count_y)


def solution(mesh):
    placed = (
        P(("gx", "gy"), None, None),
        P(("gx", "gy"), None, None),
        P(("gx", "gy"), None),
        P(("gx", "gy"), None),
        P(("gx", "gy")),
        P(("gx", "gy")),
    )
    return jax.shard_map(
        local,
        mesh=mesh,
        in_specs=placed,
        out_specs=(P(None, "gx", "gy"), P(None, "gx", "gy")),
        check_vma=False,
    )
```

```python
import jax
import jax.numpy as jnp
from jax import lax
from jax.experimental import pallas as pl
from jax.experimental.pallas import tpu as pltpu
from jax.sharding import PartitionSpec as P

CX = 64
CY = 256
CZ = 16
TX = 8
TY = 16
POINTS = 128
ITERS = 3
LANES = 128
GROUP = 16
SHIFT = 6.5
TRUST = 100.0

screen_weight = 4.0
MESH = pl.DeviceIdType.MESH


def arrange_kernel(slot_ref, tile_ref, count_ref, frac_ref, norm_ref, cell_ref, out_ref):
    blocks = frac_ref.shape[0]
    lane = lax.broadcasted_iota(jnp.int32, (1, LANES), 1)
    out_ref[...] = jnp.zeros_like(out_ref)

    def place(k, carry):
        slot = slot_ref[k]
        out_ref[slot, 0:3, :] = frac_ref[k]
        out_ref[slot, 3:6, :] = norm_ref[k]
        out_ref[slot, 6:7, :] = cell_ref[pl.ds(k, 1), :].astype(jnp.float32)
        header = jnp.where(lane == 0, tile_ref[k], jnp.where(lane == 1, count_ref[k], 0))
        out_ref[slot, 7:8, :] = header.astype(jnp.float32)
        return carry

    lax.fori_loop(0, blocks, place, 0)


def arrange(slot, tile, count, fractions, normals, cells, slots):
    smem = pl.BlockSpec(memory_space=pltpu.SMEM)
    vmem = pl.BlockSpec(memory_space=pltpu.VMEM)
    return pl.pallas_call(
        arrange_kernel,
        out_shape=jax.ShapeDtypeStruct((slots, 8, LANES), jnp.float32),
        in_specs=[smem, smem, smem, vmem, vmem, vmem],
        out_specs=vmem,
        compiler_params=pltpu.CompilerParams(vmem_limit_bytes=16 << 20),
    )(slot, tile, count, fractions, normals, cells)


def split(value):
    high = value.astype(jnp.bfloat16)
    return high, (value - high.astype(jnp.float32)).astype(jnp.bfloat16)


def taps(anchor, offset, length):
    place = lax.broadcasted_iota(jnp.int32, (length, POINTS), 0).astype(jnp.float32)
    lower = place == anchor
    upper = place == anchor + 1.0
    weight = jnp.where(lower, 1.0 - offset, jnp.where(upper, offset, 0.0))
    slope = jnp.where(lower, -1.0, jnp.where(upper, 1.0, 0.0))
    return weight, slope


def splat_tile(block, count):
    lane = lax.broadcasted_iota(jnp.int32, (1, POINTS), 1)
    valid = lane < count
    cell = block[6:7]
    remains = jnp.floor((cell + 0.5) * (1.0 / (CZ - 1)))
    plane = cell - remains * (CZ - 1)
    row = jnp.floor((remains + 0.5) * (1.0 / (TY - 1)))
    column = remains - row * (TY - 1)
    row = jnp.where(valid, row, -4.0)
    wx, sx = taps(row, block[0:1], TX)
    wy, sy = taps(column, block[1:2], TY)
    wz, sz = taps(plane, block[2:3], CZ)
    sx = sx * block[3:4]
    sy = sy * block[4:5]
    tx = wx * block[5:6]
    first = jnp.concatenate(
        [wz[z : z + 1] * sx + sz[z : z + 1] * tx for z in range(CZ)], axis=0
    )
    second = jnp.concatenate([wz[z : z + 1] * wx for z in range(CZ)], axis=0)
    big = jnp.concatenate([first, second], axis=1)
    top = jnp.concatenate([wy, sy], axis=1)
    low = jnp.concatenate([jnp.zeros_like(wy), wy], axis=1)
    small = jnp.concatenate([top, low], axis=0)
    big_high, big_low = split(big)
    small_high, small_low = split(small)
    dims = (((1,), (1,)), ((), ()))
    both = lax.dot_general(
        jnp.concatenate([small_high, small_low], axis=0),
        big_high,
        dims,
        preferred_element_type=jnp.float32,
    )
    rest = lax.dot_general(small_high, big_low, dims, preferred_element_type=jnp.float32)
    return both[: 2 * TY] + both[2 * TY :] + rest


def splat_kernel(tile_ref, count_ref, blocks_ref, acc_ref, order):
    slots = blocks_ref.shape[0]
    acc_ref[...] = jnp.zeros_like(acc_ref)

    def gather(i, carry):
        used, empty = carry
        some = count_ref[i] > 0
        order[used] = i
        return used + some.astype(jnp.int32), jnp.where(some, empty, i)

    used, empty = lax.fori_loop(
        0, slots, gather, (jnp.int32(0), jnp.int32(0)), unroll=8
    )
    for extra in range(GROUP):
        order[used + extra] = empty

    def work(j, carry):
        made = []
        for u in range(GROUP):
            slot = order[j * GROUP + u]
            made.append((tile_ref[slot], splat_tile(blocks_ref[slot], count_ref[slot])))
        tiles_y = CY // TY
        for tile, values in made:
            x = tile // tiles_y
            y = pl.multiple_of((tile % tiles_y) * TY, TY)
            acc_ref[x, 0, pl.ds(y, TY), :] += values[:TY]
            acc_ref[x, 1, pl.ds(y, TY), :] += values[TY:]
        return carry

    lax.fori_loop(0, (used + GROUP - 1) // GROUP, work, 0)


def splat(tile, count, blocks):
    slots = blocks.shape[0]
    smem = pl.BlockSpec(memory_space=pltpu.SMEM)
    vmem = pl.BlockSpec(memory_space=pltpu.VMEM)
    return pl.pallas_call(
        splat_kernel,
        out_shape=jax.ShapeDtypeStruct((CX // TX, 2, CY, CZ * TX), jnp.float32),
        in_specs=[smem, smem, vmem],
        out_specs=vmem,
        scratch_shapes=[pltpu.SMEM((slots + GROUP,), jnp.int32)],
        compiler_params=pltpu.CompilerParams(vmem_limit_bytes=24 << 20),
    )(tile, count, blocks)


def fold(value):
    total = value[0:8]
    for k in range(1, value.shape[0] // 8):
        total = total + value[8 * k : 8 * k + 8]
    return total


def solve_kernel(
    count_x, count_y,
    acc_ref, x_ref, r_ref,
    rp, dg, p, s, w, rim,
    row_out, row_in, col_out, col_in, part_y, part_x, got_y, got_x,
    row_s, row_r, col_s, col_r, y_s, y_r, x_s, x_r,
):
    me_x, me_y = lax.axis_index("gx"), lax.axis_index("gy")

    def at(dx, dy):
        return (lax.rem(me_x + dx + count_x, count_x), lax.rem(me_y + dy + count_y, count_y))

    barrier = pltpu.get_barrier_semaphore()

    def greet_y(d, carry):
        pl.semaphore_signal(barrier, inc=1, device_id=at(0, d), device_id_type=MESH)
        return carry

    def greet_x(d, carry):
        pl.semaphore_signal(barrier, inc=1, device_id=at(d, 0), device_id_type=MESH)
        return carry

    lax.fori_loop(1, count_y, greet_y, 0)
    lax.fori_loop(1, count_x, greet_x, 0)
    for dx in (-1, 1):
        for dy in (-1, 1):
            pl.semaphore_signal(barrier, inc=1, device_id=at(dx, dy), device_id_type=MESH)

    sub8 = lax.broadcasted_iota(jnp.int32, (8, LANES), 0)
    lane8 = lax.broadcasted_iota(jnp.int32, (8, LANES), 1)
    lane_half = lax.broadcasted_iota(jnp.int32, (CX, LANES), 1)
    row_half = lax.broadcasted_iota(jnp.int32, (CX, LANES), 0)

    rp[0] = jnp.zeros((CX, CY), jnp.float32)
    rp[CZ + 1] = jnp.zeros((CX, CY), jnp.float32)

    def unfold(t, carry):
        rows = pl.ds(pl.multiple_of(t * TX, TX), TX)
        source = acc_ref[t, 0].T.reshape(CZ, TX, CY)
        density = acc_ref[t, 1].T.reshape(CZ, TX, CY)
        rp[1 : CZ + 1, rows, :] = source
        dg[:, rows, :] = 6.75 + screen_weight * density
        return carry

    lax.fori_loop(0, CX // TX, unfold, 0)

    def clear(z, carry):
        zero = jnp.zeros((CX, CY), jnp.float32)
        p[z] = zero
        s[z] = zero
        x_ref[z] = zero
        return carry

    lax.fori_loop(0, CZ, clear, 0)
    pl.semaphore_wait(barrier, (count_y - 1) + (count_x - 1) + 4)

    def pack(z, carry):
        west, east = carry
        for t in range(CX // TX):
            here = rp[z + 1, 8 * t : 8 * t + 8, :]
            shift = z + CZ * t
            mine = lane8 == shift
            west = jnp.where(mine, pltpu.roll(here[:, :LANES], shift, 1), west)
            turned = pltpu.roll(here[:, LANES:], lax.rem(shift + 1, LANES), 1)
            east = jnp.where(mine, turned, east)
        return west, east

    def ask(count, target, src, dst, send, recv):
        pltpu.make_async_remote_copy(
            src_ref=src, dst_ref=dst, send_sem=send, recv_sem=recv,
            device_id=target, device_id_type=MESH,
        ).start()

    def wait_for(ref, sem):
        pltpu.make_async_copy(ref, ref, sem).wait()

    zero8 = jnp.zeros((8, LANES), jnp.float32)

    def total_of(parts):
        total = parts[0]
        for k in range(1, parts.shape[0]):
            total = total + parts[k]
        return total

    def turn(it, carry):
        gamma_old, curve_old = carry
        row_out[it, 0] = rp[1 : CZ + 1, 0, :]
        row_out[it, 1] = rp[1 : CZ + 1, CX - 1, :]
        ask(0, at(-1, 0), row_out.at[it, 0], row_in.at[it, 1], row_s.at[it], row_r.at[it])
        ask(0, at(1, 0), row_out.at[it, 1], row_in.at[it, 0], row_s.at[it], row_r.at[it])
        west, east = lax.fori_loop(0, CZ, pack, (zero8, zero8))
        col_out[it, 0] = west
        col_out[it, 1] = east
        for dx in (-1, 0, 1):
            ask(0, at(dx, -1), col_out.at[it, 0], col_in.at[it, 1, 1 - dx], col_s.at[it], col_r.at[it])
            ask(0, at(dx, 1), col_out.at[it, 1], col_in.at[it, 0, 1 - dx], col_s.at[it], col_r.at[it])

        wait_for(row_in.at[it], row_r.at[it])
        zrow = lax.broadcasted_iota(jnp.int32, (CZ, CY), 0)
        for side, there in ((0, me_x > 0), (1, me_x < count_x - 1)):
            near = row_in[it, side]
            near = (
                near
                + jnp.where(zrow > 0, pltpu.roll(near, 1, 0), 0.0)
                + jnp.where(zrow < CZ - 1, pltpu.roll(near, CZ - 1, 0), 0.0)
            )
            near = jnp.where(there, near, 0.0)
            rim[side, 0] = near[:, :LANES]
            rim[side, 1] = near[:, LANES:]
        wait_for(col_in.at[it], col_r.at[it])

        plane8 = lax.rem(lane8, CZ)

        def column(side, there):
            def summed(k, ok):
                col = col_in[it, side, k]
                col = (
                    col
                    + jnp.where(plane8 > 0, pltpu.roll(col, 1, 1), 0.0)
                    + jnp.where(plane8 < CZ - 1, pltpu.roll(col, LANES - 1, 1), 0.0)
                )
                return jnp.where(ok, col, 0.0)

            mid = summed(1, there)
            low = summed(0, jnp.logical_and(there, me_x > 0))
            high = summed(2, jnp.logical_and(there, me_x < count_x - 1))

            def down(v):
                return pltpu.roll(v, 1, 0)

            def up(v):
                return pltpu.roll(v, 7, 0)

            before = jnp.where(lane8 < CZ, pltpu.roll(down(low), CZ, 1), pltpu.roll(down(mid), CZ, 1))
            before = jnp.where(sub8 == 0, before, down(mid))
            after = jnp.where(
                lane8 >= LANES - CZ,
                pltpu.roll(up(high), LANES - CZ, 1),
                pltpu.roll(up(mid), LANES - CZ, 1),
            )
            after = jnp.where(sub8 == 7, after, up(mid))
            return before + mid + after

        west_in = column(0, me_y > 0)
        east_in = column(1, me_y < count_y - 1)

        def apply(z, sums):
            gamma, delta, eta = sums
            halves = []
            for h in range(2):
                cols = slice(h * LANES, (h + 1) * LANES)
                u = rp[z, :, cols] + rp[z + 1, :, cols] + rp[z + 2, :, cols]
                above = rim[0, h, pl.ds(z, 1), :]
                below = rim[1, h, pl.ds(z, 1), :]
                t = (
                    u
                    + jnp.where(row_half == 0, above, pltpu.roll(u, 1, 0))
                    + jnp.where(row_half == CX - 1, below, pltpu.roll(u, CX - 1, 0))
                )
                halves.append(t)
            left, right = halves
            back = lax.rem(2 * LANES - z, LANES)
            west_col = jnp.concatenate(
                [pltpu.roll(west_in, lax.rem(back + LANES - CZ * t, LANES), 1) for t in range(CX // TX)],
                axis=0,
            )
            east_col = jnp.concatenate(
                [pltpu.roll(east_in, lax.rem(back + 2 * LANES - 1 - CZ * t, LANES), 1) for t in range(CX // TX)],
                axis=0,
            )
            lr, rr = pltpu.roll(left, 1, 1), pltpu.roll(right, 1, 1)
            ll, rl = pltpu.roll(left, LANES - 1, 1), pltpu.roll(right, LANES - 1, 1)
            first, last = lane_half == 0, lane_half == LANES - 1
            box_left = left + jnp.where(first, west_col, lr) + jnp.where(last, rl, ll)
            box_right = right + jnp.where(first, lr, rr) + jnp.where(last, east_col, rl)
            for h, box in ((0, box_left), (1, box_right)):
                cols = slice(h * LANES, (h + 1) * LANES)
                v = rp[z + 1, :, cols]
                image = dg[z, :, cols] * v - 0.25 * box
                w[z, :, cols] = image
                gamma = gamma + fold(v * v)
                delta = delta + fold(v * image)
                eta = eta + fold(v * s[z, :, cols])
            return gamma, delta, eta

        gamma, delta, eta = lax.fori_loop(0, CZ, apply, (zero8, zero8, zero8))
        gamma = jnp.sum(gamma, axis=0, keepdims=True)
        delta = jnp.sum(delta, axis=0, keepdims=True)
        eta = jnp.sum(eta, axis=0, keepdims=True)
        mine = jnp.where(sub8 == 0, gamma, jnp.where(sub8 == 1, delta, jnp.where(sub8 == 2, eta, 0.0)))
        part_y[it] = mine
        got_y[it, me_y] = mine

        def send_y(d, c):
            ask(0, at(0, d), part_y.at[it], got_y.at[it, me_y], y_s.at[it], y_r.at[it])
            return c

        lax.fori_loop(1, count_y, send_y, 0)
        wait_for(got_y.at[it, pl.ds(0, count_y - 1)], y_r.at[it])
        mine = total_of(got_y.at[it])
        part_x[it] = mine
        got_x[it, me_x] = mine

        def send_x(d, c):
            ask(0, at(d, 0), part_x.at[it], got_x.at[it, me_x], x_s.at[it], x_r.at[it])
            return c

        lax.fori_loop(1, count_x, send_x, 0)
        wait_for(got_x.at[it, pl.ds(0, count_x - 1)], x_r.at[it])
        total = jnp.sum(total_of(got_x.at[it]), axis=1, keepdims=True)
        gamma, delta, eta = total[0:1], total[1:2], total[2:3]
        beta = jnp.where(it == 0, 0.0, gamma / gamma_old)
        curve = delta + 2.0 * beta * eta + beta * beta * curve_old
        alpha = gamma / curve

        def update(z, c):
            r = rp[z + 1]
            pn = r + beta * p[z]
            sn = w[z] + beta * s[z]
            p[z] = pn
            s[z] = sn
            x_ref[z] = x_ref[z] + alpha * pn
            r = r - alpha * sn
            rp[z + 1] = r
            r_ref[z] = r
            return c

        lax.fori_loop(0, CZ, update, 0)
        return gamma, curve

    one = jnp.ones((1, 1), jnp.float32)
    lax.fori_loop(0, ITERS, turn, (one, 0.0 * one))

    def finish(it, c):
        wait_for(row_out.at[it], row_s.at[it])
        wait_for(col_in.at[it], col_s.at[it])
        wait_for(got_y.at[it, pl.ds(0, count_y - 1)], y_s.at[it])
        wait_for(got_x.at[it, pl.ds(0, count_x - 1)], x_s.at[it])
        return c

    lax.fori_loop(0, ITERS, finish, 0)


def solve(acc, count_x, count_y):
    vmem = pl.BlockSpec(memory_space=pltpu.VMEM)
    field = jax.ShapeDtypeStruct((CZ, CX, CY), jnp.float32)
    cells = (CZ, CX, CY)

    def kernel(*refs):
        solve_kernel(count_x, count_y, *refs)

    return pl.pallas_call(
        kernel,
        out_shape=(field, field),
        in_specs=[vmem],
        out_specs=(vmem, vmem),
        scratch_shapes=[
            pltpu.VMEM((CZ + 2, CX, CY), jnp.float32),
            pltpu.VMEM(cells, jnp.float32),
            pltpu.VMEM(cells, jnp.float32),
            pltpu.VMEM(cells, jnp.float32),
            pltpu.VMEM(cells, jnp.float32),
            pltpu.VMEM((2, 2, CZ, LANES), jnp.float32),
            pltpu.VMEM((ITERS, 2, CZ, CY), jnp.float32),
            pltpu.VMEM((ITERS, 2, CZ, CY), jnp.float32),
            pltpu.VMEM((ITERS, 2, 8, LANES), jnp.float32),
            pltpu.VMEM((ITERS, 2, 3, 8, LANES), jnp.float32),
            pltpu.VMEM((ITERS, 8, LANES), jnp.float32),
            pltpu.VMEM((ITERS, 8, LANES), jnp.float32),
            pltpu.VMEM((ITERS, count_y, 8, LANES), jnp.float32),
            pltpu.VMEM((ITERS, count_x, 8, LANES), jnp.float32),
        ]
        + [pltpu.SemaphoreType.DMA((ITERS,))] * 8,
        compiler_params=pltpu.CompilerParams(
            collective_id=0, has_side_effects=True, vmem_limit_bytes=32 << 20
        ),
    )(acc)


def blend_kernel(
    count_x, count_y,
    acc_ref, x_ref, r_ref, flag_ref,
    vs, dg, rim, sums,
    row_out, row_in, col_out, col_in, part_y, part_x, got_y, got_x,
    row_s, row_r, col_s, col_r, y_s, y_r, x_s, x_r,
):
    me_x, me_y = lax.axis_index("gx"), lax.axis_index("gy")

    def at(dx, dy):
        return (lax.rem(me_x + dx + count_x, count_x), lax.rem(me_y + dy + count_y, count_y))

    barrier = pltpu.get_barrier_semaphore()

    def greet_y(d, carry):
        pl.semaphore_signal(barrier, inc=1, device_id=at(0, d), device_id_type=MESH)
        return carry

    def greet_x(d, carry):
        pl.semaphore_signal(barrier, inc=1, device_id=at(d, 0), device_id_type=MESH)
        return carry

    lax.fori_loop(1, count_y, greet_y, 0)
    lax.fori_loop(1, count_x, greet_x, 0)
    for dx in (-1, 1):
        for dy in (-1, 1):
            pl.semaphore_signal(barrier, inc=1, device_id=at(dx, dy), device_id_type=MESH)

    tiles_x = CX // TX
    sub8 = lax.broadcasted_iota(jnp.int32, (8, LANES), 0)
    lane8 = lax.broadcasted_iota(jnp.int32, (8, LANES), 1)
    lane_half = lax.broadcasted_iota(jnp.int32, (CX, LANES), 1)
    row_half = lax.broadcasted_iota(jnp.int32, (CX, LANES), 0)
    plane8 = lax.rem(lane8, CZ)
    zrow = lax.broadcasted_iota(jnp.int32, (CZ, CY), 0)
    yrow = lax.broadcasted_iota(jnp.int32, (CZ, CY), 1)
    zero8 = jnp.zeros((8, LANES), jnp.float32)

    for k in range(ITERS):
        vs[k, 0] = jnp.zeros((CX, CY), jnp.float32)
        vs[k, CZ + 1] = jnp.zeros((CX, CY), jnp.float32)

    def unfold(t, carry):
        rows = pl.ds(pl.multiple_of(t * TX, TX), TX)
        vs[0, 1 : CZ + 1, rows, :] = acc_ref[t, 0].T.reshape(CZ, TX, CY)
        dg[:, rows, :] = (6.75 - SHIFT) + screen_weight * acc_ref[t, 1].T.reshape(CZ, TX, CY)
        return carry

    lax.fori_loop(0, tiles_x, unfold, 0)

    def collect(z, t, left, right, west, east):
        shift = z + CZ * t
        mine = lane8 == shift
        west = jnp.where(mine, pltpu.roll(left, shift, 1), west)
        east = jnp.where(mine, pltpu.roll(right, lax.rem(shift + 1, LANES), 1), east)
        return west, east

    def first(z, carry):
        west, east, norm = carry
        for t in range(tiles_x):
            left = vs[0, z + 1, 8 * t : 8 * t + 8, :LANES]
            right = vs[0, z + 1, 8 * t : 8 * t + 8, LANES:]
            west, east = collect(z, t, left, right, west, east)
            norm = norm + left * left + right * right
        return west, east, norm

    west, east, norm = lax.fori_loop(0, CZ, first, (zero8, zero8, zero8))
    sums[0] = norm
    pl.semaphore_wait(barrier, (count_y - 1) + (count_x - 1) + 4)

    def ask(target, src, dst, send, recv):
        pltpu.make_async_remote_copy(
            src_ref=src, dst_ref=dst, send_sem=send, recv_sem=recv,
            device_id=target, device_id_type=MESH,
        ).start()

    def wait_for(ref, sem):
        pltpu.make_async_copy(ref, ref, sem).wait()

    def turn(it, carry):
        west, east = carry
        col_out[it, 0] = west
        col_out[it, 1] = east
        for dx in (-1, 1, 0):
            ask(at(dx, -1), col_out.at[it, 0], col_in.at[it, 1, 1 - dx], col_s.at[it], col_r.at[it])
            ask(at(dx, 1), col_out.at[it, 1], col_in.at[it, 0, 1 - dx], col_s.at[it], col_r.at[it])
        row_out[it, 0] = vs[it, 1 : CZ + 1, 0, :]
        row_out[it, 1] = vs[it, 1 : CZ + 1, CX - 1, :]
        ask(at(-1, 0), row_out.at[it, 0], row_in.at[it, 1], row_s.at[it], row_r.at[it])
        ask(at(1, 0), row_out.at[it, 1], row_in.at[it, 0], row_s.at[it], row_r.at[it])

        def inner(z, c):
            halves = []
            for h in range(2):
                cols = slice(h * LANES, (h + 1) * LANES)
                u = vs[it, z, :, cols] + vs[it, z + 1, :, cols] + vs[it, z + 2, :, cols]
                halves.append(
                    u
                    + jnp.where(row_half == 0, 0.0, pltpu.roll(u, 1, 0))
                    + jnp.where(row_half == CX - 1, 0.0, pltpu.roll(u, CX - 1, 0))
                )
            left, right = halves
            lr, rr = pltpu.roll(left, 1, 1), pltpu.roll(right, 1, 1)
            ll, rl = pltpu.roll(left, LANES - 1, 1), pltpu.roll(right, LANES - 1, 1)
            start, last = lane_half == 0, lane_half == LANES - 1
            box_left = left + jnp.where(start, 0.0, lr) + jnp.where(last, rl, ll)
            box_right = right + jnp.where(start, lr, rr) + jnp.where(last, 0.0, rl)
            for h, box in ((0, box_left), (1, box_right)):
                cols = slice(h * LANES, (h + 1) * LANES)
                vs[it + 1, z + 1, :, cols] = dg[z, :, cols] * vs[it, z + 1, :, cols] - 0.25 * box
            return c

        lax.fori_loop(0, CZ, inner, 0)

        wait_for(row_in.at[it], row_r.at[it])
        for side, there in ((0, me_x > 0), (1, me_x < count_x - 1)):
            near = row_in[it, side]
            near = (
                near
                + jnp.where(zrow > 0, pltpu.roll(near, 1, 0), 0.0)
                + jnp.where(zrow < CZ - 1, pltpu.roll(near, CZ - 1, 0), 0.0)
            )
            near = (
                near
                + jnp.where(yrow > 0, pltpu.roll(near, 1, 1), 0.0)
                + jnp.where(yrow < CY - 1, pltpu.roll(near, CY - 1, 1), 0.0)
            )
            near = jnp.where(there, 0.25 * near, 0.0)
            rim[side, 0] = near[:, :LANES]
            rim[side, 1] = near[:, LANES:]
        wait_for(col_in.at[it], col_r.at[it])

        def column(side, there):
            def summed(k, ok):
                col = col_in[it, side, k]
                col = (
                    col
                    + jnp.where(plane8 > 0, pltpu.roll(col, 1, 1), 0.0)
                    + jnp.where(plane8 < CZ - 1, pltpu.roll(col, LANES - 1, 1), 0.0)
                )
                return jnp.where(ok, 0.25 * col, 0.0)

            mid = summed(1, there)
            low = summed(0, jnp.logical_and(there, me_x > 0))
            high = summed(2, jnp.logical_and(there, me_x < count_x - 1))

            def down(v):
                return pltpu.roll(v, 1, 0)

            def up(v):
                return pltpu.roll(v, 7, 0)

            before = jnp.where(lane8 < CZ, pltpu.roll(down(low), CZ, 1), pltpu.roll(down(mid), CZ, 1))
            before = jnp.where(sub8 == 0, before, down(mid))
            after = jnp.where(
                lane8 >= LANES - CZ,
                pltpu.roll(up(high), LANES - CZ, 1),
                pltpu.roll(up(mid), LANES - CZ, 1),
            )
            after = jnp.where(sub8 == 7, after, up(mid))
            return before + mid + after

        west_in = column(0, me_y > 0)
        east_in = column(1, me_y < count_y - 1)

        def edge(z, carry):
            west, east, cross, norm = carry
            for t in range(tiles_x):
                rows = slice(8 * t, 8 * t + 8)
                shift = z + CZ * t
                fixes = [
                    jnp.where(lane8 == 0, pltpu.roll(west_in, lax.rem(2 * LANES - shift, LANES), 1), 0.0),
                    jnp.where(lane8 == LANES - 1, pltpu.roll(east_in, 2 * LANES - 1 - shift - LANES, 1), 0.0),
                ]
                made = []
                for h in range(2):
                    cols = slice(h * LANES, (h + 1) * LANES)
                    value = vs[it + 1, z + 1, rows, cols] - fixes[h]
                    if t == 0:
                        value = value - jnp.where(sub8 == 0, rim[0, h, pl.ds(z, 1), :], 0.0)
                    if t == tiles_x - 1:
                        value = value - jnp.where(sub8 == 7, rim[1, h, pl.ds(z, 1), :], 0.0)
                    vs[it + 1, z + 1, rows, cols] = value
                    cross = cross + value * vs[it, z + 1, rows, cols]
                    norm = norm + value * value
                    made.append(value)
                west, east = collect(z, t, made[0], made[1], west, east)
            return west, east, cross, norm

        west, east, cross, norm = lax.fori_loop(0, CZ, edge, (zero8, zero8, zero8, zero8))
        sums[2 * it + 1] = cross
        sums[2 * it + 2] = norm
        return west, east

    lax.fori_loop(0, ITERS, turn, (west, east))

    mine = zero8
    for k in range(2 * ITERS + 1):
        mine = jnp.where(sub8 == k, jnp.sum(sums[k], axis=0, keepdims=True), mine)
    part_y[...] = mine
    got_y[me_y] = mine

    def send_y(d, c):
        ask(at(0, d), part_y, got_y.at[me_y], y_s, y_r)
        return c

    lax.fori_loop(1, count_y, send_y, 0)
    wait_for(got_y.at[pl.ds(0, count_y - 1)], y_r)

    def total_of(parts):
        total = parts[0]
        for k in range(1, parts.shape[0]):
            total = total + parts[k]
        return total

    mine = total_of(got_y)
    part_x[...] = mine
    got_x[me_x] = mine

    def send_x(d, c):
        ask(at(d, 0), part_x, got_x.at[me_x], x_s, x_r)
        return c

    lax.fori_loop(1, count_x, send_x, 0)
    wait_for(got_x.at[pl.ds(0, count_x - 1)], x_r)
    total = jnp.sum(total_of(got_x), axis=1, keepdims=True)
    moment = [total[k : k + 1] for k in range(2 * ITERS + 1)]

    good = jnp.ones((1, 1), jnp.float32)

    def product(a, b, good):
        value, size = 0.0, 0.0
        for d in range(len(a) + len(b) - 1):
            pairs = [a[i] * b[d - i] for i in range(len(a)) if 0 <= d - i < len(b)]
            both = pairs[0]
            bulk = jnp.abs(pairs[0])
            for pair in pairs[1:]:
                both = both + pair
                bulk = bulk + jnp.abs(pair)
            value = value + both * moment[d]
            size = size + bulk * jnp.abs(moment[d])
        return value, jnp.where(size <= TRUST * value, good, 0.0)

    def image(a):
        padded = [SHIFT * c for c in a] + [None]
        return [
            (padded[i] if i == 0 else a[i - 1] if i == len(a) else padded[i] + a[i - 1])
            for i in range(len(a) + 1)
        ]

    def plus(a, factor, b):
        longest = max(len(a), len(b))
        made = []
        for i in range(longest):
            if i >= len(a):
                made.append(factor * b[i])
            elif i >= len(b):
                made.append(a[i])
            else:
                made.append(a[i] + factor * b[i])
        return made

    one = jnp.ones((1, 1), jnp.float32)
    residual, direction, answer = [one], [one], []
    gamma, good = product(residual, residual, good)
    for it in range(ITERS):
        curve, good = product(direction, image(direction), good)
        alpha = gamma / curve
        answer = plus(answer, alpha, direction)
        residual = plus(residual, -alpha, image(direction))
        fresh, good = product(residual, residual, good)
        direction = plus(residual, fresh / gamma, direction)
        gamma = fresh
    flag_ref[...] = jnp.broadcast_to(good, (8, LANES))

    def combine(z, c):
        for h in range(2):
            cols = slice(h * LANES, (h + 1) * LANES)
            fields = [vs[k, z + 1, :, cols] for k in range(ITERS + 1)]
            x_ref[z, :, cols] = sum(answer[k] * fields[k] for k in range(ITERS))
            r_ref[z, :, cols] = sum(residual[k] * fields[k] for k in range(ITERS + 1))
        return c

    lax.fori_loop(0, CZ, combine, 0)

    def finish(it, c):
        wait_for(row_out.at[it], row_s.at[it])
        wait_for(col_in.at[it], col_s.at[it])
        return c

    lax.fori_loop(0, ITERS, finish, 0)
    wait_for(got_y.at[pl.ds(0, count_y - 1)], y_s)
    wait_for(got_x.at[pl.ds(0, count_x - 1)], x_s)


def blend(acc, count_x, count_y):
    vmem = pl.BlockSpec(memory_space=pltpu.VMEM)
    field = jax.ShapeDtypeStruct((CZ, CX, CY), jnp.float32)

    def kernel(*refs):
        blend_kernel(count_x, count_y, *refs)

    return pl.pallas_call(
        kernel,
        out_shape=(field, field, jax.ShapeDtypeStruct((8, LANES), jnp.float32)),
        in_specs=[vmem],
        out_specs=(vmem, vmem, vmem),
        scratch_shapes=[
            pltpu.VMEM((ITERS + 1, CZ + 2, CX, CY), jnp.float32),
            pltpu.VMEM((CZ, CX, CY), jnp.float32),
            pltpu.VMEM((2, 2, CZ, LANES), jnp.float32),
            pltpu.VMEM((2 * ITERS + 1, 8, LANES), jnp.float32),
            pltpu.VMEM((ITERS, 2, CZ, CY), jnp.float32),
            pltpu.VMEM((ITERS, 2, CZ, CY), jnp.float32),
            pltpu.VMEM((ITERS, 2, 8, LANES), jnp.float32),
            pltpu.VMEM((ITERS, 2, 3, 8, LANES), jnp.float32),
            pltpu.VMEM((8, LANES), jnp.float32),
            pltpu.VMEM((8, LANES), jnp.float32),
            pltpu.VMEM((count_y, 8, LANES), jnp.float32),
            pltpu.VMEM((count_x, 8, LANES), jnp.float32),
        ]
        + [pltpu.SemaphoreType.DMA((ITERS,))] * 4
        + [pltpu.SemaphoreType.DMA] * 4,
        compiler_params=pltpu.CompilerParams(
            collective_id=1, has_side_effects=True, vmem_limit_bytes=32 << 20
        ),
    )(acc)


def local(fractions, normals, point_cells, block_owner, block_tile, block_count):
    count_x, count_y = lax.axis_size("gx"), lax.axis_size("gy")
    devices = count_x * count_y
    blocks = fractions.shape[0]
    capacity = 2 * blocks // devices
    owner = block_owner[:, 0]
    index = jnp.arange(blocks, dtype=jnp.int32)
    earlier = (owner[:, None] == owner[None, :]) & (index[None, :] < index[:, None])
    slot = owner * capacity + jnp.sum(earlier.astype(jnp.int32), axis=1)
    packed = arrange(
        slot, block_tile, block_count, fractions, normals, point_cells, devices * capacity
    )
    packed = packed.reshape(devices, capacity, 8, POINTS)
    got = lax.all_to_all(packed, ("gx", "gy"), split_axis=0, concat_axis=0, tiled=True)
    got = got.reshape(devices * capacity, 8, POINTS)
    header = got[:, 7, :2].astype(jnp.int32)
    acc = splat(header[:, 0], header[:, 1], got)
    x, r, flag = blend(acc, count_x, count_y)
    return lax.cond(
        flag[0, 0] > 0.5,
        lambda acc, x, r: (x, r),
        lambda acc, x, r: tuple(solve(acc, count_x, count_y)),
        acc, x, r,
    )


def solution(mesh):
    placed = (
        P(("gx", "gy"), None, None),
        P(("gx", "gy"), None, None),
        P(("gx", "gy"), None),
        P(("gx", "gy"), None),
        P(("gx", "gy")),
        P(("gx", "gy")),
    )
    return jax.shard_map(
        local,
        mesh=mesh,
        in_specs=placed,
        out_specs=(P(None, "gx", "gy"), P(None, "gx", "gy")),
        check_vma=False,
    )
```

```python
import jax
import jax.numpy as jnp
from jax import lax
from jax.experimental import pallas as pl
from jax.experimental.pallas import tpu as pltpu
from jax.sharding import PartitionSpec as P

CX = 64
CY = 256
CZ = 16
TX = 8
TY = 16
POINTS = 128
ITERS = 3
LANES = 128
GROUP = 32
SHIFT = 6.5
TRUST = 100.0

screen_weight = 4.0
MESH = pl.DeviceIdType.MESH


def route_kernel(
    count_x, count_y,
    tile_in, count_in, owner_in, frac_in, norm_in, cell_in, out_ref,
    tile_ref, count_ref, owner_ref, frac_ref, norm_ref, cell_ref,
    send, index_v, index_s, load_sem, copy_sem, send_sem, recv_sem,
):
    devices = count_x * count_y
    blocks = cell_ref.shape[0]
    loads = [
        pltpu.make_async_copy(source, target, load_sem.at[k])
        for k, (source, target) in enumerate(
            (
                (owner_in, owner_ref),
                (tile_in, tile_ref),
                (count_in, count_ref),
                (frac_in, frac_ref),
                (norm_in, norm_ref),
                (cell_in, cell_ref),
            )
        )
    ]
    for load in loads:
        load.start()
    me = lax.axis_index("gx") * count_y + lax.axis_index("gy")

    def place(d):
        flat = lax.rem(me + d, devices)
        return flat, (flat // count_y, lax.rem(flat, count_y))

    barrier = pltpu.get_barrier_semaphore()

    def greet(d, carry):
        pl.semaphore_signal(barrier, inc=1, device_id=place(d)[1], device_id_type=MESH)
        return carry

    lax.fori_loop(1, devices, greet, 0)

    loads[0].wait()
    owner = jnp.broadcast_to(owner_ref[...], (devices, blocks)).T
    block = lax.broadcasted_iota(jnp.int32, (blocks, devices), 0)
    named = owner == lax.broadcasted_iota(jnp.int32, (blocks, devices), 1)
    first = jnp.min(jnp.where(named, block, blocks), axis=0, keepdims=True)
    last = jnp.max(jnp.where(named, block, -1), axis=0, keepdims=True)
    sub = lax.broadcasted_iota(jnp.int32, (8, devices), 0)
    index_v[...] = jnp.where(
        sub == 0,
        first,
        jnp.where(
            sub == 1,
            last,
            jnp.where(
                sub == 2,
                (last >= 0).astype(jnp.int32),
                (last > first).astype(jnp.int32),
            ),
        ),
    )
    fetch = pltpu.make_async_copy(index_v, index_s, copy_sem)
    fetch.start()
    for load in loads[1:]:
        load.wait()
    fetch.wait()

    lane = lax.broadcasted_iota(jnp.int32, (1, LANES), 1)

    def fill(o, carry):
        for c in range(2):
            k = jnp.minimum(jnp.maximum(index_s[c, o], 0), blocks - 1)
            there = index_s[2 + c, o]
            slot = 2 * o + c
            for axis in range(3):
                send[slot, axis : axis + 1, :] = frac_ref[axis, pl.ds(k, 1), :]
                send[slot, 3 + axis : 4 + axis, :] = norm_ref[axis, pl.ds(k, 1), :]
            send[slot, 6:7, :] = cell_ref[pl.ds(k, 1), :].astype(jnp.float32)
            header = jnp.where(lane == 0, tile_ref[k], jnp.where(lane == 1, count_ref[k] * there, 0))
            send[slot, 7:8, :] = header.astype(jnp.float32)
        return carry

    lax.fori_loop(0, devices, fill, 0, unroll=4)
    keep = pltpu.make_async_copy(
        send.at[pl.ds(2 * me, 2)], out_ref.at[pl.ds(2 * me, 2)], copy_sem
    )
    keep.start()
    pl.semaphore_wait(barrier, devices - 1)

    def ship(d, carry):
        flat, target = place(d)
        pltpu.make_async_remote_copy(
            src_ref=send.at[pl.ds(2 * flat, 2)],
            dst_ref=out_ref.at[pl.ds(2 * me, 2)],
            send_sem=send_sem, recv_sem=recv_sem,
            device_id=target, device_id_type=MESH,
        ).start()
        return carry

    lax.fori_loop(1, devices, ship, 0)
    keep.wait()
    most = pl.ds(0, 2 * (devices - 1))
    pltpu.make_async_copy(out_ref.at[most], out_ref.at[most], recv_sem).wait()
    pltpu.make_async_copy(send.at[most], send.at[most], send_sem).wait()


def route(tile, count, owner, fractions, normals, cells, count_x, count_y):
    slots = 2 * count_x * count_y
    operands = (tile, count, owner, fractions, normals, cells)

    def kernel(*refs):
        route_kernel(count_x, count_y, *refs)

    return pl.pallas_call(
        kernel,
        out_shape=jax.ShapeDtypeStruct((slots, 8, LANES), jnp.float32),
        in_specs=[pl.BlockSpec(memory_space=pl.ANY)] * 6,
        out_specs=pl.BlockSpec(memory_space=pl.ANY),
        scratch_shapes=[pltpu.SMEM(tile.shape, tile.dtype), pltpu.SMEM(count.shape, count.dtype)]
        + [pltpu.VMEM(one.shape, one.dtype) for one in operands[2:]]
        + [
            pltpu.VMEM((slots, 8, LANES), jnp.float32),
            pltpu.VMEM((8, LANES), jnp.int32),
            pltpu.SMEM((8, LANES), jnp.int32),
            pltpu.SemaphoreType.DMA((6,)),
            pltpu.SemaphoreType.DMA,
            pltpu.SemaphoreType.DMA,
            pltpu.SemaphoreType.DMA,
        ],
        compiler_params=pltpu.CompilerParams(
            collective_id=2, has_side_effects=True, vmem_limit_bytes=56 << 20
        ),
    )(*operands)


def split(value):
    high = value.astype(jnp.bfloat16)
    return high, (value - high.astype(jnp.float32)).astype(jnp.bfloat16)


def taps(anchor, offset, length):
    place = lax.broadcasted_iota(jnp.int32, (length, POINTS), 0).astype(jnp.float32)
    lower = place == anchor
    upper = place == anchor + 1.0
    weight = jnp.where(lower, 1.0 - offset, jnp.where(upper, offset, 0.0))
    slope = jnp.where(lower, -1.0, jnp.where(upper, 1.0, 0.0))
    return weight, slope


def splat_tile(block, count):
    lane = lax.broadcasted_iota(jnp.int32, (1, POINTS), 1)
    cell = block[6:7]
    remains = jnp.floor((cell + 0.5) * (1.0 / (CZ - 1)))
    plane = cell - remains * (CZ - 1)
    row = jnp.floor((remains + 0.5) * (1.0 / (TY - 1)))
    column = remains - row * (TY - 1)
    row = jnp.where(lane < count, row, -4.0)
    wx, sx = taps(row, block[0:1], TX)
    wy, sy = taps(column, block[1:2], TY)
    sy = sy * block[4:5]
    fz = block[2:3]
    level = block[3:4] * sx
    rise = block[5:6] * wx
    pairs = (
        ((1.0 - fz) * level - rise, fz * level + rise),
        ((1.0 - fz) * wx, fz * wx),
    )
    at = jnp.broadcast_to(plane, (2 * TX, POINTS)).astype(jnp.bfloat16)
    place = (lax.broadcasted_iota(jnp.int32, (2 * TX, POINTS), 0) // TX).astype(jnp.float32).astype(jnp.bfloat16)
    offset = at - place
    zero = jnp.zeros((2 * TX, POINTS), jnp.bfloat16)
    high, low = [], []
    for lower, upper in pairs:
        lower = split(jnp.concatenate([lower, lower], axis=0))
        upper = split(jnp.concatenate([upper, upper], axis=0))
        for kept, under, over in zip((high, low), lower, upper):
            kept.append(
                jnp.concatenate(
                    [
                        jnp.where(offset == 2 * j, under, jnp.where(offset == 2 * j - 1, over, zero))
                        for j in range(CZ // 2)
                    ],
                    axis=0,
                )
            )
    big_high = jnp.concatenate(high, axis=1)
    big_low = jnp.concatenate(low, axis=1)
    top = jnp.concatenate([wy, sy], axis=1)
    low = jnp.concatenate([jnp.zeros_like(wy), wy], axis=1)
    small_high, small_low = split(jnp.concatenate([top, low], axis=0))
    both = lax.dot_general(
        jnp.concatenate([small_high, small_low], axis=0),
        jnp.concatenate([big_high, big_low], axis=0),
        (((1,), (1,)), ((), ())),
        preferred_element_type=jnp.float32,
    )
    return both[: 2 * TY, :POINTS] + both[2 * TY :, :POINTS] + both[: 2 * TY, POINTS:]


def splat_kernel(blocks_ref, acc_ref, blocks, header_v, header_s, order, sem):
    slots = blocks_ref.shape[0]
    load = pltpu.make_async_copy(blocks_ref, blocks, sem)
    load.start()
    acc_ref[...] = jnp.zeros_like(acc_ref)
    load.wait()
    header_v[...] = blocks[:, 7, :].T[:8].astype(jnp.int32)
    fetch = pltpu.make_async_copy(header_v, header_s, sem)
    fetch.start()
    fetch.wait()

    def gather(i, carry):
        used, empty = carry
        some = header_s[1, i] > 0
        order[used] = i
        return used + some.astype(jnp.int32), jnp.where(some, empty, i)

    used, empty = lax.fori_loop(
        0, slots, gather, (jnp.int32(0), jnp.int32(0)), unroll=8
    )
    for extra in range(GROUP):
        order[used + extra] = empty

    def work(j, carry):
        made = []
        for u in range(GROUP):
            slot = order[j * GROUP + u]
            made.append((header_s[0, slot], splat_tile(blocks[slot], header_s[1, slot])))
        tiles_y = CY // TY
        for tile, values in made:
            x = tile // tiles_y
            y = pl.multiple_of((tile % tiles_y) * TY, TY)
            acc_ref[x, 0, pl.ds(y, TY), :] += values[:TY]
            acc_ref[x, 1, pl.ds(y, TY), :] += values[TY:]
        return carry

    lax.fori_loop(0, (used + GROUP - 1) // GROUP, work, 0)


def splat(blocks):
    slots = blocks.shape[0]
    return pl.pallas_call(
        splat_kernel,
        out_shape=jax.ShapeDtypeStruct((CX // TX, 2, CY, CZ * TX), jnp.float32),
        in_specs=[pl.BlockSpec(memory_space=pl.ANY)],
        out_specs=pl.BlockSpec(memory_space=pltpu.VMEM),
        scratch_shapes=[
            pltpu.VMEM(blocks.shape, blocks.dtype),
            pltpu.VMEM((8, slots), jnp.int32),
            pltpu.SMEM((8, slots), jnp.int32),
            pltpu.SMEM((slots + GROUP,), jnp.int32),
            pltpu.SemaphoreType.DMA,
        ],
        compiler_params=pltpu.CompilerParams(vmem_limit_bytes=24 << 20),
    )(blocks)


def fold(value):
    total = value[0:8]
    for k in range(1, value.shape[0] // 8):
        total = total + value[8 * k : 8 * k + 8]
    return total


def solve_kernel(
    count_x, count_y,
    acc_ref, x_ref, r_ref,
    rp, dg, p, s, w, rim,
    row_out, row_in, col_out, col_in, part_y, part_x, got_y, got_x,
    row_s, row_r, col_s, col_r, y_s, y_r, x_s, x_r,
):
    me_x, me_y = lax.axis_index("gx"), lax.axis_index("gy")

    def at(dx, dy):
        return (lax.rem(me_x + dx + count_x, count_x), lax.rem(me_y + dy + count_y, count_y))

    barrier = pltpu.get_barrier_semaphore()

    def greet_y(d, carry):
        pl.semaphore_signal(barrier, inc=1, device_id=at(0, d), device_id_type=MESH)
        return carry

    def greet_x(d, carry):
        pl.semaphore_signal(barrier, inc=1, device_id=at(d, 0), device_id_type=MESH)
        return carry

    lax.fori_loop(1, count_y, greet_y, 0)
    lax.fori_loop(1, count_x, greet_x, 0)
    for dx in (-1, 1):
        for dy in (-1, 1):
            pl.semaphore_signal(barrier, inc=1, device_id=at(dx, dy), device_id_type=MESH)

    sub8 = lax.broadcasted_iota(jnp.int32, (8, LANES), 0)
    lane8 = lax.broadcasted_iota(jnp.int32, (8, LANES), 1)
    lane_half = lax.broadcasted_iota(jnp.int32, (CX, LANES), 1)
    row_half = lax.broadcasted_iota(jnp.int32, (CX, LANES), 0)

    rp[0] = jnp.zeros((CX, CY), jnp.float32)
    rp[CZ + 1] = jnp.zeros((CX, CY), jnp.float32)

    def unfold(t, carry):
        rows = pl.ds(pl.multiple_of(t * TX, TX), TX)
        source = acc_ref[t, 0].T.reshape(CZ, TX, CY)
        density = acc_ref[t, 1].T.reshape(CZ, TX, CY)
        rp[1 : CZ + 1, rows, :] = source
        dg[:, rows, :] = 6.75 + screen_weight * density
        return carry

    lax.fori_loop(0, CX // TX, unfold, 0)

    def clear(z, carry):
        zero = jnp.zeros((CX, CY), jnp.float32)
        p[z] = zero
        s[z] = zero
        x_ref[z] = zero
        return carry

    lax.fori_loop(0, CZ, clear, 0)
    pl.semaphore_wait(barrier, (count_y - 1) + (count_x - 1) + 4)

    def pack(z, carry):
        west, east = carry
        for t in range(CX // TX):
            here = rp[z + 1, 8 * t : 8 * t + 8, :]
            shift = z + CZ * t
            mine = lane8 == shift
            west = jnp.where(mine, pltpu.roll(here[:, :LANES], shift, 1), west)
            turned = pltpu.roll(here[:, LANES:], lax.rem(shift + 1, LANES), 1)
            east = jnp.where(mine, turned, east)
        return west, east

    def ask(count, target, src, dst, send, recv):
        pltpu.make_async_remote_copy(
            src_ref=src, dst_ref=dst, send_sem=send, recv_sem=recv,
            device_id=target, device_id_type=MESH,
        ).start()

    def wait_for(ref, sem):
        pltpu.make_async_copy(ref, ref, sem).wait()

    zero8 = jnp.zeros((8, LANES), jnp.float32)

    def total_of(parts):
        total = parts[0]
        for k in range(1, parts.shape[0]):
            total = total + parts[k]
        return total

    def turn(it, carry):
        gamma_old, curve_old = carry
        row_out[it, 0] = rp[1 : CZ + 1, 0, :]
        row_out[it, 1] = rp[1 : CZ + 1, CX - 1, :]
        ask(0, at(-1, 0), row_out.at[it, 0], row_in.at[it, 1], row_s.at[it], row_r.at[it])
        ask(0, at(1, 0), row_out.at[it, 1], row_in.at[it, 0], row_s.at[it], row_r.at[it])
        west, east = lax.fori_loop(0, CZ, pack, (zero8, zero8))
        col_out[it, 0] = west
        col_out[it, 1] = east
        for dx in (-1, 0, 1):
            ask(0, at(dx, -1), col_out.at[it, 0], col_in.at[it, 1, 1 - dx], col_s.at[it], col_r.at[it])
            ask(0, at(dx, 1), col_out.at[it, 1], col_in.at[it, 0, 1 - dx], col_s.at[it], col_r.at[it])

        wait_for(row_in.at[it], row_r.at[it])
        zrow = lax.broadcasted_iota(jnp.int32, (CZ, CY), 0)
        for side, there in ((0, me_x > 0), (1, me_x < count_x - 1)):
            near = row_in[it, side]
            near = (
                near
                + jnp.where(zrow > 0, pltpu.roll(near, 1, 0), 0.0)
                + jnp.where(zrow < CZ - 1, pltpu.roll(near, CZ - 1, 0), 0.0)
            )
            near = jnp.where(there, near, 0.0)
            rim[side, 0] = near[:, :LANES]
            rim[side, 1] = near[:, LANES:]
        wait_for(col_in.at[it], col_r.at[it])

        plane8 = lax.rem(lane8, CZ)

        def column(side, there):
            def summed(k, ok):
                col = col_in[it, side, k]
                col = (
                    col
                    + jnp.where(plane8 > 0, pltpu.roll(col, 1, 1), 0.0)
                    + jnp.where(plane8 < CZ - 1, pltpu.roll(col, LANES - 1, 1), 0.0)
                )
                return jnp.where(ok, col, 0.0)

            mid = summed(1, there)
            low = summed(0, jnp.logical_and(there, me_x > 0))
            high = summed(2, jnp.logical_and(there, me_x < count_x - 1))

            def down(v):
                return pltpu.roll(v, 1, 0)

            def up(v):
                return pltpu.roll(v, 7, 0)

            before = jnp.where(lane8 < CZ, pltpu.roll(down(low), CZ, 1), pltpu.roll(down(mid), CZ, 1))
            before = jnp.where(sub8 == 0, before, down(mid))
            after = jnp.where(
                lane8 >= LANES - CZ,
                pltpu.roll(up(high), LANES - CZ, 1),
                pltpu.roll(up(mid), LANES - CZ, 1),
            )
            after = jnp.where(sub8 == 7, after, up(mid))
            return before + mid + after

        west_in = column(0, me_y > 0)
        east_in = column(1, me_y < count_y - 1)

        def apply(z, sums):
            gamma, delta, eta = sums
            halves = []
            for h in range(2):
                cols = slice(h * LANES, (h + 1) * LANES)
                u = rp[z, :, cols] + rp[z + 1, :, cols] + rp[z + 2, :, cols]
                above = rim[0, h, pl.ds(z, 1), :]
                below = rim[1, h, pl.ds(z, 1), :]
                t = (
                    u
                    + jnp.where(row_half == 0, above, pltpu.roll(u, 1, 0))
                    + jnp.where(row_half == CX - 1, below, pltpu.roll(u, CX - 1, 0))
                )
                halves.append(t)
            left, right = halves
            back = lax.rem(2 * LANES - z, LANES)
            west_col = jnp.concatenate(
                [pltpu.roll(west_in, lax.rem(back + LANES - CZ * t, LANES), 1) for t in range(CX // TX)],
                axis=0,
            )
            east_col = jnp.concatenate(
                [pltpu.roll(east_in, lax.rem(back + 2 * LANES - 1 - CZ * t, LANES), 1) for t in range(CX // TX)],
                axis=0,
            )
            lr, rr = pltpu.roll(left, 1, 1), pltpu.roll(right, 1, 1)
            ll, rl = pltpu.roll(left, LANES - 1, 1), pltpu.roll(right, LANES - 1, 1)
            first, last = lane_half == 0, lane_half == LANES - 1
            box_left = left + jnp.where(first, west_col, lr) + jnp.where(last, rl, ll)
            box_right = right + jnp.where(first, lr, rr) + jnp.where(last, east_col, rl)
            for h, box in ((0, box_left), (1, box_right)):
                cols = slice(h * LANES, (h + 1) * LANES)
                v = rp[z + 1, :, cols]
                image = dg[z, :, cols] * v - 0.25 * box
                w[z, :, cols] = image
                gamma = gamma + fold(v * v)
                delta = delta + fold(v * image)
                eta = eta + fold(v * s[z, :, cols])
            return gamma, delta, eta

        gamma, delta, eta = lax.fori_loop(0, CZ, apply, (zero8, zero8, zero8))
        gamma = jnp.sum(gamma, axis=0, keepdims=True)
        delta = jnp.sum(delta, axis=0, keepdims=True)
        eta = jnp.sum(eta, axis=0, keepdims=True)
        mine = jnp.where(sub8 == 0, gamma, jnp.where(sub8 == 1, delta, jnp.where(sub8 == 2, eta, 0.0)))
        part_y[it] = mine
        got_y[it, me_y] = mine

        def send_y(d, c):
            ask(0, at(0, d), part_y.at[it], got_y.at[it, me_y], y_s.at[it], y_r.at[it])
            return c

        lax.fori_loop(1, count_y, send_y, 0)
        wait_for(got_y.at[it, pl.ds(0, count_y - 1)], y_r.at[it])
        mine = total_of(got_y.at[it])
        part_x[it] = mine
        got_x[it, me_x] = mine

        def send_x(d, c):
            ask(0, at(d, 0), part_x.at[it], got_x.at[it, me_x], x_s.at[it], x_r.at[it])
            return c

        lax.fori_loop(1, count_x, send_x, 0)
        wait_for(got_x.at[it, pl.ds(0, count_x - 1)], x_r.at[it])
        total = jnp.sum(total_of(got_x.at[it]), axis=1, keepdims=True)
        gamma, delta, eta = total[0:1], total[1:2], total[2:3]
        beta = jnp.where(it == 0, 0.0, gamma / gamma_old)
        curve = delta + 2.0 * beta * eta + beta * beta * curve_old
        alpha = gamma / curve

        def update(z, c):
            r = rp[z + 1]
            pn = r + beta * p[z]
            sn = w[z] + beta * s[z]
            p[z] = pn
            s[z] = sn
            x_ref[z] = x_ref[z] + alpha * pn
            r = r - alpha * sn
            rp[z + 1] = r
            r_ref[z] = r
            return c

        lax.fori_loop(0, CZ, update, 0)
        return gamma, curve

    one = jnp.ones((1, 1), jnp.float32)
    lax.fori_loop(0, ITERS, turn, (one, 0.0 * one))

    def finish(it, c):
        wait_for(row_out.at[it], row_s.at[it])
        wait_for(col_in.at[it], col_s.at[it])
        wait_for(got_y.at[it, pl.ds(0, count_y - 1)], y_s.at[it])
        wait_for(got_x.at[it, pl.ds(0, count_x - 1)], x_s.at[it])
        return c

    lax.fori_loop(0, ITERS, finish, 0)


def solve(acc, count_x, count_y):
    vmem = pl.BlockSpec(memory_space=pltpu.VMEM)
    field = jax.ShapeDtypeStruct((CZ, CX, CY), jnp.float32)
    cells = (CZ, CX, CY)

    def kernel(*refs):
        solve_kernel(count_x, count_y, *refs)

    return pl.pallas_call(
        kernel,
        out_shape=(field, field),
        in_specs=[vmem],
        out_specs=(vmem, vmem),
        scratch_shapes=[
            pltpu.VMEM((CZ + 2, CX, CY), jnp.float32),
            pltpu.VMEM(cells, jnp.float32),
            pltpu.VMEM(cells, jnp.float32),
            pltpu.VMEM(cells, jnp.float32),
            pltpu.VMEM(cells, jnp.float32),
            pltpu.VMEM((2, 2, CZ, LANES), jnp.float32),
            pltpu.VMEM((ITERS, 2, CZ, CY), jnp.float32),
            pltpu.VMEM((ITERS, 2, CZ, CY), jnp.float32),
            pltpu.VMEM((ITERS, 2, 8, LANES), jnp.float32),
            pltpu.VMEM((ITERS, 2, 3, 8, LANES), jnp.float32),
            pltpu.VMEM((ITERS, 8, LANES), jnp.float32),
            pltpu.VMEM((ITERS, 8, LANES), jnp.float32),
            pltpu.VMEM((ITERS, count_y, 8, LANES), jnp.float32),
            pltpu.VMEM((ITERS, count_x, 8, LANES), jnp.float32),
        ]
        + [pltpu.SemaphoreType.DMA((ITERS,))] * 8,
        compiler_params=pltpu.CompilerParams(
            collective_id=0, has_side_effects=True, vmem_limit_bytes=32 << 20
        ),
    )(acc)


def blend_kernel(
    count_x, count_y,
    acc_ref, x_ref, r_ref, flag_ref,
    vs, dg, rim, sums,
    row_out, row_in, col_out, col_in, part_y, part_x, got_y, got_x,
    row_s, row_r, col_s, col_r, y_s, y_r, x_s, x_r,
):
    me_x, me_y = lax.axis_index("gx"), lax.axis_index("gy")

    def at(dx, dy):
        return (lax.rem(me_x + dx + count_x, count_x), lax.rem(me_y + dy + count_y, count_y))

    barrier = pltpu.get_barrier_semaphore()

    def greet_y(d, carry):
        pl.semaphore_signal(barrier, inc=1, device_id=at(0, d), device_id_type=MESH)
        return carry

    def greet_x(d, carry):
        pl.semaphore_signal(barrier, inc=1, device_id=at(d, 0), device_id_type=MESH)
        return carry

    lax.fori_loop(1, count_y, greet_y, 0)
    lax.fori_loop(1, count_x, greet_x, 0)
    for dx in (-1, 1):
        for dy in (-1, 1):
            pl.semaphore_signal(barrier, inc=1, device_id=at(dx, dy), device_id_type=MESH)

    tiles_x = CX // TX
    sub8 = lax.broadcasted_iota(jnp.int32, (8, LANES), 0)
    lane8 = lax.broadcasted_iota(jnp.int32, (8, LANES), 1)
    lane_half = lax.broadcasted_iota(jnp.int32, (CX, LANES), 1)
    row_half = lax.broadcasted_iota(jnp.int32, (CX, LANES), 0)
    plane8 = lax.rem(lane8, CZ)
    zrow = lax.broadcasted_iota(jnp.int32, (CZ, CY), 0)
    yrow = lax.broadcasted_iota(jnp.int32, (CZ, CY), 1)
    zero8 = jnp.zeros((8, LANES), jnp.float32)

    for k in range(ITERS):
        vs[k, 0] = jnp.zeros((CX, CY), jnp.float32)
        vs[k, CZ + 1] = jnp.zeros((CX, CY), jnp.float32)

    def unfold(t, carry):
        rows = pl.ds(pl.multiple_of(t * TX, TX), TX)
        vs[0, 1 : CZ + 1, rows, :] = acc_ref[t, 0].T.reshape(CZ, TX, CY)
        dg[:, rows, :] = (6.75 - SHIFT) + screen_weight * acc_ref[t, 1].T.reshape(CZ, TX, CY)
        return carry

    lax.fori_loop(0, tiles_x, unfold, 0)

    def collect(z, t, left, right, west, east):
        shift = z + CZ * t
        mine = lane8 == shift
        west = jnp.where(mine, pltpu.roll(left, shift, 1), west)
        east = jnp.where(mine, pltpu.roll(right, lax.rem(shift + 1, LANES), 1), east)
        return west, east

    def first(z, carry):
        west, east, norm = carry
        for t in range(tiles_x):
            left = vs[0, z + 1, 8 * t : 8 * t + 8, :LANES]
            right = vs[0, z + 1, 8 * t : 8 * t + 8, LANES:]
            west, east = collect(z, t, left, right, west, east)
            norm = norm + left * left + right * right
        return west, east, norm

    west, east, norm = lax.fori_loop(0, CZ, first, (zero8, zero8, zero8), unroll=4)
    sums[0] = norm
    pl.semaphore_wait(barrier, (count_y - 1) + (count_x - 1) + 4)

    def ask(target, src, dst, send, recv):
        pltpu.make_async_remote_copy(
            src_ref=src, dst_ref=dst, send_sem=send, recv_sem=recv,
            device_id=target, device_id_type=MESH,
        ).start()

    def wait_for(ref, sem):
        pltpu.make_async_copy(ref, ref, sem).wait()

    def turn(it, carry):
        west, east = carry
        col_out[it, 0] = west
        col_out[it, 1] = east
        for dx in (-1, 1, 0):
            ask(at(dx, -1), col_out.at[it, 0], col_in.at[it, 1, 1 - dx], col_s.at[it], col_r.at[it])
            ask(at(dx, 1), col_out.at[it, 1], col_in.at[it, 0, 1 - dx], col_s.at[it], col_r.at[it])
        row_out[it, 0] = vs[it, 1 : CZ + 1, 0, :]
        row_out[it, 1] = vs[it, 1 : CZ + 1, CX - 1, :]
        ask(at(-1, 0), row_out.at[it, 0], row_in.at[it, 1], row_s.at[it], row_r.at[it])
        ask(at(1, 0), row_out.at[it, 1], row_in.at[it, 0], row_s.at[it], row_r.at[it])

        def inner(z, c):
            halves = []
            for h in range(2):
                cols = slice(h * LANES, (h + 1) * LANES)
                u = vs[it, z, :, cols] + vs[it, z + 1, :, cols] + vs[it, z + 2, :, cols]
                halves.append(
                    u
                    + jnp.where(row_half == 0, 0.0, pltpu.roll(u, 1, 0))
                    + jnp.where(row_half == CX - 1, 0.0, pltpu.roll(u, CX - 1, 0))
                )
            left, right = halves
            lr, rr = pltpu.roll(left, 1, 1), pltpu.roll(right, 1, 1)
            ll, rl = pltpu.roll(left, LANES - 1, 1), pltpu.roll(right, LANES - 1, 1)
            start, last = lane_half == 0, lane_half == LANES - 1
            box_left = left + jnp.where(start, 0.0, lr) + jnp.where(last, rl, ll)
            box_right = right + jnp.where(start, lr, rr) + jnp.where(last, 0.0, rl)
            for h, box in ((0, box_left), (1, box_right)):
                cols = slice(h * LANES, (h + 1) * LANES)
                vs[it + 1, z + 1, :, cols] = dg[z, :, cols] * vs[it, z + 1, :, cols] - 0.25 * box
            return c

        lax.fori_loop(0, CZ, inner, 0, unroll=4)

        wait_for(row_in.at[it], row_r.at[it])
        for side, there in ((0, me_x > 0), (1, me_x < count_x - 1)):
            near = row_in[it, side]
            near = (
                near
                + jnp.where(zrow > 0, pltpu.roll(near, 1, 0), 0.0)
                + jnp.where(zrow < CZ - 1, pltpu.roll(near, CZ - 1, 0), 0.0)
            )
            near = (
                near
                + jnp.where(yrow > 0, pltpu.roll(near, 1, 1), 0.0)
                + jnp.where(yrow < CY - 1, pltpu.roll(near, CY - 1, 1), 0.0)
            )
            near = jnp.where(there, 0.25 * near, 0.0)
            rim[side, 0] = near[:, :LANES]
            rim[side, 1] = near[:, LANES:]
        wait_for(col_in.at[it], col_r.at[it])

        def column(side, there):
            def summed(k, ok):
                col = col_in[it, side, k]
                col = (
                    col
                    + jnp.where(plane8 > 0, pltpu.roll(col, 1, 1), 0.0)
                    + jnp.where(plane8 < CZ - 1, pltpu.roll(col, LANES - 1, 1), 0.0)
                )
                return jnp.where(ok, 0.25 * col, 0.0)

            mid = summed(1, there)
            low = summed(0, jnp.logical_and(there, me_x > 0))
            high = summed(2, jnp.logical_and(there, me_x < count_x - 1))

            def down(v):
                return pltpu.roll(v, 1, 0)

            def up(v):
                return pltpu.roll(v, 7, 0)

            before = jnp.where(lane8 < CZ, pltpu.roll(down(low), CZ, 1), pltpu.roll(down(mid), CZ, 1))
            before = jnp.where(sub8 == 0, before, down(mid))
            after = jnp.where(
                lane8 >= LANES - CZ,
                pltpu.roll(up(high), LANES - CZ, 1),
                pltpu.roll(up(mid), LANES - CZ, 1),
            )
            after = jnp.where(sub8 == 7, after, up(mid))
            return before + mid + after

        west_in = column(0, me_y > 0)
        east_in = column(1, me_y < count_y - 1)

        def edge(z, carry):
            west, east, cross, norm = carry
            for t in range(tiles_x):
                rows = slice(8 * t, 8 * t + 8)
                shift = z + CZ * t
                fixes = [
                    jnp.where(lane8 == 0, pltpu.roll(west_in, lax.rem(2 * LANES - shift, LANES), 1), 0.0),
                    jnp.where(lane8 == LANES - 1, pltpu.roll(east_in, 2 * LANES - 1 - shift - LANES, 1), 0.0),
                ]
                made = []
                for h in range(2):
                    cols = slice(h * LANES, (h + 1) * LANES)
                    value = vs[it + 1, z + 1, rows, cols] - fixes[h]
                    if t == 0:
                        value = value - jnp.where(sub8 == 0, rim[0, h, pl.ds(z, 1), :], 0.0)
                    if t == tiles_x - 1:
                        value = value - jnp.where(sub8 == 7, rim[1, h, pl.ds(z, 1), :], 0.0)
                    vs[it + 1, z + 1, rows, cols] = value
                    cross = cross + value * vs[it, z + 1, rows, cols]
                    norm = norm + value * value
                    made.append(value)
                west, east = collect(z, t, made[0], made[1], west, east)
            return west, east, cross, norm

        west, east, cross, norm = lax.fori_loop(0, CZ, edge, (zero8, zero8, zero8, zero8), unroll=4)
        sums[2 * it + 1] = cross
        sums[2 * it + 2] = norm
        return west, east

    lax.fori_loop(0, ITERS, turn, (west, east))

    mine = zero8
    for k in range(2 * ITERS + 1):
        mine = jnp.where(sub8 == k, jnp.sum(sums[k], axis=0, keepdims=True), mine)
    part_y[...] = mine
    got_y[me_y] = mine

    def send_y(d, c):
        ask(at(0, d), part_y, got_y.at[me_y], y_s, y_r)
        return c

    lax.fori_loop(1, count_y, send_y, 0)
    wait_for(got_y.at[pl.ds(0, count_y - 1)], y_r)

    def total_of(parts):
        total = parts[0]
        for k in range(1, parts.shape[0]):
            total = total + parts[k]
        return total

    mine = total_of(got_y)
    part_x[...] = mine
    got_x[me_x] = mine

    def send_x(d, c):
        ask(at(d, 0), part_x, got_x.at[me_x], x_s, x_r)
        return c

    lax.fori_loop(1, count_x, send_x, 0)
    wait_for(got_x.at[pl.ds(0, count_x - 1)], x_r)
    total = jnp.sum(total_of(got_x), axis=1, keepdims=True)
    moment = [total[k : k + 1] for k in range(2 * ITERS + 1)]

    good = jnp.ones((1, 1), jnp.float32)

    def product(a, b, good):
        value, size = 0.0, 0.0
        for d in range(len(a) + len(b) - 1):
            pairs = [a[i] * b[d - i] for i in range(len(a)) if 0 <= d - i < len(b)]
            both = pairs[0]
            bulk = jnp.abs(pairs[0])
            for pair in pairs[1:]:
                both = both + pair
                bulk = bulk + jnp.abs(pair)
            value = value + both * moment[d]
            size = size + bulk * jnp.abs(moment[d])
        return value, jnp.where(size <= TRUST * value, good, 0.0)

    def image(a):
        padded = [SHIFT * c for c in a] + [None]
        return [
            (padded[i] if i == 0 else a[i - 1] if i == len(a) else padded[i] + a[i - 1])
            for i in range(len(a) + 1)
        ]

    def plus(a, factor, b):
        longest = max(len(a), len(b))
        made = []
        for i in range(longest):
            if i >= len(a):
                made.append(factor * b[i])
            elif i >= len(b):
                made.append(a[i])
            else:
                made.append(a[i] + factor * b[i])
        return made

    one = jnp.ones((1, 1), jnp.float32)
    residual, direction, answer = [one], [one], []
    gamma, good = product(residual, residual, good)
    for it in range(ITERS):
        curve, good = product(direction, image(direction), good)
        alpha = gamma / curve
        answer = plus(answer, alpha, direction)
        residual = plus(residual, -alpha, image(direction))
        fresh, good = product(residual, residual, good)
        direction = plus(residual, fresh / gamma, direction)
        gamma = fresh
    flag_ref[...] = good

    def combine(z, c):
        for h in range(2):
            cols = slice(h * LANES, (h + 1) * LANES)
            fields = [vs[k, z + 1, :, cols] for k in range(ITERS + 1)]
            x_ref[z, :, cols] = sum(answer[k] * fields[k] for k in range(ITERS))
            r_ref[z, :, cols] = sum(residual[k] * fields[k] for k in range(ITERS + 1))
        return c

    lax.fori_loop(0, CZ, combine, 0, unroll=2)

    def finish(it, c):
        wait_for(row_out.at[it], row_s.at[it])
        wait_for(col_in.at[it], col_s.at[it])
        return c

    lax.fori_loop(0, ITERS, finish, 0)
    wait_for(got_y.at[pl.ds(0, count_y - 1)], y_s)
    wait_for(got_x.at[pl.ds(0, count_x - 1)], x_s)


def blend(acc, count_x, count_y):
    vmem = pl.BlockSpec(memory_space=pltpu.VMEM)
    field = jax.ShapeDtypeStruct((CZ, CX, CY), jnp.float32)

    def kernel(*refs):
        blend_kernel(count_x, count_y, *refs)

    return pl.pallas_call(
        kernel,
        out_shape=(field, field, jax.ShapeDtypeStruct((1, 1), jnp.float32)),
        in_specs=[vmem],
        out_specs=(vmem, vmem, vmem),
        scratch_shapes=[
            pltpu.VMEM((ITERS + 1, CZ + 2, CX, CY), jnp.float32),
            pltpu.VMEM((CZ, CX, CY), jnp.float32),
            pltpu.VMEM((2, 2, CZ, LANES), jnp.float32),
            pltpu.VMEM((2 * ITERS + 1, 8, LANES), jnp.float32),
            pltpu.VMEM((ITERS, 2, CZ, CY), jnp.float32),
            pltpu.VMEM((ITERS, 2, CZ, CY), jnp.float32),
            pltpu.VMEM((ITERS, 2, 8, LANES), jnp.float32),
            pltpu.VMEM((ITERS, 2, 3, 8, LANES), jnp.float32),
            pltpu.VMEM((8, LANES), jnp.float32),
            pltpu.VMEM((8, LANES), jnp.float32),
            pltpu.VMEM((count_y, 8, LANES), jnp.float32),
            pltpu.VMEM((count_x, 8, LANES), jnp.float32),
        ]
        + [pltpu.SemaphoreType.DMA((ITERS,))] * 4
        + [pltpu.SemaphoreType.DMA] * 4,
        compiler_params=pltpu.CompilerParams(
            collective_id=1, has_side_effects=True, vmem_limit_bytes=32 << 20
        ),
    )(acc)


def local(fractions, normals, point_cells, block_owner, block_tile, block_count):
    count_x, count_y = lax.axis_size("gx"), lax.axis_size("gy")
    got = route(
        block_tile,
        block_count,
        block_owner.reshape(1, -1),
        jnp.transpose(fractions, (1, 0, 2)),
        jnp.transpose(normals, (1, 0, 2)),
        point_cells,
        count_x,
        count_y,
    )
    acc = splat(got)
    x, r, flag = blend(acc, count_x, count_y)
    return lax.cond(
        flag[0, 0] > 0.5,
        lambda acc, x, r: (x, r),
        lambda acc, x, r: tuple(solve(acc, count_x, count_y)),
        acc, x, r,
    )


def solution(mesh):
    placed = (
        P(("gx", "gy"), None, None),
        P(("gx", "gy"), None, None),
        P(("gx", "gy"), None),
        P(("gx", "gy"), None),
        P(("gx", "gy")),
        P(("gx", "gy")),
    )
    return jax.shard_map(
        local,
        mesh=mesh,
        in_specs=placed,
        out_specs=(P(None, "gx", "gy"), P(None, "gx", "gy")),
        check_vma=False,
    )
```

```python
import jax
import jax.numpy as jnp
from jax import lax
from jax.experimental import pallas as pl
from jax.experimental.pallas import tpu as pltpu
from jax.sharding import PartitionSpec as P

CX = 64
CY = 256
CZ = 16
TX = 8
TY = 16
POINTS = 128
ITERS = 3
LANES = 128
GROUP = 32
SHIFT = 6.5
TRUST = 100.0

screen_weight = 4.0
MESH = pl.DeviceIdType.MESH


def route_kernel(
    count_x, count_y,
    tile_in, count_in, owner_in, frac_in, norm_in, cell_in, out_ref,
    tile_ref, count_ref, owner_ref, frac_ref, norm_ref, cell_ref,
    send, index_v, index_s, load_sem, copy_sem, send_sem, recv_sem,
):
    devices = count_x * count_y
    blocks = cell_ref.shape[0]
    loads = [
        pltpu.make_async_copy(source, target, load_sem.at[k])
        for k, (source, target) in enumerate(
            (
                (owner_in, owner_ref),
                (tile_in, tile_ref),
                (count_in, count_ref),
                (frac_in, frac_ref),
                (norm_in, norm_ref),
                (cell_in, cell_ref),
            )
        )
    ]
    for load in loads:
        load.start()
    me = lax.axis_index("gx") * count_y + lax.axis_index("gy")

    def place(d):
        flat = lax.rem(me + d, devices)
        return flat, (flat // count_y, lax.rem(flat, count_y))

    barrier = pltpu.get_barrier_semaphore()

    def greet(d, carry):
        pl.semaphore_signal(barrier, inc=1, device_id=place(d)[1], device_id_type=MESH)
        return carry

    lax.fori_loop(1, devices, greet, 0)

    loads[0].wait()
    owner = jnp.broadcast_to(owner_ref[...], (devices, blocks)).T
    block = lax.broadcasted_iota(jnp.int32, (blocks, devices), 0)
    named = owner == lax.broadcasted_iota(jnp.int32, (blocks, devices), 1)
    first = jnp.min(jnp.where(named, block, blocks), axis=0, keepdims=True)
    last = jnp.max(jnp.where(named, block, -1), axis=0, keepdims=True)
    sub = lax.broadcasted_iota(jnp.int32, (8, devices), 0)
    index_v[...] = jnp.where(
        sub == 0,
        first,
        jnp.where(
            sub == 1,
            last,
            jnp.where(
                sub == 2,
                (last >= 0).astype(jnp.int32),
                (last > first).astype(jnp.int32),
            ),
        ),
    )
    fetch = pltpu.make_async_copy(index_v, index_s, copy_sem)
    fetch.start()
    for load in loads[1:]:
        load.wait()
    fetch.wait()

    lane = lax.broadcasted_iota(jnp.int32, (1, LANES), 1)

    def fill(o, carry):
        for c in range(2):
            k = jnp.minimum(jnp.maximum(index_s[c, o], 0), blocks - 1)
            there = index_s[2 + c, o]
            slot = 2 * o + c
            for axis in range(3):
                send[slot, axis : axis + 1, :] = frac_ref[axis, pl.ds(k, 1), :]
                send[slot, 3 + axis : 4 + axis, :] = norm_ref[axis, pl.ds(k, 1), :]
            send[slot, 6:7, :] = cell_ref[pl.ds(k, 1), :].astype(jnp.float32)
            header = jnp.where(lane == 0, tile_ref[k], jnp.where(lane == 1, count_ref[k] * there, 0))
            send[slot, 7:8, :] = header.astype(jnp.float32)
        return carry

    lax.fori_loop(0, devices, fill, 0, unroll=4)
    keep = pltpu.make_async_copy(
        send.at[pl.ds(2 * me, 2)], out_ref.at[pl.ds(2 * me, 2)], copy_sem
    )
    keep.start()
    pl.semaphore_wait(barrier, devices - 1)

    def ship(d, carry):
        flat, target = place(d)
        pltpu.make_async_remote_copy(
            src_ref=send.at[pl.ds(2 * flat, 2)],
            dst_ref=out_ref.at[pl.ds(2 * me, 2)],
            send_sem=send_sem, recv_sem=recv_sem,
            device_id=target, device_id_type=MESH,
        ).start()
        return carry

    lax.fori_loop(1, devices, ship, 0)
    keep.wait()
    most = pl.ds(0, 2 * (devices - 1))
    pltpu.make_async_copy(out_ref.at[most], out_ref.at[most], recv_sem).wait()
    pltpu.make_async_copy(send.at[most], send.at[most], send_sem).wait()


def route(tile, count, owner, fractions, normals, cells, count_x, count_y):
    slots = 2 * count_x * count_y
    operands = (tile, count, owner, fractions, normals, cells)

    def kernel(*refs):
        route_kernel(count_x, count_y, *refs)

    return pl.pallas_call(
        kernel,
        out_shape=jax.ShapeDtypeStruct((slots, 8, LANES), jnp.float32),
        in_specs=[pl.BlockSpec(memory_space=pl.ANY)] * 6,
        out_specs=pl.BlockSpec(memory_space=pl.ANY),
        scratch_shapes=[pltpu.SMEM(tile.shape, tile.dtype), pltpu.SMEM(count.shape, count.dtype)]
        + [pltpu.VMEM(one.shape, one.dtype) for one in operands[2:]]
        + [
            pltpu.VMEM((slots, 8, LANES), jnp.float32),
            pltpu.VMEM((8, LANES), jnp.int32),
            pltpu.SMEM((8, LANES), jnp.int32),
            pltpu.SemaphoreType.DMA((6,)),
            pltpu.SemaphoreType.DMA,
            pltpu.SemaphoreType.DMA,
            pltpu.SemaphoreType.DMA,
        ],
        compiler_params=pltpu.CompilerParams(
            collective_id=2, has_side_effects=True, vmem_limit_bytes=56 << 20
        ),
    )(*operands)


def split(value):
    high = value.astype(jnp.bfloat16)
    return high, (value - high.astype(jnp.float32)).astype(jnp.bfloat16)


def taps(anchor, offset, length):
    place = lax.broadcasted_iota(jnp.int32, (length, POINTS), 0).astype(jnp.float32)
    lower = place == anchor
    upper = place == anchor + 1.0
    weight = jnp.where(lower, 1.0 - offset, jnp.where(upper, offset, 0.0))
    slope = jnp.where(lower, -1.0, jnp.where(upper, 1.0, 0.0))
    return weight, slope


def splat_tile(block, count):
    lane = lax.broadcasted_iota(jnp.int32, (1, POINTS), 1)
    cell = block[6:7]
    remains = jnp.floor((cell + 0.5) * (1.0 / (CZ - 1)))
    plane = cell - remains * (CZ - 1)
    row = jnp.floor((remains + 0.5) * (1.0 / (TY - 1)))
    column = remains - row * (TY - 1)
    row = jnp.where(lane < count, row, -4.0)
    wx, sx = taps(row, block[0:1], TX)
    wy, sy = taps(column, block[1:2], TY)
    sy = sy * block[4:5]
    fz = block[2:3]
    level = block[3:4] * sx
    rise = block[5:6] * wx
    pairs = (
        ((1.0 - fz) * level - rise, fz * level + rise),
        ((1.0 - fz) * wx, fz * wx),
    )
    at = jnp.broadcast_to(plane, (2 * TX, POINTS)).astype(jnp.bfloat16)
    place = (lax.broadcasted_iota(jnp.int32, (2 * TX, POINTS), 0) // TX).astype(jnp.float32).astype(jnp.bfloat16)
    offset = at - place
    zero = jnp.zeros((2 * TX, POINTS), jnp.bfloat16)
    high, low = [], []
    for lower, upper in pairs:
        lower = split(jnp.concatenate([lower, lower], axis=0))
        upper = split(jnp.concatenate([upper, upper], axis=0))
        for kept, under, over in zip((high, low), lower, upper):
            kept.append(
                jnp.concatenate(
                    [
                        jnp.where(offset == 2 * j, under, jnp.where(offset == 2 * j - 1, over, zero))
                        for j in range(CZ // 2)
                    ],
                    axis=0,
                )
            )
    big_high = jnp.concatenate(high, axis=1)
    big_low = jnp.concatenate(low, axis=1)
    top = jnp.concatenate([wy, sy], axis=1)
    low = jnp.concatenate([jnp.zeros_like(wy), wy], axis=1)
    small_high, small_low = split(jnp.concatenate([top, low], axis=0))
    both = lax.dot_general(
        jnp.concatenate([small_high, small_low], axis=0),
        jnp.concatenate([big_high, big_low], axis=0),
        (((1,), (1,)), ((), ())),
        preferred_element_type=jnp.float32,
    )
    return both[: 2 * TY, :POINTS] + both[2 * TY :, :POINTS] + both[: 2 * TY, POINTS:]


def splat_kernel(blocks_ref, acc_ref, blocks, header_v, header_s, order, sem):
    slots = blocks_ref.shape[0]
    load = pltpu.make_async_copy(blocks_ref, blocks, sem)
    load.start()
    acc_ref[...] = jnp.zeros_like(acc_ref)
    load.wait()
    header_v[...] = blocks[:, 7, :].T[:8].astype(jnp.int32)
    fetch = pltpu.make_async_copy(header_v, header_s, sem)
    fetch.start()
    fetch.wait()

    def gather(i, carry):
        used, empty = carry
        some = header_s[1, i] > 0
        order[used] = i
        return used + some.astype(jnp.int32), jnp.where(some, empty, i)

    used, empty = lax.fori_loop(
        0, slots, gather, (jnp.int32(0), jnp.int32(0)), unroll=8
    )
    for extra in range(GROUP):
        order[used + extra] = empty

    def work(j, carry):
        made = []
        for u in range(GROUP):
            slot = order[j * GROUP + u]
            made.append((header_s[0, slot], splat_tile(blocks[slot], header_s[1, slot])))
        tiles_y = CY // TY
        for tile, values in made:
            x = tile // tiles_y
            y = pl.multiple_of((tile % tiles_y) * TY, TY)
            acc_ref[x, 0, pl.ds(y, TY), :] += values[:TY]
            acc_ref[x, 1, pl.ds(y, TY), :] += values[TY:]
        return carry

    lax.fori_loop(0, (used + GROUP - 1) // GROUP, work, 0)


def splat(blocks):
    slots = blocks.shape[0]
    return pl.pallas_call(
        splat_kernel,
        out_shape=jax.ShapeDtypeStruct((CX // TX, 2, CY, CZ * TX), jnp.float32),
        in_specs=[pl.BlockSpec(memory_space=pl.ANY)],
        out_specs=pl.BlockSpec(memory_space=pltpu.VMEM),
        scratch_shapes=[
            pltpu.VMEM(blocks.shape, blocks.dtype),
            pltpu.VMEM((8, slots), jnp.int32),
            pltpu.SMEM((8, slots), jnp.int32),
            pltpu.SMEM((slots + GROUP,), jnp.int32),
            pltpu.SemaphoreType.DMA,
        ],
        compiler_params=pltpu.CompilerParams(vmem_limit_bytes=24 << 20),
    )(blocks)


def fold(value):
    total = value[0:8]
    for k in range(1, value.shape[0] // 8):
        total = total + value[8 * k : 8 * k + 8]
    return total


def solve_kernel(
    count_x, count_y,
    acc_ref, x_ref, r_ref,
    rp, dg, p, s, w, rim,
    row_out, row_in, col_out, col_in, part_y, part_x, got_y, got_x,
    row_s, row_r, col_s, col_r, y_s, y_r, x_s, x_r,
):
    me_x, me_y = lax.axis_index("gx"), lax.axis_index("gy")

    def at(dx, dy):
        return (lax.rem(me_x + dx + count_x, count_x), lax.rem(me_y + dy + count_y, count_y))

    barrier = pltpu.get_barrier_semaphore()

    def greet_y(d, carry):
        pl.semaphore_signal(barrier, inc=1, device_id=at(0, d), device_id_type=MESH)
        return carry

    def greet_x(d, carry):
        pl.semaphore_signal(barrier, inc=1, device_id=at(d, 0), device_id_type=MESH)
        return carry

    lax.fori_loop(1, count_y, greet_y, 0)
    lax.fori_loop(1, count_x, greet_x, 0)
    for dx in (-1, 1):
        for dy in (-1, 1):
            pl.semaphore_signal(barrier, inc=1, device_id=at(dx, dy), device_id_type=MESH)

    sub8 = lax.broadcasted_iota(jnp.int32, (8, LANES), 0)
    lane8 = lax.broadcasted_iota(jnp.int32, (8, LANES), 1)
    lane_half = lax.broadcasted_iota(jnp.int32, (CX, LANES), 1)
    row_half = lax.broadcasted_iota(jnp.int32, (CX, LANES), 0)

    rp[0] = jnp.zeros((CX, CY), jnp.float32)
    rp[CZ + 1] = jnp.zeros((CX, CY), jnp.float32)

    def unfold(t, carry):
        rows = pl.ds(pl.multiple_of(t * TX, TX), TX)
        source = acc_ref[t, 0].T.reshape(CZ, TX, CY)
        density = acc_ref[t, 1].T.reshape(CZ, TX, CY)
        rp[1 : CZ + 1, rows, :] = source
        dg[:, rows, :] = 6.75 + screen_weight * density
        return carry

    lax.fori_loop(0, CX // TX, unfold, 0)

    def clear(z, carry):
        zero = jnp.zeros((CX, CY), jnp.float32)
        p[z] = zero
        s[z] = zero
        x_ref[z] = zero
        return carry

    lax.fori_loop(0, CZ, clear, 0)
    pl.semaphore_wait(barrier, (count_y - 1) + (count_x - 1) + 4)

    def pack(z, carry):
        west, east = carry
        for t in range(CX // TX):
            here = rp[z + 1, 8 * t : 8 * t + 8, :]
            shift = z + CZ * t
            mine = lane8 == shift
            west = jnp.where(mine, pltpu.roll(here[:, :LANES], shift, 1), west)
            turned = pltpu.roll(here[:, LANES:], lax.rem(shift + 1, LANES), 1)
            east = jnp.where(mine, turned, east)
        return west, east

    def ask(count, target, src, dst, send, recv):
        pltpu.make_async_remote_copy(
            src_ref=src, dst_ref=dst, send_sem=send, recv_sem=recv,
            device_id=target, device_id_type=MESH,
        ).start()

    def wait_for(ref, sem):
        pltpu.make_async_copy(ref, ref, sem).wait()

    zero8 = jnp.zeros((8, LANES), jnp.float32)

    def total_of(parts):
        total = parts[0]
        for k in range(1, parts.shape[0]):
            total = total + parts[k]
        return total

    def turn(it, carry):
        gamma_old, curve_old = carry
        row_out[it, 0] = rp[1 : CZ + 1, 0, :]
        row_out[it, 1] = rp[1 : CZ + 1, CX - 1, :]
        ask(0, at(-1, 0), row_out.at[it, 0], row_in.at[it, 1], row_s.at[it], row_r.at[it])
        ask(0, at(1, 0), row_out.at[it, 1], row_in.at[it, 0], row_s.at[it], row_r.at[it])
        west, east = lax.fori_loop(0, CZ, pack, (zero8, zero8))
        col_out[it, 0] = west
        col_out[it, 1] = east
        for dx in (-1, 0, 1):
            ask(0, at(dx, -1), col_out.at[it, 0], col_in.at[it, 1, 1 - dx], col_s.at[it], col_r.at[it])
            ask(0, at(dx, 1), col_out.at[it, 1], col_in.at[it, 0, 1 - dx], col_s.at[it], col_r.at[it])

        wait_for(row_in.at[it], row_r.at[it])
        zrow = lax.broadcasted_iota(jnp.int32, (CZ, CY), 0)
        for side, there in ((0, me_x > 0), (1, me_x < count_x - 1)):
            near = row_in[it, side]
            near = (
                near
                + jnp.where(zrow > 0, pltpu.roll(near, 1, 0), 0.0)
                + jnp.where(zrow < CZ - 1, pltpu.roll(near, CZ - 1, 0), 0.0)
            )
            near = jnp.where(there, near, 0.0)
            rim[side, 0] = near[:, :LANES]
            rim[side, 1] = near[:, LANES:]
        wait_for(col_in.at[it], col_r.at[it])

        plane8 = lax.rem(lane8, CZ)

        def column(side, there):
            def summed(k, ok):
                col = col_in[it, side, k]
                col = (
                    col
                    + jnp.where(plane8 > 0, pltpu.roll(col, 1, 1), 0.0)
                    + jnp.where(plane8 < CZ - 1, pltpu.roll(col, LANES - 1, 1), 0.0)
                )
                return jnp.where(ok, col, 0.0)

            mid = summed(1, there)
            low = summed(0, jnp.logical_and(there, me_x > 0))
            high = summed(2, jnp.logical_and(there, me_x < count_x - 1))

            def down(v):
                return pltpu.roll(v, 1, 0)

            def up(v):
                return pltpu.roll(v, 7, 0)

            before = jnp.where(lane8 < CZ, pltpu.roll(down(low), CZ, 1), pltpu.roll(down(mid), CZ, 1))
            before = jnp.where(sub8 == 0, before, down(mid))
            after = jnp.where(
                lane8 >= LANES - CZ,
                pltpu.roll(up(high), LANES - CZ, 1),
                pltpu.roll(up(mid), LANES - CZ, 1),
            )
            after = jnp.where(sub8 == 7, after, up(mid))
            return before + mid + after

        west_in = column(0, me_y > 0)
        east_in = column(1, me_y < count_y - 1)

        def apply(z, sums):
            gamma, delta, eta = sums
            halves = []
            for h in range(2):
                cols = slice(h * LANES, (h + 1) * LANES)
                u = rp[z, :, cols] + rp[z + 1, :, cols] + rp[z + 2, :, cols]
                above = rim[0, h, pl.ds(z, 1), :]
                below = rim[1, h, pl.ds(z, 1), :]
                t = (
                    u
                    + jnp.where(row_half == 0, above, pltpu.roll(u, 1, 0))
                    + jnp.where(row_half == CX - 1, below, pltpu.roll(u, CX - 1, 0))
                )
                halves.append(t)
            left, right = halves
            back = lax.rem(2 * LANES - z, LANES)
            west_col = jnp.concatenate(
                [pltpu.roll(west_in, lax.rem(back + LANES - CZ * t, LANES), 1) for t in range(CX // TX)],
                axis=0,
            )
            east_col = jnp.concatenate(
                [pltpu.roll(east_in, lax.rem(back + 2 * LANES - 1 - CZ * t, LANES), 1) for t in range(CX // TX)],
                axis=0,
            )
            lr, rr = pltpu.roll(left, 1, 1), pltpu.roll(right, 1, 1)
            ll, rl = pltpu.roll(left, LANES - 1, 1), pltpu.roll(right, LANES - 1, 1)
            first, last = lane_half == 0, lane_half == LANES - 1
            box_left = left + jnp.where(first, west_col, lr) + jnp.where(last, rl, ll)
            box_right = right + jnp.where(first, lr, rr) + jnp.where(last, east_col, rl)
            for h, box in ((0, box_left), (1, box_right)):
                cols = slice(h * LANES, (h + 1) * LANES)
                v = rp[z + 1, :, cols]
                image = dg[z, :, cols] * v - 0.25 * box
                w[z, :, cols] = image
                gamma = gamma + fold(v * v)
                delta = delta + fold(v * image)
                eta = eta + fold(v * s[z, :, cols])
            return gamma, delta, eta

        gamma, delta, eta = lax.fori_loop(0, CZ, apply, (zero8, zero8, zero8))
        gamma = jnp.sum(gamma, axis=0, keepdims=True)
        delta = jnp.sum(delta, axis=0, keepdims=True)
        eta = jnp.sum(eta, axis=0, keepdims=True)
        mine = jnp.where(sub8 == 0, gamma, jnp.where(sub8 == 1, delta, jnp.where(sub8 == 2, eta, 0.0)))
        part_y[it] = mine
        got_y[it, me_y] = mine

        def send_y(d, c):
            ask(0, at(0, d), part_y.at[it], got_y.at[it, me_y], y_s.at[it], y_r.at[it])
            return c

        lax.fori_loop(1, count_y, send_y, 0)
        wait_for(got_y.at[it, pl.ds(0, count_y - 1)], y_r.at[it])
        mine = total_of(got_y.at[it])
        part_x[it] = mine
        got_x[it, me_x] = mine

        def send_x(d, c):
            ask(0, at(d, 0), part_x.at[it], got_x.at[it, me_x], x_s.at[it], x_r.at[it])
            return c

        lax.fori_loop(1, count_x, send_x, 0)
        wait_for(got_x.at[it, pl.ds(0, count_x - 1)], x_r.at[it])
        total = jnp.sum(total_of(got_x.at[it]), axis=1, keepdims=True)
        gamma, delta, eta = total[0:1], total[1:2], total[2:3]
        beta = jnp.where(it == 0, 0.0, gamma / gamma_old)
        curve = delta + 2.0 * beta * eta + beta * beta * curve_old
        alpha = gamma / curve

        def update(z, c):
            r = rp[z + 1]
            pn = r + beta * p[z]
            sn = w[z] + beta * s[z]
            p[z] = pn
            s[z] = sn
            x_ref[z] = x_ref[z] + alpha * pn
            r = r - alpha * sn
            rp[z + 1] = r
            r_ref[z] = r
            return c

        lax.fori_loop(0, CZ, update, 0)
        return gamma, curve

    one = jnp.ones((1, 1), jnp.float32)
    lax.fori_loop(0, ITERS, turn, (one, 0.0 * one))

    def finish(it, c):
        wait_for(row_out.at[it], row_s.at[it])
        wait_for(col_in.at[it], col_s.at[it])
        wait_for(got_y.at[it, pl.ds(0, count_y - 1)], y_s.at[it])
        wait_for(got_x.at[it, pl.ds(0, count_x - 1)], x_s.at[it])
        return c

    lax.fori_loop(0, ITERS, finish, 0)


def solve(acc, count_x, count_y):
    vmem = pl.BlockSpec(memory_space=pltpu.VMEM)
    field = jax.ShapeDtypeStruct((CZ, CX, CY), jnp.float32)
    cells = (CZ, CX, CY)

    def kernel(*refs):
        solve_kernel(count_x, count_y, *refs)

    return pl.pallas_call(
        kernel,
        out_shape=(field, field),
        in_specs=[vmem],
        out_specs=(vmem, vmem),
        scratch_shapes=[
            pltpu.VMEM((CZ + 2, CX, CY), jnp.float32),
            pltpu.VMEM(cells, jnp.float32),
            pltpu.VMEM(cells, jnp.float32),
            pltpu.VMEM(cells, jnp.float32),
            pltpu.VMEM(cells, jnp.float32),
            pltpu.VMEM((2, 2, CZ, LANES), jnp.float32),
            pltpu.VMEM((ITERS, 2, CZ, CY), jnp.float32),
            pltpu.VMEM((ITERS, 2, CZ, CY), jnp.float32),
            pltpu.VMEM((ITERS, 2, 8, LANES), jnp.float32),
            pltpu.VMEM((ITERS, 2, 3, 8, LANES), jnp.float32),
            pltpu.VMEM((ITERS, 8, LANES), jnp.float32),
            pltpu.VMEM((ITERS, 8, LANES), jnp.float32),
            pltpu.VMEM((ITERS, count_y, 8, LANES), jnp.float32),
            pltpu.VMEM((ITERS, count_x, 8, LANES), jnp.float32),
        ]
        + [pltpu.SemaphoreType.DMA((ITERS,))] * 8,
        compiler_params=pltpu.CompilerParams(
            collective_id=0, has_side_effects=True, vmem_limit_bytes=32 << 20
        ),
    )(acc)


def blend_kernel(
    count_x, count_y,
    acc_ref, x_ref, r_ref, flag_ref,
    vs, dg, rim, sums,
    row_out, row_in, col_out, col_in, part_y, part_x, got_y, got_x,
    row_s, row_r, col_s, col_r, y_s, y_r, x_s, x_r,
):
    me_x, me_y = lax.axis_index("gx"), lax.axis_index("gy")

    def at(dx, dy):
        return (lax.rem(me_x + dx + count_x, count_x), lax.rem(me_y + dy + count_y, count_y))

    barrier = pltpu.get_barrier_semaphore()

    def greet_y(d, carry):
        pl.semaphore_signal(barrier, inc=1, device_id=at(0, d), device_id_type=MESH)
        return carry

    def greet_x(d, carry):
        pl.semaphore_signal(barrier, inc=1, device_id=at(d, 0), device_id_type=MESH)
        return carry

    lax.fori_loop(1, count_y, greet_y, 0)
    lax.fori_loop(1, count_x, greet_x, 0)
    for dx in (-1, 1):
        for dy in (-1, 1):
            pl.semaphore_signal(barrier, inc=1, device_id=at(dx, dy), device_id_type=MESH)

    tiles_x = CX // TX
    sub8 = lax.broadcasted_iota(jnp.int32, (8, LANES), 0)
    lane8 = lax.broadcasted_iota(jnp.int32, (8, LANES), 1)
    lane_half = lax.broadcasted_iota(jnp.int32, (CX, LANES), 1)
    row_half = lax.broadcasted_iota(jnp.int32, (CX, LANES), 0)
    plane8 = lax.rem(lane8, CZ)
    zrow = lax.broadcasted_iota(jnp.int32, (CZ, CY), 0)
    yrow = lax.broadcasted_iota(jnp.int32, (CZ, CY), 1)
    zero8 = jnp.zeros((8, LANES), jnp.float32)

    for k in range(ITERS):
        vs[k, 0] = jnp.zeros((CX, CY), jnp.float32)
        vs[k, CZ + 1] = jnp.zeros((CX, CY), jnp.float32)

    def unfold(t, carry):
        rows = pl.ds(pl.multiple_of(t * TX, TX), TX)
        vs[0, 1 : CZ + 1, rows, :] = acc_ref[t, 0].T.reshape(CZ, TX, CY)
        dg[:, rows, :] = (6.75 - SHIFT) + screen_weight * acc_ref[t, 1].T.reshape(CZ, TX, CY)
        return carry

    lax.fori_loop(0, tiles_x, unfold, 0)

    def collect(z, t, left, right, west, east):
        shift = z + CZ * t
        mine = lane8 == shift
        west = jnp.where(mine, pltpu.roll(left, shift, 1), west)
        east = jnp.where(mine, pltpu.roll(right, lax.rem(shift + 1, LANES), 1), east)
        return west, east

    def first(z, carry):
        west, east, norm = carry
        for t in range(tiles_x):
            left = vs[0, z + 1, 8 * t : 8 * t + 8, :LANES]
            right = vs[0, z + 1, 8 * t : 8 * t + 8, LANES:]
            west, east = collect(z, t, left, right, west, east)
            norm = norm + left * left + right * right
        return west, east, norm

    west, east, norm = lax.fori_loop(0, CZ, first, (zero8, zero8, zero8), unroll=4)
    sums[0] = norm
    pl.semaphore_wait(barrier, (count_y - 1) + (count_x - 1) + 4)

    def ask(target, src, dst, send, recv):
        pltpu.make_async_remote_copy(
            src_ref=src, dst_ref=dst, send_sem=send, recv_sem=recv,
            device_id=target, device_id_type=MESH,
        ).start()

    def wait_for(ref, sem):
        pltpu.make_async_copy(ref, ref, sem).wait()

    def share(it, west, east, low, high):
        col_out[it, 0] = west
        col_out[it, 1] = east
        for dx in (-1, 1, 0):
            ask(at(dx, -1), col_out.at[it, 0], col_in.at[it, 1, 1 - dx], col_s.at[it], col_r.at[it])
            ask(at(dx, 1), col_out.at[it, 1], col_in.at[it, 0, 1 - dx], col_s.at[it], col_r.at[it])
        row_out[it, 0] = low
        row_out[it, 1] = high
        ask(at(-1, 0), row_out.at[it, 0], row_in.at[it, 1], row_s.at[it], row_r.at[it])
        ask(at(1, 0), row_out.at[it, 1], row_in.at[it, 0], row_s.at[it], row_r.at[it])

    share(0, west, east, vs[0, 1 : CZ + 1, 0, :], vs[0, 1 : CZ + 1, CX - 1, :])

    zcol = lax.broadcasted_iota(jnp.int32, (CZ, LANES), 0)
    lane_z = lax.broadcasted_iota(jnp.int32, (CZ, LANES), 1)

    def turn(it, carry):
        def inner(z, c):
            west, east = c
            halves = []
            for h in range(2):
                cols = slice(h * LANES, (h + 1) * LANES)
                u = vs[it, z, :, cols] + vs[it, z + 1, :, cols] + vs[it, z + 2, :, cols]
                halves.append(
                    u
                    + jnp.where(row_half == 0, 0.0, pltpu.roll(u, 1, 0))
                    + jnp.where(row_half == CX - 1, 0.0, pltpu.roll(u, CX - 1, 0))
                )
            left, right = halves
            lr, rr = pltpu.roll(left, 1, 1), pltpu.roll(right, 1, 1)
            ll, rl = pltpu.roll(left, LANES - 1, 1), pltpu.roll(right, LANES - 1, 1)
            start, last = lane_half == 0, lane_half == LANES - 1
            box_left = left + jnp.where(start, 0.0, lr) + jnp.where(last, rl, ll)
            box_right = right + jnp.where(start, lr, rr) + jnp.where(last, 0.0, rl)
            made = []
            for h, box in ((0, box_left), (1, box_right)):
                cols = slice(h * LANES, (h + 1) * LANES)
                value = dg[z, :, cols] * vs[it, z + 1, :, cols] - 0.25 * box
                vs[it + 1, z + 1, :, cols] = value
                made.append(value)
            for t in range(tiles_x):
                rows = slice(8 * t, 8 * t + 8)
                west, east = collect(z, t, made[0][rows], made[1][rows], west, east)
            return west, east

        west, east = lax.fori_loop(0, CZ, inner, (zero8, zero8), unroll=4)

        wait_for(row_in.at[it], row_r.at[it])
        for side, there in ((0, me_x > 0), (1, me_x < count_x - 1)):
            near = row_in[it, side]
            near = (
                near
                + jnp.where(zrow > 0, pltpu.roll(near, 1, 0), 0.0)
                + jnp.where(zrow < CZ - 1, pltpu.roll(near, CZ - 1, 0), 0.0)
            )
            near = (
                near
                + jnp.where(yrow > 0, pltpu.roll(near, 1, 1), 0.0)
                + jnp.where(yrow < CY - 1, pltpu.roll(near, CY - 1, 1), 0.0)
            )
            near = jnp.where(there, 0.25 * near, 0.0)
            rim[side, 0] = near[:, :LANES]
            rim[side, 1] = near[:, LANES:]
        wait_for(col_in.at[it], col_r.at[it])

        def column(side, there):
            def summed(k, ok):
                col = col_in[it, side, k]
                col = (
                    col
                    + jnp.where(plane8 > 0, pltpu.roll(col, 1, 1), 0.0)
                    + jnp.where(plane8 < CZ - 1, pltpu.roll(col, LANES - 1, 1), 0.0)
                )
                return jnp.where(ok, 0.25 * col, 0.0)

            mid = summed(1, there)
            low = summed(0, jnp.logical_and(there, me_x > 0))
            high = summed(2, jnp.logical_and(there, me_x < count_x - 1))

            def down(v):
                return pltpu.roll(v, 1, 0)

            def up(v):
                return pltpu.roll(v, 7, 0)

            before = jnp.where(lane8 < CZ, pltpu.roll(down(low), CZ, 1), pltpu.roll(down(mid), CZ, 1))
            before = jnp.where(sub8 == 0, before, down(mid))
            after = jnp.where(
                lane8 >= LANES - CZ,
                pltpu.roll(up(high), LANES - CZ, 1),
                pltpu.roll(up(mid), LANES - CZ, 1),
            )
            after = jnp.where(sub8 == 7, after, up(mid))
            return before + mid + after

        west_in = column(0, me_y > 0)
        east_in = column(1, me_y < count_y - 1)

        @pl.when(it < ITERS - 1)
        def _():
            def packed(side, h, lane, first):
                column = jnp.broadcast_to(rim[side, h, :, lane : lane + 1], (CZ, LANES))
                return jnp.sum(jnp.where(lane_z == zcol + first, column, 0.0), axis=0, keepdims=True)

            def spread(column, sub, first):
                row = jnp.broadcast_to(column[sub : sub + 1], (CZ, LANES))
                return jnp.sum(jnp.where(lane_z == zcol + first, row, 0.0), axis=1, keepdims=True)

            final = LANES - CZ

            def corners(column, fix, h, lane):
                return (
                    column
                    - fix
                    - jnp.where(sub8 == 0, packed(0, h, lane, 0), 0.0)
                    - jnp.where(sub8 == 7, packed(1, h, lane, final), 0.0)
                )

            def row(side, sub, first):
                near = vs[it + 1, 1 : CZ + 1, (CX - 1) * side, :]
                left = near[:, :LANES] - jnp.where(lane_z == 0, spread(west_in, sub, first), 0.0)
                right = near[:, LANES:] - jnp.where(lane_z == LANES - 1, spread(east_in, sub, first), 0.0)
                return jnp.concatenate([left - rim[side, 0], right - rim[side, 1]], axis=1)

            share(
                it + 1,
                corners(west, west_in, 0, 0),
                corners(east, east_in, 1, LANES - 1),
                row(0, 0, 0),
                row(1, 7, final),
            )

        def edge(z, carry):
            cross, norm = carry
            for t in range(tiles_x):
                rows = slice(8 * t, 8 * t + 8)
                shift = z + CZ * t
                fixes = [
                    jnp.where(lane8 == 0, pltpu.roll(west_in, lax.rem(2 * LANES - shift, LANES), 1), 0.0),
                    jnp.where(lane8 == LANES - 1, pltpu.roll(east_in, 2 * LANES - 1 - shift - LANES, 1), 0.0),
                ]
                for h in range(2):
                    cols = slice(h * LANES, (h + 1) * LANES)
                    value = vs[it + 1, z + 1, rows, cols] - fixes[h]
                    if t == 0:
                        value = value - jnp.where(sub8 == 0, rim[0, h, pl.ds(z, 1), :], 0.0)
                    if t == tiles_x - 1:
                        value = value - jnp.where(sub8 == 7, rim[1, h, pl.ds(z, 1), :], 0.0)
                    vs[it + 1, z + 1, rows, cols] = value
                    cross = cross + value * vs[it, z + 1, rows, cols]
                    norm = norm + value * value
            return cross, norm

        cross, norm = lax.fori_loop(0, CZ, edge, (zero8, zero8), unroll=4)
        sums[2 * it + 1] = cross
        sums[2 * it + 2] = norm
        return carry

    lax.fori_loop(0, ITERS, turn, 0)

    mine = zero8
    for k in range(2 * ITERS + 1):
        mine = jnp.where(sub8 == k, jnp.sum(sums[k], axis=0, keepdims=True), mine)
    part_y[...] = mine
    got_y[me_y] = mine

    def send_y(d, c):
        ask(at(0, d), part_y, got_y.at[me_y], y_s, y_r)
        return c

    lax.fori_loop(1, count_y, send_y, 0)
    wait_for(got_y.at[pl.ds(0, count_y - 1)], y_r)

    def total_of(parts):
        total = parts[0]
        for k in range(1, parts.shape[0]):
            total = total + parts[k]
        return total

    mine = total_of(got_y)
    part_x[...] = mine
    got_x[me_x] = mine

    def send_x(d, c):
        ask(at(d, 0), part_x, got_x.at[me_x], x_s, x_r)
        return c

    lax.fori_loop(1, count_x, send_x, 0)
    wait_for(got_x.at[pl.ds(0, count_x - 1)], x_r)
    total = jnp.sum(total_of(got_x), axis=1, keepdims=True)
    moment = [total[k : k + 1] for k in range(2 * ITERS + 1)]

    good = jnp.ones((1, 1), jnp.float32)

    def product(a, b, good):
        value, size = 0.0, 0.0
        for d in range(len(a) + len(b) - 1):
            pairs = [a[i] * b[d - i] for i in range(len(a)) if 0 <= d - i < len(b)]
            both = pairs[0]
            bulk = jnp.abs(pairs[0])
            for pair in pairs[1:]:
                both = both + pair
                bulk = bulk + jnp.abs(pair)
            value = value + both * moment[d]
            size = size + bulk * jnp.abs(moment[d])
        return value, jnp.where(size <= TRUST * value, good, 0.0)

    def image(a):
        padded = [SHIFT * c for c in a] + [None]
        return [
            (padded[i] if i == 0 else a[i - 1] if i == len(a) else padded[i] + a[i - 1])
            for i in range(len(a) + 1)
        ]

    def plus(a, factor, b):
        longest = max(len(a), len(b))
        made = []
        for i in range(longest):
            if i >= len(a):
                made.append(factor * b[i])
            elif i >= len(b):
                made.append(a[i])
            else:
                made.append(a[i] + factor * b[i])
        return made

    one = jnp.ones((1, 1), jnp.float32)
    residual, direction, answer = [one], [one], []
    gamma, good = product(residual, residual, good)
    for it in range(ITERS):
        curve, good = product(direction, image(direction), good)
        alpha = gamma / curve
        answer = plus(answer, alpha, direction)
        residual = plus(residual, -alpha, image(direction))
        fresh, good = product(residual, residual, good)
        direction = plus(residual, fresh / gamma, direction)
        gamma = fresh
    flag_ref[...] = good

    def combine(z, c):
        for h in range(2):
            cols = slice(h * LANES, (h + 1) * LANES)
            fields = [vs[k, z + 1, :, cols] for k in range(ITERS + 1)]
            x_ref[z, :, cols] = sum(answer[k] * fields[k] for k in range(ITERS))
            r_ref[z, :, cols] = sum(residual[k] * fields[k] for k in range(ITERS + 1))
        return c

    lax.fori_loop(0, CZ, combine, 0, unroll=2)

    def finish(it, c):
        wait_for(row_out.at[it], row_s.at[it])
        wait_for(col_in.at[it], col_s.at[it])
        return c

    lax.fori_loop(0, ITERS, finish, 0)
    wait_for(got_y.at[pl.ds(0, count_y - 1)], y_s)
    wait_for(got_x.at[pl.ds(0, count_x - 1)], x_s)


def blend(acc, count_x, count_y):
    vmem = pl.BlockSpec(memory_space=pltpu.VMEM)
    field = jax.ShapeDtypeStruct((CZ, CX, CY), jnp.float32)

    def kernel(*refs):
        blend_kernel(count_x, count_y, *refs)

    return pl.pallas_call(
        kernel,
        out_shape=(field, field, jax.ShapeDtypeStruct((1, 1), jnp.float32)),
        in_specs=[vmem],
        out_specs=(vmem, vmem, vmem),
        scratch_shapes=[
            pltpu.VMEM((ITERS + 1, CZ + 2, CX, CY), jnp.float32),
            pltpu.VMEM((CZ, CX, CY), jnp.float32),
            pltpu.VMEM((2, 2, CZ, LANES), jnp.float32),
            pltpu.VMEM((2 * ITERS + 1, 8, LANES), jnp.float32),
            pltpu.VMEM((ITERS, 2, CZ, CY), jnp.float32),
            pltpu.VMEM((ITERS, 2, CZ, CY), jnp.float32),
            pltpu.VMEM((ITERS, 2, 8, LANES), jnp.float32),
            pltpu.VMEM((ITERS, 2, 3, 8, LANES), jnp.float32),
            pltpu.VMEM((8, LANES), jnp.float32),
            pltpu.VMEM((8, LANES), jnp.float32),
            pltpu.VMEM((count_y, 8, LANES), jnp.float32),
            pltpu.VMEM((count_x, 8, LANES), jnp.float32),
        ]
        + [pltpu.SemaphoreType.DMA((ITERS,))] * 4
        + [pltpu.SemaphoreType.DMA] * 4,
        compiler_params=pltpu.CompilerParams(
            collective_id=1, has_side_effects=True, vmem_limit_bytes=32 << 20
        ),
    )(acc)


def local(fractions, normals, point_cells, block_owner, block_tile, block_count):
    count_x, count_y = lax.axis_size("gx"), lax.axis_size("gy")
    got = route(
        block_tile,
        block_count,
        block_owner.reshape(1, -1),
        jnp.transpose(fractions, (1, 0, 2)),
        jnp.transpose(normals, (1, 0, 2)),
        point_cells,
        count_x,
        count_y,
    )
    acc = splat(got)
    x, r, flag = blend(acc, count_x, count_y)
    return lax.cond(
        flag[0, 0] > 0.5,
        lambda acc, x, r: (x, r),
        lambda acc, x, r: tuple(solve(acc, count_x, count_y)),
        acc, x, r,
    )


def solution(mesh):
    placed = (
        P(("gx", "gy"), None, None),
        P(("gx", "gy"), None, None),
        P(("gx", "gy"), None),
        P(("gx", "gy"), None),
        P(("gx", "gy")),
        P(("gx", "gy")),
    )
    return jax.shard_map(
        local,
        mesh=mesh,
        in_specs=placed,
        out_specs=(P(None, "gx", "gy"), P(None, "gx", "gy")),
        check_vma=False,
    )
```

```python
import jax
import jax.numpy as jnp
from jax import lax
from jax.experimental import pallas as pl
from jax.experimental.pallas import tpu as pltpu
from jax.sharding import PartitionSpec as P

CX = 64
CY = 256
CZ = 16
TX = 8
TY = 16
POINTS = 128
ITERS = 3
LANES = 128
GROUP = 64
SHIFT = 6.5
STRIDE = 37
TRUST = 100.0

screen_weight = 4.0
MESH = pl.DeviceIdType.MESH


def route_kernel(
    count_x, count_y,
    tile_in, count_in, owner_in, frac_in, norm_in, cell_in, out_ref,
    tile_ref, count_ref, owner_ref, frac_ref, norm_ref, cell_ref,
    send, index_v, index_s, load_sem, copy_sem, send_sem, recv_sem,
):
    devices = count_x * count_y
    blocks = cell_ref.shape[0]
    loads = [
        pltpu.make_async_copy(source, target, load_sem.at[k])
        for k, (source, target) in enumerate(
            (
                (owner_in, owner_ref),
                (tile_in, tile_ref),
                (count_in, count_ref),
                (frac_in, frac_ref),
                (norm_in, norm_ref),
                (cell_in, cell_ref),
            )
        )
    ]
    for load in loads:
        load.start()
    me = lax.axis_index("gx") * count_y + lax.axis_index("gy")

    def place(d):
        flat = lax.rem(me + lax.rem(d * STRIDE, devices), devices)
        return flat, (flat // count_y, lax.rem(flat, count_y))

    barrier = pltpu.get_barrier_semaphore()

    def greet(d, carry):
        pl.semaphore_signal(barrier, inc=1, device_id=place(d)[1], device_id_type=MESH)
        return carry

    lax.fori_loop(1, devices, greet, 0)

    loads[0].wait()
    owner = jnp.broadcast_to(owner_ref[...], (devices, blocks)).T
    block = lax.broadcasted_iota(jnp.int32, (blocks, devices), 0)
    named = owner == lax.broadcasted_iota(jnp.int32, (blocks, devices), 1)
    first = jnp.min(jnp.where(named, block, blocks), axis=0, keepdims=True)
    last = jnp.max(jnp.where(named, block, -1), axis=0, keepdims=True)
    sub = lax.broadcasted_iota(jnp.int32, (8, devices), 0)
    index_v[...] = jnp.where(
        sub == 0,
        first,
        jnp.where(
            sub == 1,
            last,
            jnp.where(
                sub == 2,
                (last >= 0).astype(jnp.int32),
                (last > first).astype(jnp.int32),
            ),
        ),
    )
    fetch = pltpu.make_async_copy(index_v, index_s, copy_sem)
    fetch.start()
    for load in loads[1:]:
        load.wait()
    fetch.wait()

    lane = lax.broadcasted_iota(jnp.int32, (1, LANES), 1)

    def fill(o):
        for c in range(2):
            k = jnp.minimum(jnp.maximum(index_s[c, o], 0), blocks - 1)
            there = index_s[2 + c, o]
            slot = 2 * o + c
            for axis in range(3):
                send[slot, axis : axis + 1, :] = frac_ref[axis, pl.ds(k, 1), :]
                send[slot, 3 + axis : 4 + axis, :] = norm_ref[axis, pl.ds(k, 1), :]
            send[slot, 6:7, :] = cell_ref[pl.ds(k, 1), :].astype(jnp.float32)
            header = jnp.where(lane == 0, tile_ref[k], jnp.where(lane == 1, count_ref[k] * there, 0))
            send[slot, 7:8, :] = header.astype(jnp.float32)

    pl.semaphore_wait(barrier, devices - 1)

    def ship(d, carry):
        flat, target = place(d)
        fill(flat)
        pltpu.make_async_remote_copy(
            src_ref=send.at[pl.ds(2 * flat, 2)],
            dst_ref=out_ref.at[pl.ds(2 * me, 2)],
            send_sem=send_sem, recv_sem=recv_sem,
            device_id=target, device_id_type=MESH,
        ).start()
        return carry

    lax.fori_loop(1, devices, ship, 0)
    fill(me)
    keep = pltpu.make_async_copy(
        send.at[pl.ds(2 * me, 2)], out_ref.at[pl.ds(2 * me, 2)], copy_sem
    )
    keep.start()
    keep.wait()
    most = pl.ds(0, 2 * (devices - 1))
    pltpu.make_async_copy(out_ref.at[most], out_ref.at[most], recv_sem).wait()
    pltpu.make_async_copy(send.at[most], send.at[most], send_sem).wait()


def route(tile, count, owner, fractions, normals, cells, count_x, count_y):
    slots = 2 * count_x * count_y
    operands = (tile, count, owner, fractions, normals, cells)

    def kernel(*refs):
        route_kernel(count_x, count_y, *refs)

    return pl.pallas_call(
        kernel,
        out_shape=jax.ShapeDtypeStruct((slots, 8, LANES), jnp.float32),
        in_specs=[pl.BlockSpec(memory_space=pl.ANY)] * 6,
        out_specs=pl.BlockSpec(memory_space=pl.ANY),
        scratch_shapes=[pltpu.SMEM(tile.shape, tile.dtype), pltpu.SMEM(count.shape, count.dtype)]
        + [pltpu.VMEM(one.shape, one.dtype) for one in operands[2:]]
        + [
            pltpu.VMEM((slots, 8, LANES), jnp.float32),
            pltpu.VMEM((8, LANES), jnp.int32),
            pltpu.SMEM((8, LANES), jnp.int32),
            pltpu.SemaphoreType.DMA((6,)),
            pltpu.SemaphoreType.DMA,
            pltpu.SemaphoreType.DMA,
            pltpu.SemaphoreType.DMA,
        ],
        compiler_params=pltpu.CompilerParams(
            collective_id=2, has_side_effects=True, vmem_limit_bytes=56 << 20
        ),
    )(*operands)


def split(value):
    high = value.astype(jnp.bfloat16)
    return high, (value - high.astype(jnp.float32)).astype(jnp.bfloat16)


def taps(anchor, offset, length):
    place = lax.broadcasted_iota(jnp.int32, (length, POINTS), 0).astype(jnp.float32)
    lower = place == anchor
    upper = place == anchor + 1.0
    weight = jnp.where(lower, 1.0 - offset, jnp.where(upper, offset, 0.0))
    slope = jnp.where(lower, -1.0, jnp.where(upper, 1.0, 0.0))
    return weight, slope


def splat_tile(block, count):
    lane = lax.broadcasted_iota(jnp.int32, (1, POINTS), 1)
    cell = block[6:7]
    remains = jnp.floor((cell + 0.5) * (1.0 / (CZ - 1)))
    plane = cell - remains * (CZ - 1)
    row = jnp.floor((remains + 0.5) * (1.0 / (TY - 1)))
    column = remains - row * (TY - 1)
    row = jnp.where(lane < count, row, -4.0)
    wx, sx = taps(row, block[0:1], TX)
    wy, sy = taps(column, block[1:2], TY)
    sy = sy * block[4:5]
    fz = block[2:3]
    level = block[3:4] * sx
    rise = block[5:6] * wx
    pairs = (
        ((1.0 - fz) * level - rise, fz * level + rise),
        ((1.0 - fz) * wx, fz * wx),
    )
    at = jnp.broadcast_to(plane, (2 * TX, POINTS)).astype(jnp.bfloat16)
    place = (lax.broadcasted_iota(jnp.int32, (2 * TX, POINTS), 0) // TX).astype(jnp.float32).astype(jnp.bfloat16)
    offset = at - place
    zero = jnp.zeros((2 * TX, POINTS), jnp.bfloat16)
    high, low = [], []
    for lower, upper in pairs:
        lower = split(jnp.concatenate([lower, lower], axis=0))
        upper = split(jnp.concatenate([upper, upper], axis=0))
        for kept, under, over in zip((high, low), lower, upper):
            kept.append(
                jnp.concatenate(
                    [
                        jnp.where(offset == 2 * j, under, jnp.where(offset == 2 * j - 1, over, zero))
                        for j in range(CZ // 2)
                    ],
                    axis=0,
                )
            )
    big_high = jnp.concatenate(high, axis=1)
    big_low = jnp.concatenate(low, axis=1)
    top = jnp.concatenate([wy, sy], axis=1)
    low = jnp.concatenate([jnp.zeros_like(wy), wy], axis=1)
    small_high, small_low = split(jnp.concatenate([top, low], axis=0))
    both = lax.dot_general(
        jnp.concatenate([small_high, small_low], axis=0),
        jnp.concatenate([big_high, big_low], axis=0),
        (((1,), (1,)), ((), ())),
        preferred_element_type=jnp.float32,
    )
    return both[: 2 * TY, :POINTS] + both[2 * TY :, :POINTS] + both[: 2 * TY, POINTS:]


def splat_kernel(blocks_ref, acc_ref, blocks, header_v, header_s, order, sem):
    slots = blocks_ref.shape[0]
    load = pltpu.make_async_copy(blocks_ref, blocks, sem)
    load.start()
    acc_ref[...] = jnp.zeros_like(acc_ref)
    load.wait()
    header_v[...] = blocks[:, 7, :].T[:8].astype(jnp.int32)
    fetch = pltpu.make_async_copy(header_v, header_s, sem)
    fetch.start()
    fetch.wait()

    def gather(i, carry):
        used, empty = carry
        some = header_s[1, i] > 0
        order[used] = i
        return used + some.astype(jnp.int32), jnp.where(some, empty, i)

    used, empty = lax.fori_loop(
        0, slots, gather, (jnp.int32(0), jnp.int32(0)), unroll=8
    )
    for extra in range(GROUP):
        order[used + extra] = empty

    def work(j, carry):
        made = []
        for u in range(GROUP):
            slot = order[j * GROUP + u]
            made.append((header_s[0, slot], splat_tile(blocks[slot], header_s[1, slot])))
        tiles_y = CY // TY
        for tile, values in made:
            x = tile // tiles_y
            y = pl.multiple_of((tile % tiles_y) * TY, TY)
            acc_ref[x, 0, pl.ds(y, TY), :] += values[:TY]
            acc_ref[x, 1, pl.ds(y, TY), :] += values[TY:]
        return carry

    lax.fori_loop(0, (used + GROUP - 1) // GROUP, work, 0)


def splat(blocks):
    slots = blocks.shape[0]
    return pl.pallas_call(
        splat_kernel,
        out_shape=jax.ShapeDtypeStruct((CX // TX, 2, CY, CZ * TX), jnp.float32),
        in_specs=[pl.BlockSpec(memory_space=pl.ANY)],
        out_specs=pl.BlockSpec(memory_space=pltpu.VMEM),
        scratch_shapes=[
            pltpu.VMEM(blocks.shape, blocks.dtype),
            pltpu.VMEM((8, slots), jnp.int32),
            pltpu.SMEM((8, slots), jnp.int32),
            pltpu.SMEM((slots + GROUP,), jnp.int32),
            pltpu.SemaphoreType.DMA,
        ],
        compiler_params=pltpu.CompilerParams(vmem_limit_bytes=24 << 20),
    )(blocks)


def fold(value):
    total = value[0:8]
    for k in range(1, value.shape[0] // 8):
        total = total + value[8 * k : 8 * k + 8]
    return total


def solve_kernel(
    count_x, count_y,
    acc_ref, x_ref, r_ref,
    rp, dg, p, s, w, rim,
    row_out, row_in, col_out, col_in, part_y, part_x, got_y, got_x,
    row_s, row_r, col_s, col_r, y_s, y_r, x_s, x_r,
):
    me_x, me_y = lax.axis_index("gx"), lax.axis_index("gy")

    def at(dx, dy):
        return (lax.rem(me_x + dx + count_x, count_x), lax.rem(me_y + dy + count_y, count_y))

    barrier = pltpu.get_barrier_semaphore()

    def greet_y(d, carry):
        pl.semaphore_signal(barrier, inc=1, device_id=at(0, d), device_id_type=MESH)
        return carry

    def greet_x(d, carry):
        pl.semaphore_signal(barrier, inc=1, device_id=at(d, 0), device_id_type=MESH)
        return carry

    lax.fori_loop(1, count_y, greet_y, 0)
    lax.fori_loop(1, count_x, greet_x, 0)
    for dx in (-1, 1):
        for dy in (-1, 1):
            pl.semaphore_signal(barrier, inc=1, device_id=at(dx, dy), device_id_type=MESH)

    sub8 = lax.broadcasted_iota(jnp.int32, (8, LANES), 0)
    lane8 = lax.broadcasted_iota(jnp.int32, (8, LANES), 1)
    lane_half = lax.broadcasted_iota(jnp.int32, (CX, LANES), 1)
    row_half = lax.broadcasted_iota(jnp.int32, (CX, LANES), 0)

    rp[0] = jnp.zeros((CX, CY), jnp.float32)
    rp[CZ + 1] = jnp.zeros((CX, CY), jnp.float32)

    def unfold(t, carry):
        rows = pl.ds(pl.multiple_of(t * TX, TX), TX)
        source = acc_ref[t, 0].T.reshape(CZ, TX, CY)
        density = acc_ref[t, 1].T.reshape(CZ, TX, CY)
        rp[1 : CZ + 1, rows, :] = source
        dg[:, rows, :] = 6.75 + screen_weight * density
        return carry

    lax.fori_loop(0, CX // TX, unfold, 0)

    def clear(z, carry):
        zero = jnp.zeros((CX, CY), jnp.float32)
        p[z] = zero
        s[z] = zero
        x_ref[z] = zero
        return carry

    lax.fori_loop(0, CZ, clear, 0)
    pl.semaphore_wait(barrier, (count_y - 1) + (count_x - 1) + 4)

    def pack(z, carry):
        west, east = carry
        for t in range(CX // TX):
            here = rp[z + 1, 8 * t : 8 * t + 8, :]
            shift = z + CZ * t
            mine = lane8 == shift
            west = jnp.where(mine, pltpu.roll(here[:, :LANES], shift, 1), west)
            turned = pltpu.roll(here[:, LANES:], lax.rem(shift + 1, LANES), 1)
            east = jnp.where(mine, turned, east)
        return west, east

    def ask(count, target, src, dst, send, recv):
        pltpu.make_async_remote_copy(
            src_ref=src, dst_ref=dst, send_sem=send, recv_sem=recv,
            device_id=target, device_id_type=MESH,
        ).start()

    def wait_for(ref, sem):
        pltpu.make_async_copy(ref, ref, sem).wait()

    zero8 = jnp.zeros((8, LANES), jnp.float32)

    def total_of(parts):
        total = parts[0]
        for k in range(1, parts.shape[0]):
            total = total + parts[k]
        return total

    def turn(it, carry):
        gamma_old, curve_old = carry
        row_out[it, 0] = rp[1 : CZ + 1, 0, :]
        row_out[it, 1] = rp[1 : CZ + 1, CX - 1, :]
        ask(0, at(-1, 0), row_out.at[it, 0], row_in.at[it, 1], row_s.at[it], row_r.at[it])
        ask(0, at(1, 0), row_out.at[it, 1], row_in.at[it, 0], row_s.at[it], row_r.at[it])
        west, east = lax.fori_loop(0, CZ, pack, (zero8, zero8))
        col_out[it, 0] = west
        col_out[it, 1] = east
        for dx in (-1, 0, 1):
            ask(0, at(dx, -1), col_out.at[it, 0], col_in.at[it, 1, 1 - dx], col_s.at[it], col_r.at[it])
            ask(0, at(dx, 1), col_out.at[it, 1], col_in.at[it, 0, 1 - dx], col_s.at[it], col_r.at[it])

        wait_for(row_in.at[it], row_r.at[it])
        zrow = lax.broadcasted_iota(jnp.int32, (CZ, CY), 0)
        for side, there in ((0, me_x > 0), (1, me_x < count_x - 1)):
            near = row_in[it, side]
            near = (
                near
                + jnp.where(zrow > 0, pltpu.roll(near, 1, 0), 0.0)
                + jnp.where(zrow < CZ - 1, pltpu.roll(near, CZ - 1, 0), 0.0)
            )
            near = jnp.where(there, near, 0.0)
            rim[side, 0] = near[:, :LANES]
            rim[side, 1] = near[:, LANES:]
        wait_for(col_in.at[it], col_r.at[it])

        plane8 = lax.rem(lane8, CZ)

        def column(side, there):
            def summed(k, ok):
                col = col_in[it, side, k]
                col = (
                    col
                    + jnp.where(plane8 > 0, pltpu.roll(col, 1, 1), 0.0)
                    + jnp.where(plane8 < CZ - 1, pltpu.roll(col, LANES - 1, 1), 0.0)
                )
                return jnp.where(ok, col, 0.0)

            mid = summed(1, there)
            low = summed(0, jnp.logical_and(there, me_x > 0))
            high = summed(2, jnp.logical_and(there, me_x < count_x - 1))

            def down(v):
                return pltpu.roll(v, 1, 0)

            def up(v):
                return pltpu.roll(v, 7, 0)

            before = jnp.where(lane8 < CZ, pltpu.roll(down(low), CZ, 1), pltpu.roll(down(mid), CZ, 1))
            before = jnp.where(sub8 == 0, before, down(mid))
            after = jnp.where(
                lane8 >= LANES - CZ,
                pltpu.roll(up(high), LANES - CZ, 1),
                pltpu.roll(up(mid), LANES - CZ, 1),
            )
            after = jnp.where(sub8 == 7, after, up(mid))
            return before + mid + after

        west_in = column(0, me_y > 0)
        east_in = column(1, me_y < count_y - 1)

        def apply(z, sums):
            gamma, delta, eta = sums
            halves = []
            for h in range(2):
                cols = slice(h * LANES, (h + 1) * LANES)
                u = rp[z, :, cols] + rp[z + 1, :, cols] + rp[z + 2, :, cols]
                above = rim[0, h, pl.ds(z, 1), :]
                below = rim[1, h, pl.ds(z, 1), :]
                t = (
                    u
                    + jnp.where(row_half == 0, above, pltpu.roll(u, 1, 0))
                    + jnp.where(row_half == CX - 1, below, pltpu.roll(u, CX - 1, 0))
                )
                halves.append(t)
            left, right = halves
            back = lax.rem(2 * LANES - z, LANES)
            west_col = jnp.concatenate(
                [pltpu.roll(west_in, lax.rem(back + LANES - CZ * t, LANES), 1) for t in range(CX // TX)],
                axis=0,
            )
            east_col = jnp.concatenate(
                [pltpu.roll(east_in, lax.rem(back + 2 * LANES - 1 - CZ * t, LANES), 1) for t in range(CX // TX)],
                axis=0,
            )
            lr, rr = pltpu.roll(left, 1, 1), pltpu.roll(right, 1, 1)
            ll, rl = pltpu.roll(left, LANES - 1, 1), pltpu.roll(right, LANES - 1, 1)
            first, last = lane_half == 0, lane_half == LANES - 1
            box_left = left + jnp.where(first, west_col, lr) + jnp.where(last, rl, ll)
            box_right = right + jnp.where(first, lr, rr) + jnp.where(last, east_col, rl)
            for h, box in ((0, box_left), (1, box_right)):
                cols = slice(h * LANES, (h + 1) * LANES)
                v = rp[z + 1, :, cols]
                image = dg[z, :, cols] * v - 0.25 * box
                w[z, :, cols] = image
                gamma = gamma + fold(v * v)
                delta = delta + fold(v * image)
                eta = eta + fold(v * s[z, :, cols])
            return gamma, delta, eta

        gamma, delta, eta = lax.fori_loop(0, CZ, apply, (zero8, zero8, zero8))
        gamma = jnp.sum(gamma, axis=0, keepdims=True)
        delta = jnp.sum(delta, axis=0, keepdims=True)
        eta = jnp.sum(eta, axis=0, keepdims=True)
        mine = jnp.where(sub8 == 0, gamma, jnp.where(sub8 == 1, delta, jnp.where(sub8 == 2, eta, 0.0)))
        part_y[it] = mine
        got_y[it, me_y] = mine

        def send_y(d, c):
            ask(0, at(0, d), part_y.at[it], got_y.at[it, me_y], y_s.at[it], y_r.at[it])
            return c

        lax.fori_loop(1, count_y, send_y, 0)
        wait_for(got_y.at[it, pl.ds(0, count_y - 1)], y_r.at[it])
        mine = total_of(got_y.at[it])
        part_x[it] = mine
        got_x[it, me_x] = mine

        def send_x(d, c):
            ask(0, at(d, 0), part_x.at[it], got_x.at[it, me_x], x_s.at[it], x_r.at[it])
            return c

        lax.fori_loop(1, count_x, send_x, 0)
        wait_for(got_x.at[it, pl.ds(0, count_x - 1)], x_r.at[it])
        total = jnp.sum(total_of(got_x.at[it]), axis=1, keepdims=True)
        gamma, delta, eta = total[0:1], total[1:2], total[2:3]
        beta = jnp.where(it == 0, 0.0, gamma / gamma_old)
        curve = delta + 2.0 * beta * eta + beta * beta * curve_old
        alpha = gamma / curve

        def update(z, c):
            r = rp[z + 1]
            pn = r + beta * p[z]
            sn = w[z] + beta * s[z]
            p[z] = pn
            s[z] = sn
            x_ref[z] = x_ref[z] + alpha * pn
            r = r - alpha * sn
            rp[z + 1] = r
            r_ref[z] = r
            return c

        lax.fori_loop(0, CZ, update, 0)
        return gamma, curve

    one = jnp.ones((1, 1), jnp.float32)
    lax.fori_loop(0, ITERS, turn, (one, 0.0 * one))

    def finish(it, c):
        wait_for(row_out.at[it], row_s.at[it])
        wait_for(col_in.at[it], col_s.at[it])
        wait_for(got_y.at[it, pl.ds(0, count_y - 1)], y_s.at[it])
        wait_for(got_x.at[it, pl.ds(0, count_x - 1)], x_s.at[it])
        return c

    lax.fori_loop(0, ITERS, finish, 0)


def solve(acc, count_x, count_y):
    vmem = pl.BlockSpec(memory_space=pltpu.VMEM)
    field = jax.ShapeDtypeStruct((CZ, CX, CY), jnp.float32)
    cells = (CZ, CX, CY)

    def kernel(*refs):
        solve_kernel(count_x, count_y, *refs)

    return pl.pallas_call(
        kernel,
        out_shape=(field, field),
        in_specs=[vmem],
        out_specs=(vmem, vmem),
        scratch_shapes=[
            pltpu.VMEM((CZ + 2, CX, CY), jnp.float32),
            pltpu.VMEM(cells, jnp.float32),
            pltpu.VMEM(cells, jnp.float32),
            pltpu.VMEM(cells, jnp.float32),
            pltpu.VMEM(cells, jnp.float32),
            pltpu.VMEM((2, 2, CZ, LANES), jnp.float32),
            pltpu.VMEM((ITERS, 2, CZ, CY), jnp.float32),
            pltpu.VMEM((ITERS, 2, CZ, CY), jnp.float32),
            pltpu.VMEM((ITERS, 2, 8, LANES), jnp.float32),
            pltpu.VMEM((ITERS, 2, 3, 8, LANES), jnp.float32),
            pltpu.VMEM((ITERS, 8, LANES), jnp.float32),
            pltpu.VMEM((ITERS, 8, LANES), jnp.float32),
            pltpu.VMEM((ITERS, count_y, 8, LANES), jnp.float32),
            pltpu.VMEM((ITERS, count_x, 8, LANES), jnp.float32),
        ]
        + [pltpu.SemaphoreType.DMA((ITERS,))] * 8,
        compiler_params=pltpu.CompilerParams(
            collective_id=0, has_side_effects=True, vmem_limit_bytes=32 << 20
        ),
    )(acc)


def blend_kernel(
    count_x, count_y,
    acc_ref, x_ref, r_ref, flag_ref,
    vs, dg, rim, sums,
    row_out, row_in, col_out, col_in, part_y, part_x, got_y, got_x,
    row_s, row_r, col_s, col_r, y_s, y_r, x_s, x_r,
):
    me_x, me_y = lax.axis_index("gx"), lax.axis_index("gy")

    def at(dx, dy):
        return (lax.rem(me_x + dx + count_x, count_x), lax.rem(me_y + dy + count_y, count_y))

    barrier = pltpu.get_barrier_semaphore()

    def greet_y(d, carry):
        pl.semaphore_signal(barrier, inc=1, device_id=at(0, d), device_id_type=MESH)
        return carry

    def greet_x(d, carry):
        pl.semaphore_signal(barrier, inc=1, device_id=at(d, 0), device_id_type=MESH)
        return carry

    lax.fori_loop(1, count_y, greet_y, 0)
    lax.fori_loop(1, count_x, greet_x, 0)
    for dx in (-1, 1):
        for dy in (-1, 1):
            pl.semaphore_signal(barrier, inc=1, device_id=at(dx, dy), device_id_type=MESH)

    tiles_x = CX // TX
    sub8 = lax.broadcasted_iota(jnp.int32, (8, LANES), 0)
    lane8 = lax.broadcasted_iota(jnp.int32, (8, LANES), 1)
    lane_half = lax.broadcasted_iota(jnp.int32, (CX, LANES), 1)
    row_half = lax.broadcasted_iota(jnp.int32, (CX, LANES), 0)
    plane8 = lax.rem(lane8, CZ)
    zrow = lax.broadcasted_iota(jnp.int32, (CZ, CY), 0)
    yrow = lax.broadcasted_iota(jnp.int32, (CZ, CY), 1)
    zero8 = jnp.zeros((8, LANES), jnp.float32)

    for k in range(ITERS):
        vs[k, 0] = jnp.zeros((CX, CY), jnp.float32)
        vs[k, CZ + 1] = jnp.zeros((CX, CY), jnp.float32)

    def unfold(t, carry):
        rows = pl.ds(pl.multiple_of(t * TX, TX), TX)
        vs[0, 1 : CZ + 1, rows, :] = acc_ref[t, 0].T.reshape(CZ, TX, CY)
        dg[:, rows, :] = (6.75 - SHIFT) + screen_weight * acc_ref[t, 1].T.reshape(CZ, TX, CY)
        return carry

    lax.fori_loop(0, tiles_x, unfold, 0)

    def collect(z, t, left, right, west, east):
        shift = z + CZ * t
        mine = lane8 == shift
        west = jnp.where(mine, pltpu.roll(left, shift, 1), west)
        east = jnp.where(mine, pltpu.roll(right, lax.rem(shift + 1, LANES), 1), east)
        return west, east

    def first(z, carry):
        west, east, norm = carry
        for t in range(tiles_x):
            left = vs[0, z + 1, 8 * t : 8 * t + 8, :LANES]
            right = vs[0, z + 1, 8 * t : 8 * t + 8, LANES:]
            west, east = collect(z, t, left, right, west, east)
            norm = norm + left * left + right * right
        return west, east, norm

    west, east, norm = lax.fori_loop(0, CZ, first, (zero8, zero8, zero8), unroll=4)
    sums[0] = norm
    pl.semaphore_wait(barrier, (count_y - 1) + (count_x - 1) + 4)

    def ask(target, src, dst, send, recv):
        pltpu.make_async_remote_copy(
            src_ref=src, dst_ref=dst, send_sem=send, recv_sem=recv,
            device_id=target, device_id_type=MESH,
        ).start()

    def wait_for(ref, sem):
        pltpu.make_async_copy(ref, ref, sem).wait()

    def share(it, west, east, low, high):
        col_out[it, 0] = west
        col_out[it, 1] = east
        for dx in (-1, 1, 0):
            ask(at(dx, -1), col_out.at[it, 0], col_in.at[it, 1, 1 - dx], col_s.at[it], col_r.at[it])
            ask(at(dx, 1), col_out.at[it, 1], col_in.at[it, 0, 1 - dx], col_s.at[it], col_r.at[it])
        row_out[it, 0] = low
        row_out[it, 1] = high
        ask(at(-1, 0), row_out.at[it, 0], row_in.at[it, 1], row_s.at[it], row_r.at[it])
        ask(at(1, 0), row_out.at[it, 1], row_in.at[it, 0], row_s.at[it], row_r.at[it])

    share(0, west, east, vs[0, 1 : CZ + 1, 0, :], vs[0, 1 : CZ + 1, CX - 1, :])

    zcol = lax.broadcasted_iota(jnp.int32, (CZ, LANES), 0)
    lane_z = lax.broadcasted_iota(jnp.int32, (CZ, LANES), 1)

    def turn(it, carry):
        def inner(z, c):
            west, east = c
            halves = []
            for h in range(2):
                cols = slice(h * LANES, (h + 1) * LANES)
                u = vs[it, z, :, cols] + vs[it, z + 1, :, cols] + vs[it, z + 2, :, cols]
                halves.append(
                    u
                    + jnp.where(row_half == 0, 0.0, pltpu.roll(u, 1, 0))
                    + jnp.where(row_half == CX - 1, 0.0, pltpu.roll(u, CX - 1, 0))
                )
            left, right = halves
            lr, rr = pltpu.roll(left, 1, 1), pltpu.roll(right, 1, 1)
            ll, rl = pltpu.roll(left, LANES - 1, 1), pltpu.roll(right, LANES - 1, 1)
            start, last = lane_half == 0, lane_half == LANES - 1
            box_left = left + jnp.where(start, 0.0, lr) + jnp.where(last, rl, ll)
            box_right = right + jnp.where(start, lr, rr) + jnp.where(last, 0.0, rl)
            made = []
            for h, box in ((0, box_left), (1, box_right)):
                cols = slice(h * LANES, (h + 1) * LANES)
                value = dg[z, :, cols] * vs[it, z + 1, :, cols] - 0.25 * box
                vs[it + 1, z + 1, :, cols] = value
                made.append(value)
            for t in range(tiles_x):
                rows = slice(8 * t, 8 * t + 8)
                west, east = collect(z, t, made[0][rows], made[1][rows], west, east)
            return west, east

        west, east = lax.fori_loop(0, CZ, inner, (zero8, zero8), unroll=4)

        wait_for(row_in.at[it], row_r.at[it])
        for side, there in ((0, me_x > 0), (1, me_x < count_x - 1)):
            near = row_in[it, side]
            near = (
                near
                + jnp.where(zrow > 0, pltpu.roll(near, 1, 0), 0.0)
                + jnp.where(zrow < CZ - 1, pltpu.roll(near, CZ - 1, 0), 0.0)
            )
            near = (
                near
                + jnp.where(yrow > 0, pltpu.roll(near, 1, 1), 0.0)
                + jnp.where(yrow < CY - 1, pltpu.roll(near, CY - 1, 1), 0.0)
            )
            near = jnp.where(there, 0.25 * near, 0.0)
            rim[side, 0] = near[:, :LANES]
            rim[side, 1] = near[:, LANES:]
        wait_for(col_in.at[it], col_r.at[it])

        def column(side, there):
            def summed(k, ok):
                col = col_in[it, side, k]
                col = (
                    col
                    + jnp.where(plane8 > 0, pltpu.roll(col, 1, 1), 0.0)
                    + jnp.where(plane8 < CZ - 1, pltpu.roll(col, LANES - 1, 1), 0.0)
                )
                return jnp.where(ok, 0.25 * col, 0.0)

            mid = summed(1, there)
            low = summed(0, jnp.logical_and(there, me_x > 0))
            high = summed(2, jnp.logical_and(there, me_x < count_x - 1))

            def down(v):
                return pltpu.roll(v, 1, 0)

            def up(v):
                return pltpu.roll(v, 7, 0)

            before = jnp.where(lane8 < CZ, pltpu.roll(down(low), CZ, 1), pltpu.roll(down(mid), CZ, 1))
            before = jnp.where(sub8 == 0, before, down(mid))
            after = jnp.where(
                lane8 >= LANES - CZ,
                pltpu.roll(up(high), LANES - CZ, 1),
                pltpu.roll(up(mid), LANES - CZ, 1),
            )
            after = jnp.where(sub8 == 7, after, up(mid))
            return before + mid + after

        west_in = column(0, me_y > 0)
        east_in = column(1, me_y < count_y - 1)

        @pl.when(it < ITERS - 1)
        def _():
            def packed(side, h, lane, first):
                column = jnp.broadcast_to(rim[side, h, :, lane : lane + 1], (CZ, LANES))
                return jnp.sum(jnp.where(lane_z == zcol + first, column, 0.0), axis=0, keepdims=True)

            def spread(column, sub, first):
                row = jnp.broadcast_to(column[sub : sub + 1], (CZ, LANES))
                return jnp.sum(jnp.where(lane_z == zcol + first, row, 0.0), axis=1, keepdims=True)

            final = LANES - CZ

            def corners(column, fix, h, lane):
                return (
                    column
                    - fix
                    - jnp.where(sub8 == 0, packed(0, h, lane, 0), 0.0)
                    - jnp.where(sub8 == 7, packed(1, h, lane, final), 0.0)
                )

            def row(side, sub, first):
                near = vs[it + 1, 1 : CZ + 1, (CX - 1) * side, :]
                left = near[:, :LANES] - jnp.where(lane_z == 0, spread(west_in, sub, first), 0.0)
                right = near[:, LANES:] - jnp.where(lane_z == LANES - 1, spread(east_in, sub, first), 0.0)
                return jnp.concatenate([left - rim[side, 0], right - rim[side, 1]], axis=1)

            share(
                it + 1,
                corners(west, west_in, 0, 0),
                corners(east, east_in, 1, LANES - 1),
                row(0, 0, 0),
                row(1, 7, final),
            )

        def edge(z, carry):
            cross, norm = carry
            for t in range(tiles_x):
                rows = slice(8 * t, 8 * t + 8)
                shift = z + CZ * t
                fixes = [
                    jnp.where(lane8 == 0, pltpu.roll(west_in, lax.rem(2 * LANES - shift, LANES), 1), 0.0),
                    jnp.where(lane8 == LANES - 1, pltpu.roll(east_in, 2 * LANES - 1 - shift - LANES, 1), 0.0),
                ]
                for h in range(2):
                    cols = slice(h * LANES, (h + 1) * LANES)
                    value = vs[it + 1, z + 1, rows, cols] - fixes[h]
                    if t == 0:
                        value = value - jnp.where(sub8 == 0, rim[0, h, pl.ds(z, 1), :], 0.0)
                    if t == tiles_x - 1:
                        value = value - jnp.where(sub8 == 7, rim[1, h, pl.ds(z, 1), :], 0.0)
                    vs[it + 1, z + 1, rows, cols] = value
                    cross = cross + value * vs[it, z + 1, rows, cols]
                    norm = norm + value * value
            return cross, norm

        cross, norm = lax.fori_loop(0, CZ, edge, (zero8, zero8), unroll=4)
        sums[2 * it + 1] = cross
        sums[2 * it + 2] = norm
        return carry

    lax.fori_loop(0, ITERS, turn, 0)

    mine = zero8
    for k in range(2 * ITERS + 1):
        mine = jnp.where(sub8 == k, jnp.sum(sums[k], axis=0, keepdims=True), mine)
    part_y[...] = mine
    got_y[me_y] = mine

    def send_y(d, c):
        ask(at(0, d), part_y, got_y.at[me_y], y_s, y_r)
        return c

    lax.fori_loop(1, count_y, send_y, 0)
    wait_for(got_y.at[pl.ds(0, count_y - 1)], y_r)

    def total_of(parts):
        total = parts[0]
        for k in range(1, parts.shape[0]):
            total = total + parts[k]
        return total

    mine = total_of(got_y)
    part_x[...] = mine
    got_x[me_x] = mine

    def send_x(d, c):
        ask(at(d, 0), part_x, got_x.at[me_x], x_s, x_r)
        return c

    lax.fori_loop(1, count_x, send_x, 0)
    wait_for(got_x.at[pl.ds(0, count_x - 1)], x_r)
    total = jnp.sum(total_of(got_x), axis=1, keepdims=True)
    moment = [total[k : k + 1] for k in range(2 * ITERS + 1)]

    good = jnp.ones((1, 1), jnp.float32)

    def product(a, b, good):
        value, size = 0.0, 0.0
        for d in range(len(a) + len(b) - 1):
            pairs = [a[i] * b[d - i] for i in range(len(a)) if 0 <= d - i < len(b)]
            both = pairs[0]
            bulk = jnp.abs(pairs[0])
            for pair in pairs[1:]:
                both = both + pair
                bulk = bulk + jnp.abs(pair)
            value = value + both * moment[d]
            size = size + bulk * jnp.abs(moment[d])
        return value, jnp.where(size <= TRUST * value, good, 0.0)

    def image(a):
        padded = [SHIFT * c for c in a] + [None]
        return [
            (padded[i] if i == 0 else a[i - 1] if i == len(a) else padded[i] + a[i - 1])
            for i in range(len(a) + 1)
        ]

    def plus(a, factor, b):
        longest = max(len(a), len(b))
        made = []
        for i in range(longest):
            if i >= len(a):
                made.append(factor * b[i])
            elif i >= len(b):
                made.append(a[i])
            else:
                made.append(a[i] + factor * b[i])
        return made

    one = jnp.ones((1, 1), jnp.float32)
    residual, direction, answer = [one], [one], []
    gamma, good = product(residual, residual, good)
    for it in range(ITERS):
        curve, good = product(direction, image(direction), good)
        alpha = gamma / curve
        answer = plus(answer, alpha, direction)
        residual = plus(residual, -alpha, image(direction))
        fresh, good = product(residual, residual, good)
        direction = plus(residual, fresh / gamma, direction)
        gamma = fresh
    flag_ref[...] = good

    def combine(z, c):
        for h in range(2):
            cols = slice(h * LANES, (h + 1) * LANES)
            fields = [vs[k, z + 1, :, cols] for k in range(ITERS + 1)]
            x_ref[z, :, cols] = sum(answer[k] * fields[k] for k in range(ITERS))
            r_ref[z, :, cols] = sum(residual[k] * fields[k] for k in range(ITERS + 1))
        return c

    lax.fori_loop(0, CZ, combine, 0, unroll=2)

    def finish(it, c):
        wait_for(row_out.at[it], row_s.at[it])
        wait_for(col_in.at[it], col_s.at[it])
        return c

    lax.fori_loop(0, ITERS, finish, 0)
    wait_for(got_y.at[pl.ds(0, count_y - 1)], y_s)
    wait_for(got_x.at[pl.ds(0, count_x - 1)], x_s)


def blend(acc, count_x, count_y):
    vmem = pl.BlockSpec(memory_space=pltpu.VMEM)
    field = jax.ShapeDtypeStruct((CZ, CX, CY), jnp.float32)

    def kernel(*refs):
        blend_kernel(count_x, count_y, *refs)

    return pl.pallas_call(
        kernel,
        out_shape=(field, field, jax.ShapeDtypeStruct((1, 1), jnp.float32)),
        in_specs=[vmem],
        out_specs=(vmem, vmem, vmem),
        scratch_shapes=[
            pltpu.VMEM((ITERS + 1, CZ + 2, CX, CY), jnp.float32),
            pltpu.VMEM((CZ, CX, CY), jnp.float32),
            pltpu.VMEM((2, 2, CZ, LANES), jnp.float32),
            pltpu.VMEM((2 * ITERS + 1, 8, LANES), jnp.float32),
            pltpu.VMEM((ITERS, 2, CZ, CY), jnp.float32),
            pltpu.VMEM((ITERS, 2, CZ, CY), jnp.float32),
            pltpu.VMEM((ITERS, 2, 8, LANES), jnp.float32),
            pltpu.VMEM((ITERS, 2, 3, 8, LANES), jnp.float32),
            pltpu.VMEM((8, LANES), jnp.float32),
            pltpu.VMEM((8, LANES), jnp.float32),
            pltpu.VMEM((count_y, 8, LANES), jnp.float32),
            pltpu.VMEM((count_x, 8, LANES), jnp.float32),
        ]
        + [pltpu.SemaphoreType.DMA((ITERS,))] * 4
        + [pltpu.SemaphoreType.DMA] * 4,
        compiler_params=pltpu.CompilerParams(
            collective_id=1, has_side_effects=True, vmem_limit_bytes=32 << 20
        ),
    )(acc)


def local(fractions, normals, point_cells, block_owner, block_tile, block_count):
    count_x, count_y = lax.axis_size("gx"), lax.axis_size("gy")
    got = route(
        block_tile,
        block_count,
        block_owner.reshape(1, -1),
        jnp.transpose(fractions, (1, 0, 2)),
        jnp.transpose(normals, (1, 0, 2)),
        point_cells,
        count_x,
        count_y,
    )
    acc = splat(got)
    x, r, flag = blend(acc, count_x, count_y)
    return lax.cond(
        flag[0, 0] > 0.5,
        lambda acc, x, r: (x, r),
        lambda acc, x, r: tuple(solve(acc, count_x, count_y)),
        acc, x, r,
    )


def solution(mesh):
    placed = (
        P(("gx", "gy"), None, None),
        P(("gx", "gy"), None, None),
        P(("gx", "gy"), None),
        P(("gx", "gy"), None),
        P(("gx", "gy")),
        P(("gx", "gy")),
    )
    return jax.shard_map(
        local,
        mesh=mesh,
        in_specs=placed,
        out_specs=(P(None, "gx", "gy"), P(None, "gx", "gy")),
        check_vma=False,
    )
```

```python
import jax
import jax.numpy as jnp
from jax import lax
from jax.experimental import pallas as pl
from jax.experimental.pallas import tpu as pltpu
from jax.sharding import PartitionSpec as P

CX = 64
CY = 256
CZ = 16
TX = 8
TY = 16
POINTS = 128
ITERS = 3
LANES = 128
GROUP = 64
SHIFT = 6.5
STRIDE = 37
TRUST = 100.0

screen_weight = 4.0
MESH = pl.DeviceIdType.MESH


def route_kernel(
    count_x, count_y,
    tile_in, count_in, owner_in, frac_in, norm_in, cell_in, out_ref,
    tile_ref, count_ref, owner_ref, frac_ref, norm_ref, cell_ref,
    send, index_v, index_s, load_sem, copy_sem, send_sem, recv_sem,
):
    devices = count_x * count_y
    blocks = cell_ref.shape[0]
    loads = [
        pltpu.make_async_copy(source, target, load_sem.at[k])
        for k, (source, target) in enumerate(
            (
                (owner_in, owner_ref),
                (tile_in, tile_ref),
                (count_in, count_ref),
                (frac_in, frac_ref),
                (norm_in, norm_ref),
                (cell_in, cell_ref),
            )
        )
    ]
    for load in loads:
        load.start()
    me = lax.axis_index("gx") * count_y + lax.axis_index("gy")

    def place(d):
        flat = lax.rem(me + lax.rem(d * STRIDE, devices), devices)
        return flat, (flat // count_y, lax.rem(flat, count_y))

    barrier = pltpu.get_barrier_semaphore()

    def greet(d, carry):
        pl.semaphore_signal(barrier, inc=1, device_id=place(d)[1], device_id_type=MESH)
        return carry

    lax.fori_loop(1, devices, greet, 0)

    loads[0].wait()
    owner = jnp.broadcast_to(owner_ref[...], (devices, blocks)).T
    block = lax.broadcasted_iota(jnp.int32, (blocks, devices), 0)
    named = owner == lax.broadcasted_iota(jnp.int32, (blocks, devices), 1)
    first = jnp.min(jnp.where(named, block, blocks), axis=0, keepdims=True)
    last = jnp.max(jnp.where(named, block, -1), axis=0, keepdims=True)
    sub = lax.broadcasted_iota(jnp.int32, (8, devices), 0)
    index_v[...] = jnp.where(
        sub == 0,
        first,
        jnp.where(
            sub == 1,
            last,
            jnp.where(
                sub == 2,
                (last >= 0).astype(jnp.int32),
                (last > first).astype(jnp.int32),
            ),
        ),
    )
    fetch = pltpu.make_async_copy(index_v, index_s, copy_sem)
    fetch.start()
    for load in loads[1:]:
        load.wait()
    fetch.wait()

    lane = lax.broadcasted_iota(jnp.int32, (1, LANES), 1)

    def fill(o):
        for c in range(2):
            k = jnp.minimum(jnp.maximum(index_s[c, o], 0), blocks - 1)
            there = index_s[2 + c, o]
            slot = 2 * o + c
            for axis in range(3):
                send[slot, axis : axis + 1, :] = frac_ref[axis, pl.ds(k, 1), :]
                send[slot, 3 + axis : 4 + axis, :] = norm_ref[axis, pl.ds(k, 1), :]
            send[slot, 6:7, :] = cell_ref[pl.ds(k, 1), :].astype(jnp.float32)
            header = jnp.where(lane == 0, tile_ref[k], jnp.where(lane == 1, count_ref[k] * there, 0))
            send[slot, 7:8, :] = header.astype(jnp.float32)

    pl.semaphore_wait(barrier, devices - 1)

    def ship(d, carry):
        flat, target = place(d)
        fill(flat)
        pltpu.make_async_remote_copy(
            src_ref=send.at[pl.ds(2 * flat, 2)],
            dst_ref=out_ref.at[pl.ds(2 * me, 2)],
            send_sem=send_sem, recv_sem=recv_sem,
            device_id=target, device_id_type=MESH,
        ).start()
        return carry

    lax.fori_loop(1, devices, ship, 0)
    fill(me)
    keep = pltpu.make_async_copy(
        send.at[pl.ds(2 * me, 2)], out_ref.at[pl.ds(2 * me, 2)], copy_sem
    )
    keep.start()
    keep.wait()
    most = pl.ds(0, 2 * (devices - 1))
    pltpu.make_async_copy(out_ref.at[most], out_ref.at[most], recv_sem).wait()
    pltpu.make_async_copy(send.at[most], send.at[most], send_sem).wait()


def route(tile, count, owner, fractions, normals, cells, count_x, count_y):
    slots = 2 * count_x * count_y
    operands = (tile, count, owner, fractions, normals, cells)

    def kernel(*refs):
        route_kernel(count_x, count_y, *refs)

    return pl.pallas_call(
        kernel,
        out_shape=jax.ShapeDtypeStruct((slots, 8, LANES), jnp.float32),
        in_specs=[pl.BlockSpec(memory_space=pl.ANY)] * 6,
        out_specs=pl.BlockSpec(memory_space=pl.ANY),
        scratch_shapes=[pltpu.SMEM(tile.shape, tile.dtype), pltpu.SMEM(count.shape, count.dtype)]
        + [pltpu.VMEM(one.shape, one.dtype) for one in operands[2:]]
        + [
            pltpu.VMEM((slots, 8, LANES), jnp.float32),
            pltpu.VMEM((8, LANES), jnp.int32),
            pltpu.SMEM((8, LANES), jnp.int32),
            pltpu.SemaphoreType.DMA((6,)),
            pltpu.SemaphoreType.DMA,
            pltpu.SemaphoreType.DMA,
            pltpu.SemaphoreType.DMA,
        ],
        compiler_params=pltpu.CompilerParams(
            collective_id=2, has_side_effects=True, vmem_limit_bytes=56 << 20
        ),
    )(*operands)


def split(value):
    high = value.astype(jnp.bfloat16)
    return high, (value - high.astype(jnp.float32)).astype(jnp.bfloat16)


def taps(anchor, offset, length):
    place = lax.broadcasted_iota(jnp.int32, (length, POINTS), 0).astype(jnp.float32)
    lower = place == anchor
    upper = place == anchor + 1.0
    weight = jnp.where(lower, 1.0 - offset, jnp.where(upper, offset, 0.0))
    slope = jnp.where(lower, -1.0, jnp.where(upper, 1.0, 0.0))
    return weight, slope


def splat_tile(block, count):
    lane = lax.broadcasted_iota(jnp.int32, (1, POINTS), 1)
    cell = block[6:7]
    remains = jnp.floor((cell + 0.5) * (1.0 / (CZ - 1)))
    plane = cell - remains * (CZ - 1)
    row = jnp.floor((remains + 0.5) * (1.0 / (TY - 1)))
    column = remains - row * (TY - 1)
    row = jnp.where(lane < count, row, -4.0)
    wx, sx = taps(row, block[0:1], TX)
    wy, sy = taps(column, block[1:2], TY)
    sy = sy * block[4:5]
    fz = block[2:3]
    level = block[3:4] * sx
    rise = block[5:6] * wx
    pairs = (
        ((1.0 - fz) * level - rise, fz * level + rise),
        ((1.0 - fz) * wx, fz * wx),
    )
    at = jnp.broadcast_to(plane, (2 * TX, POINTS)).astype(jnp.bfloat16)
    place = (lax.broadcasted_iota(jnp.int32, (2 * TX, POINTS), 0) // TX).astype(jnp.float32).astype(jnp.bfloat16)
    offset = at - place
    zero = jnp.zeros((2 * TX, POINTS), jnp.bfloat16)
    high, low = [], []
    for lower, upper in pairs:
        lower = split(jnp.concatenate([lower, lower], axis=0))
        upper = split(jnp.concatenate([upper, upper], axis=0))
        for kept, under, over in zip((high, low), lower, upper):
            kept.append(
                jnp.concatenate(
                    [
                        jnp.where(offset == 2 * j, under, jnp.where(offset == 2 * j - 1, over, zero))
                        for j in range(CZ // 2)
                    ],
                    axis=0,
                )
            )
    big_high = jnp.concatenate(high, axis=1)
    big_low = jnp.concatenate(low, axis=1)
    top = jnp.concatenate([wy, sy], axis=1)
    low = jnp.concatenate([jnp.zeros_like(wy), wy], axis=1)
    small_high, small_low = split(jnp.concatenate([top, low], axis=0))
    both = lax.dot_general(
        jnp.concatenate([small_high, small_low], axis=0),
        jnp.concatenate([big_high, big_low], axis=0),
        (((1,), (1,)), ((), ())),
        preferred_element_type=jnp.float32,
    )
    return both[: 2 * TY, :POINTS] + both[2 * TY :, :POINTS] + both[: 2 * TY, POINTS:]


def splat_kernel(blocks_ref, acc_ref, blocks, header_v, header_s, order, sem):
    slots = blocks_ref.shape[0]
    load = pltpu.make_async_copy(blocks_ref, blocks, sem)
    load.start()
    acc_ref[...] = jnp.zeros_like(acc_ref)
    load.wait()
    header_v[...] = blocks[:, 7, :].T[:8].astype(jnp.int32)
    fetch = pltpu.make_async_copy(header_v, header_s, sem)
    fetch.start()
    fetch.wait()

    def gather(i, carry):
        used, empty = carry
        some = header_s[1, i] > 0
        order[used] = i
        return used + some.astype(jnp.int32), jnp.where(some, empty, i)

    used, empty = lax.fori_loop(
        0, slots, gather, (jnp.int32(0), jnp.int32(0)), unroll=8
    )
    for extra in range(GROUP):
        order[used + extra] = empty

    def work(j, carry):
        made = []
        for u in range(GROUP):
            slot = order[j * GROUP + u]
            made.append((header_s[0, slot], splat_tile(blocks[slot], header_s[1, slot])))
        tiles_y = CY // TY
        for tile, values in made:
            x = tile // tiles_y
            y = pl.multiple_of((tile % tiles_y) * TY, TY)
            acc_ref[x, 0, pl.ds(y, TY), :] += values[:TY]
            acc_ref[x, 1, pl.ds(y, TY), :] += values[TY:]
        return carry

    lax.fori_loop(0, (used + GROUP - 1) // GROUP, work, 0)


def splat(blocks):
    slots = blocks.shape[0]
    return pl.pallas_call(
        splat_kernel,
        out_shape=jax.ShapeDtypeStruct((CX // TX, 2, CY, CZ * TX), jnp.float32),
        in_specs=[pl.BlockSpec(memory_space=pl.ANY)],
        out_specs=pl.BlockSpec(memory_space=pltpu.VMEM),
        scratch_shapes=[
            pltpu.VMEM(blocks.shape, blocks.dtype),
            pltpu.VMEM((8, slots), jnp.int32),
            pltpu.SMEM((8, slots), jnp.int32),
            pltpu.SMEM((slots + GROUP,), jnp.int32),
            pltpu.SemaphoreType.DMA,
        ],
        compiler_params=pltpu.CompilerParams(vmem_limit_bytes=58 << 20),
    )(blocks)


def fold(value):
    total = value[0:8]
    for k in range(1, value.shape[0] // 8):
        total = total + value[8 * k : 8 * k + 8]
    return total


def solve_kernel(
    count_x, count_y,
    acc_ref, x_ref, r_ref,
    rp, dg, p, s, w, rim,
    row_out, row_in, col_out, col_in, part_y, part_x, got_y, got_x,
    row_s, row_r, col_s, col_r, y_s, y_r, x_s, x_r,
):
    me_x, me_y = lax.axis_index("gx"), lax.axis_index("gy")

    def at(dx, dy):
        return (lax.rem(me_x + dx + count_x, count_x), lax.rem(me_y + dy + count_y, count_y))

    barrier = pltpu.get_barrier_semaphore()

    def greet_y(d, carry):
        pl.semaphore_signal(barrier, inc=1, device_id=at(0, d), device_id_type=MESH)
        return carry

    def greet_x(d, carry):
        pl.semaphore_signal(barrier, inc=1, device_id=at(d, 0), device_id_type=MESH)
        return carry

    lax.fori_loop(1, count_y, greet_y, 0)
    lax.fori_loop(1, count_x, greet_x, 0)
    for dx in (-1, 1):
        for dy in (-1, 1):
            pl.semaphore_signal(barrier, inc=1, device_id=at(dx, dy), device_id_type=MESH)

    sub8 = lax.broadcasted_iota(jnp.int32, (8, LANES), 0)
    lane8 = lax.broadcasted_iota(jnp.int32, (8, LANES), 1)
    lane_half = lax.broadcasted_iota(jnp.int32, (CX, LANES), 1)
    row_half = lax.broadcasted_iota(jnp.int32, (CX, LANES), 0)

    rp[0] = jnp.zeros((CX, CY), jnp.float32)
    rp[CZ + 1] = jnp.zeros((CX, CY), jnp.float32)

    def unfold(t, carry):
        rows = pl.ds(pl.multiple_of(t * TX, TX), TX)
        source = acc_ref[t, 0].T.reshape(CZ, TX, CY)
        density = acc_ref[t, 1].T.reshape(CZ, TX, CY)
        rp[1 : CZ + 1, rows, :] = source
        dg[:, rows, :] = 6.75 + screen_weight * density
        return carry

    lax.fori_loop(0, CX // TX, unfold, 0)

    def clear(z, carry):
        zero = jnp.zeros((CX, CY), jnp.float32)
        p[z] = zero
        s[z] = zero
        x_ref[z] = zero
        return carry

    lax.fori_loop(0, CZ, clear, 0)
    pl.semaphore_wait(barrier, (count_y - 1) + (count_x - 1) + 4)

    def pack(z, carry):
        west, east = carry
        for t in range(CX // TX):
            here = rp[z + 1, 8 * t : 8 * t + 8, :]
            shift = z + CZ * t
            mine = lane8 == shift
            west = jnp.where(mine, pltpu.roll(here[:, :LANES], shift, 1), west)
            turned = pltpu.roll(here[:, LANES:], lax.rem(shift + 1, LANES), 1)
            east = jnp.where(mine, turned, east)
        return west, east

    def ask(count, target, src, dst, send, recv):
        pltpu.make_async_remote_copy(
            src_ref=src, dst_ref=dst, send_sem=send, recv_sem=recv,
            device_id=target, device_id_type=MESH,
        ).start()

    def wait_for(ref, sem):
        pltpu.make_async_copy(ref, ref, sem).wait()

    zero8 = jnp.zeros((8, LANES), jnp.float32)

    def total_of(parts):
        total = parts[0]
        for k in range(1, parts.shape[0]):
            total = total + parts[k]
        return total

    def turn(it, carry):
        gamma_old, curve_old = carry
        row_out[it, 0] = rp[1 : CZ + 1, 0, :]
        row_out[it, 1] = rp[1 : CZ + 1, CX - 1, :]
        ask(0, at(-1, 0), row_out.at[it, 0], row_in.at[it, 1], row_s.at[it], row_r.at[it])
        ask(0, at(1, 0), row_out.at[it, 1], row_in.at[it, 0], row_s.at[it], row_r.at[it])
        west, east = lax.fori_loop(0, CZ, pack, (zero8, zero8))
        col_out[it, 0] = west
        col_out[it, 1] = east
        for dx in (-1, 0, 1):
            ask(0, at(dx, -1), col_out.at[it, 0], col_in.at[it, 1, 1 - dx], col_s.at[it], col_r.at[it])
            ask(0, at(dx, 1), col_out.at[it, 1], col_in.at[it, 0, 1 - dx], col_s.at[it], col_r.at[it])

        wait_for(row_in.at[it], row_r.at[it])
        zrow = lax.broadcasted_iota(jnp.int32, (CZ, CY), 0)
        for side, there in ((0, me_x > 0), (1, me_x < count_x - 1)):
            near = row_in[it, side]
            near = (
                near
                + jnp.where(zrow > 0, pltpu.roll(near, 1, 0), 0.0)
                + jnp.where(zrow < CZ - 1, pltpu.roll(near, CZ - 1, 0), 0.0)
            )
            near = jnp.where(there, near, 0.0)
            rim[side, 0] = near[:, :LANES]
            rim[side, 1] = near[:, LANES:]
        wait_for(col_in.at[it], col_r.at[it])

        plane8 = lax.rem(lane8, CZ)

        def column(side, there):
            def summed(k, ok):
                col = col_in[it, side, k]
                col = (
                    col
                    + jnp.where(plane8 > 0, pltpu.roll(col, 1, 1), 0.0)
                    + jnp.where(plane8 < CZ - 1, pltpu.roll(col, LANES - 1, 1), 0.0)
                )
                return jnp.where(ok, col, 0.0)

            mid = summed(1, there)
            low = summed(0, jnp.logical_and(there, me_x > 0))
            high = summed(2, jnp.logical_and(there, me_x < count_x - 1))

            def down(v):
                return pltpu.roll(v, 1, 0)

            def up(v):
                return pltpu.roll(v, 7, 0)

            before = jnp.where(lane8 < CZ, pltpu.roll(down(low), CZ, 1), pltpu.roll(down(mid), CZ, 1))
            before = jnp.where(sub8 == 0, before, down(mid))
            after = jnp.where(
                lane8 >= LANES - CZ,
                pltpu.roll(up(high), LANES - CZ, 1),
                pltpu.roll(up(mid), LANES - CZ, 1),
            )
            after = jnp.where(sub8 == 7, after, up(mid))
            return before + mid + after

        west_in = column(0, me_y > 0)
        east_in = column(1, me_y < count_y - 1)

        def apply(z, sums):
            gamma, delta, eta = sums
            halves = []
            for h in range(2):
                cols = slice(h * LANES, (h + 1) * LANES)
                u = rp[z, :, cols] + rp[z + 1, :, cols] + rp[z + 2, :, cols]
                above = rim[0, h, pl.ds(z, 1), :]
                below = rim[1, h, pl.ds(z, 1), :]
                t = (
                    u
                    + jnp.where(row_half == 0, above, pltpu.roll(u, 1, 0))
                    + jnp.where(row_half == CX - 1, below, pltpu.roll(u, CX - 1, 0))
                )
                halves.append(t)
            left, right = halves
            back = lax.rem(2 * LANES - z, LANES)
            west_col = jnp.concatenate(
                [pltpu.roll(west_in, lax.rem(back + LANES - CZ * t, LANES), 1) for t in range(CX // TX)],
                axis=0,
            )
            east_col = jnp.concatenate(
                [pltpu.roll(east_in, lax.rem(back + 2 * LANES - 1 - CZ * t, LANES), 1) for t in range(CX // TX)],
                axis=0,
            )
            lr, rr = pltpu.roll(left, 1, 1), pltpu.roll(right, 1, 1)
            ll, rl = pltpu.roll(left, LANES - 1, 1), pltpu.roll(right, LANES - 1, 1)
            first, last = lane_half == 0, lane_half == LANES - 1
            box_left = left + jnp.where(first, west_col, lr) + jnp.where(last, rl, ll)
            box_right = right + jnp.where(first, lr, rr) + jnp.where(last, east_col, rl)
            for h, box in ((0, box_left), (1, box_right)):
                cols = slice(h * LANES, (h + 1) * LANES)
                v = rp[z + 1, :, cols]
                image = dg[z, :, cols] * v - 0.25 * box
                w[z, :, cols] = image
                gamma = gamma + fold(v * v)
                delta = delta + fold(v * image)
                eta = eta + fold(v * s[z, :, cols])
            return gamma, delta, eta

        gamma, delta, eta = lax.fori_loop(0, CZ, apply, (zero8, zero8, zero8))
        gamma = jnp.sum(gamma, axis=0, keepdims=True)
        delta = jnp.sum(delta, axis=0, keepdims=True)
        eta = jnp.sum(eta, axis=0, keepdims=True)
        mine = jnp.where(sub8 == 0, gamma, jnp.where(sub8 == 1, delta, jnp.where(sub8 == 2, eta, 0.0)))
        part_y[it] = mine
        got_y[it, me_y] = mine

        def send_y(d, c):
            ask(0, at(0, d), part_y.at[it], got_y.at[it, me_y], y_s.at[it], y_r.at[it])
            return c

        lax.fori_loop(1, count_y, send_y, 0)
        wait_for(got_y.at[it, pl.ds(0, count_y - 1)], y_r.at[it])
        mine = total_of(got_y.at[it])
        part_x[it] = mine
        got_x[it, me_x] = mine

        def send_x(d, c):
            ask(0, at(d, 0), part_x.at[it], got_x.at[it, me_x], x_s.at[it], x_r.at[it])
            return c

        lax.fori_loop(1, count_x, send_x, 0)
        wait_for(got_x.at[it, pl.ds(0, count_x - 1)], x_r.at[it])
        total = jnp.sum(total_of(got_x.at[it]), axis=1, keepdims=True)
        gamma, delta, eta = total[0:1], total[1:2], total[2:3]
        beta = jnp.where(it == 0, 0.0, gamma / gamma_old)
        curve = delta + 2.0 * beta * eta + beta * beta * curve_old
        alpha = gamma / curve

        def update(z, c):
            r = rp[z + 1]
            pn = r + beta * p[z]
            sn = w[z] + beta * s[z]
            p[z] = pn
            s[z] = sn
            x_ref[z] = x_ref[z] + alpha * pn
            r = r - alpha * sn
            rp[z + 1] = r
            r_ref[z] = r
            return c

        lax.fori_loop(0, CZ, update, 0)
        return gamma, curve

    one = jnp.ones((1, 1), jnp.float32)
    lax.fori_loop(0, ITERS, turn, (one, 0.0 * one))

    def finish(it, c):
        wait_for(row_out.at[it], row_s.at[it])
        wait_for(col_in.at[it], col_s.at[it])
        wait_for(got_y.at[it, pl.ds(0, count_y - 1)], y_s.at[it])
        wait_for(got_x.at[it, pl.ds(0, count_x - 1)], x_s.at[it])
        return c

    lax.fori_loop(0, ITERS, finish, 0)


def solve(acc, count_x, count_y):
    vmem = pl.BlockSpec(memory_space=pltpu.VMEM)
    field = jax.ShapeDtypeStruct((CZ, CX, CY), jnp.float32)
    cells = (CZ, CX, CY)

    def kernel(*refs):
        solve_kernel(count_x, count_y, *refs)

    return pl.pallas_call(
        kernel,
        out_shape=(field, field),
        in_specs=[vmem],
        out_specs=(vmem, vmem),
        scratch_shapes=[
            pltpu.VMEM((CZ + 2, CX, CY), jnp.float32),
            pltpu.VMEM(cells, jnp.float32),
            pltpu.VMEM(cells, jnp.float32),
            pltpu.VMEM(cells, jnp.float32),
            pltpu.VMEM(cells, jnp.float32),
            pltpu.VMEM((2, 2, CZ, LANES), jnp.float32),
            pltpu.VMEM((ITERS, 2, CZ, CY), jnp.float32),
            pltpu.VMEM((ITERS, 2, CZ, CY), jnp.float32),
            pltpu.VMEM((ITERS, 2, 8, LANES), jnp.float32),
            pltpu.VMEM((ITERS, 2, 3, 8, LANES), jnp.float32),
            pltpu.VMEM((ITERS, 8, LANES), jnp.float32),
            pltpu.VMEM((ITERS, 8, LANES), jnp.float32),
            pltpu.VMEM((ITERS, count_y, 8, LANES), jnp.float32),
            pltpu.VMEM((ITERS, count_x, 8, LANES), jnp.float32),
        ]
        + [pltpu.SemaphoreType.DMA((ITERS,))] * 8,
        compiler_params=pltpu.CompilerParams(
            collective_id=0, has_side_effects=True, vmem_limit_bytes=32 << 20
        ),
    )(acc)


def blend_kernel(
    count_x, count_y,
    acc_ref, x_ref, r_ref, flag_ref,
    vs, dg, rim, sums,
    row_out, row_in, col_out, col_in, part_y, part_x, got_y, got_x,
    row_s, row_r, col_s, col_r, y_s, y_r, x_s, x_r,
):
    me_x, me_y = lax.axis_index("gx"), lax.axis_index("gy")

    def at(dx, dy):
        return (lax.rem(me_x + dx + count_x, count_x), lax.rem(me_y + dy + count_y, count_y))

    barrier = pltpu.get_barrier_semaphore()

    def greet_y(d, carry):
        pl.semaphore_signal(barrier, inc=1, device_id=at(0, d), device_id_type=MESH)
        return carry

    def greet_x(d, carry):
        pl.semaphore_signal(barrier, inc=1, device_id=at(d, 0), device_id_type=MESH)
        return carry

    lax.fori_loop(1, count_y, greet_y, 0)
    lax.fori_loop(1, count_x, greet_x, 0)
    for dx in (-1, 1):
        for dy in (-1, 1):
            pl.semaphore_signal(barrier, inc=1, device_id=at(dx, dy), device_id_type=MESH)

    tiles_x = CX // TX
    sub8 = lax.broadcasted_iota(jnp.int32, (8, LANES), 0)
    lane8 = lax.broadcasted_iota(jnp.int32, (8, LANES), 1)
    lane_half = lax.broadcasted_iota(jnp.int32, (CX, LANES), 1)
    row_half = lax.broadcasted_iota(jnp.int32, (CX, LANES), 0)
    plane8 = lax.rem(lane8, CZ)
    zrow = lax.broadcasted_iota(jnp.int32, (CZ, CY), 0)
    yrow = lax.broadcasted_iota(jnp.int32, (CZ, CY), 1)
    zero8 = jnp.zeros((8, LANES), jnp.float32)

    for k in range(ITERS):
        vs[k, 0] = jnp.zeros((CX, CY), jnp.float32)
        vs[k, CZ + 1] = jnp.zeros((CX, CY), jnp.float32)

    def unfold(t, carry):
        rows = pl.ds(pl.multiple_of(t * TX, TX), TX)
        vs[0, 1 : CZ + 1, rows, :] = acc_ref[t, 0].T.reshape(CZ, TX, CY)
        dg[:, rows, :] = (6.75 - SHIFT) + screen_weight * acc_ref[t, 1].T.reshape(CZ, TX, CY)
        return carry

    lax.fori_loop(0, tiles_x, unfold, 0, unroll=4)

    def collect(z, t, left, right, west, east):
        shift = z + CZ * t
        mine = lane8 == shift
        west = jnp.where(mine, pltpu.roll(left, shift, 1), west)
        east = jnp.where(mine, pltpu.roll(right, lax.rem(shift + 1, LANES), 1), east)
        return west, east

    def first(z, carry):
        west, east, norm = carry
        for t in range(tiles_x):
            left = vs[0, z + 1, 8 * t : 8 * t + 8, :LANES]
            right = vs[0, z + 1, 8 * t : 8 * t + 8, LANES:]
            west, east = collect(z, t, left, right, west, east)
            norm = norm + left * left + right * right
        return west, east, norm

    west, east, norm = lax.fori_loop(0, CZ, first, (zero8, zero8, zero8), unroll=4)
    sums[0] = norm
    pl.semaphore_wait(barrier, (count_y - 1) + (count_x - 1) + 4)

    def ask(target, src, dst, send, recv):
        pltpu.make_async_remote_copy(
            src_ref=src, dst_ref=dst, send_sem=send, recv_sem=recv,
            device_id=target, device_id_type=MESH,
        ).start()

    def wait_for(ref, sem):
        pltpu.make_async_copy(ref, ref, sem).wait()

    def share(it, west, east, low, high):
        col_out[it, 0] = west
        col_out[it, 1] = east
        for dx in (-1, 1, 0):
            ask(at(dx, -1), col_out.at[it, 0], col_in.at[it, 1, 1 - dx], col_s.at[it], col_r.at[it])
            ask(at(dx, 1), col_out.at[it, 1], col_in.at[it, 0, 1 - dx], col_s.at[it], col_r.at[it])
        row_out[it, 0] = low
        row_out[it, 1] = high
        ask(at(-1, 0), row_out.at[it, 0], row_in.at[it, 1], row_s.at[it], row_r.at[it])
        ask(at(1, 0), row_out.at[it, 1], row_in.at[it, 0], row_s.at[it], row_r.at[it])

    share(0, west, east, vs[0, 1 : CZ + 1, 0, :], vs[0, 1 : CZ + 1, CX - 1, :])

    zcol = lax.broadcasted_iota(jnp.int32, (CZ, LANES), 0)
    lane_z = lax.broadcasted_iota(jnp.int32, (CZ, LANES), 1)

    def turn(it, carry):
        def inner(z, c):
            west, east = c
            halves = []
            for h in range(2):
                cols = slice(h * LANES, (h + 1) * LANES)
                u = vs[it, z, :, cols] + vs[it, z + 1, :, cols] + vs[it, z + 2, :, cols]
                halves.append(
                    u
                    + jnp.where(row_half == 0, 0.0, pltpu.roll(u, 1, 0))
                    + jnp.where(row_half == CX - 1, 0.0, pltpu.roll(u, CX - 1, 0))
                )
            left, right = halves
            lr, rr = pltpu.roll(left, 1, 1), pltpu.roll(right, 1, 1)
            ll, rl = pltpu.roll(left, LANES - 1, 1), pltpu.roll(right, LANES - 1, 1)
            start, last = lane_half == 0, lane_half == LANES - 1
            box_left = left + jnp.where(start, 0.0, lr) + jnp.where(last, rl, ll)
            box_right = right + jnp.where(start, lr, rr) + jnp.where(last, 0.0, rl)
            made = []
            for h, box in ((0, box_left), (1, box_right)):
                cols = slice(h * LANES, (h + 1) * LANES)
                value = dg[z, :, cols] * vs[it, z + 1, :, cols] - 0.25 * box
                vs[it + 1, z + 1, :, cols] = value
                made.append(value)
            for t in range(tiles_x):
                rows = slice(8 * t, 8 * t + 8)
                west, east = collect(z, t, made[0][rows], made[1][rows], west, east)
            return west, east

        west, east = lax.fori_loop(0, CZ, inner, (zero8, zero8), unroll=4)

        wait_for(row_in.at[it], row_r.at[it])
        for side, there in ((0, me_x > 0), (1, me_x < count_x - 1)):
            near = row_in[it, side]
            near = (
                near
                + jnp.where(zrow > 0, pltpu.roll(near, 1, 0), 0.0)
                + jnp.where(zrow < CZ - 1, pltpu.roll(near, CZ - 1, 0), 0.0)
            )
            near = (
                near
                + jnp.where(yrow > 0, pltpu.roll(near, 1, 1), 0.0)
                + jnp.where(yrow < CY - 1, pltpu.roll(near, CY - 1, 1), 0.0)
            )
            near = jnp.where(there, 0.25 * near, 0.0)
            rim[side, 0] = near[:, :LANES]
            rim[side, 1] = near[:, LANES:]
        wait_for(col_in.at[it], col_r.at[it])

        def column(side, there):
            def summed(k, ok):
                col = col_in[it, side, k]
                col = (
                    col
                    + jnp.where(plane8 > 0, pltpu.roll(col, 1, 1), 0.0)
                    + jnp.where(plane8 < CZ - 1, pltpu.roll(col, LANES - 1, 1), 0.0)
                )
                return jnp.where(ok, 0.25 * col, 0.0)

            mid = summed(1, there)
            low = summed(0, jnp.logical_and(there, me_x > 0))
            high = summed(2, jnp.logical_and(there, me_x < count_x - 1))

            def down(v):
                return pltpu.roll(v, 1, 0)

            def up(v):
                return pltpu.roll(v, 7, 0)

            before = jnp.where(lane8 < CZ, pltpu.roll(down(low), CZ, 1), pltpu.roll(down(mid), CZ, 1))
            before = jnp.where(sub8 == 0, before, down(mid))
            after = jnp.where(
                lane8 >= LANES - CZ,
                pltpu.roll(up(high), LANES - CZ, 1),
                pltpu.roll(up(mid), LANES - CZ, 1),
            )
            after = jnp.where(sub8 == 7, after, up(mid))
            return before + mid + after

        west_in = column(0, me_y > 0)
        east_in = column(1, me_y < count_y - 1)

        @pl.when(it < ITERS - 1)
        def _():
            def packed(side, h, lane, first):
                column = jnp.broadcast_to(rim[side, h, :, lane : lane + 1], (CZ, LANES))
                return jnp.sum(jnp.where(lane_z == zcol + first, column, 0.0), axis=0, keepdims=True)

            def spread(column, sub, first):
                row = jnp.broadcast_to(column[sub : sub + 1], (CZ, LANES))
                return jnp.sum(jnp.where(lane_z == zcol + first, row, 0.0), axis=1, keepdims=True)

            final = LANES - CZ

            def corners(column, fix, h, lane):
                return (
                    column
                    - fix
                    - jnp.where(sub8 == 0, packed(0, h, lane, 0), 0.0)
                    - jnp.where(sub8 == 7, packed(1, h, lane, final), 0.0)
                )

            def row(side, sub, first):
                near = vs[it + 1, 1 : CZ + 1, (CX - 1) * side, :]
                left = near[:, :LANES] - jnp.where(lane_z == 0, spread(west_in, sub, first), 0.0)
                right = near[:, LANES:] - jnp.where(lane_z == LANES - 1, spread(east_in, sub, first), 0.0)
                return jnp.concatenate([left - rim[side, 0], right - rim[side, 1]], axis=1)

            share(
                it + 1,
                corners(west, west_in, 0, 0),
                corners(east, east_in, 1, LANES - 1),
                row(0, 0, 0),
                row(1, 7, final),
            )

        def edge(z, carry):
            cross, norm = carry
            for t in range(tiles_x):
                rows = slice(8 * t, 8 * t + 8)
                shift = z + CZ * t
                fixes = [
                    jnp.where(lane8 == 0, pltpu.roll(west_in, lax.rem(2 * LANES - shift, LANES), 1), 0.0),
                    jnp.where(lane8 == LANES - 1, pltpu.roll(east_in, 2 * LANES - 1 - shift - LANES, 1), 0.0),
                ]
                for h in range(2):
                    cols = slice(h * LANES, (h + 1) * LANES)
                    value = vs[it + 1, z + 1, rows, cols] - fixes[h]
                    if t == 0:
                        value = value - jnp.where(sub8 == 0, rim[0, h, pl.ds(z, 1), :], 0.0)
                    if t == tiles_x - 1:
                        value = value - jnp.where(sub8 == 7, rim[1, h, pl.ds(z, 1), :], 0.0)
                    vs[it + 1, z + 1, rows, cols] = value
                    cross = cross + value * vs[it, z + 1, rows, cols]
                    norm = norm + value * value
            return cross, norm

        cross, norm = lax.fori_loop(0, CZ, edge, (zero8, zero8), unroll=4)
        sums[2 * it + 1] = cross
        sums[2 * it + 2] = norm
        return carry

    lax.fori_loop(0, ITERS, turn, 0)

    mine = zero8
    for k in range(2 * ITERS + 1):
        mine = jnp.where(sub8 == k, jnp.sum(sums[k], axis=0, keepdims=True), mine)
    part_y[...] = mine
    got_y[me_y] = mine

    def send_y(d, c):
        ask(at(0, d), part_y, got_y.at[me_y], y_s, y_r)
        return c

    lax.fori_loop(1, count_y, send_y, 0)
    wait_for(got_y.at[pl.ds(0, count_y - 1)], y_r)

    def total_of(parts):
        total = parts[0]
        for k in range(1, parts.shape[0]):
            total = total + parts[k]
        return total

    mine = total_of(got_y)
    part_x[...] = mine
    got_x[me_x] = mine

    def send_x(d, c):
        ask(at(d, 0), part_x, got_x.at[me_x], x_s, x_r)
        return c

    lax.fori_loop(1, count_x, send_x, 0)
    wait_for(got_x.at[pl.ds(0, count_x - 1)], x_r)
    total = jnp.sum(total_of(got_x), axis=1, keepdims=True)
    moment = [total[k : k + 1] for k in range(2 * ITERS + 1)]

    good = jnp.ones((1, 1), jnp.float32)

    def product(a, b, good):
        value, size = 0.0, 0.0
        for d in range(len(a) + len(b) - 1):
            pairs = [a[i] * b[d - i] for i in range(len(a)) if 0 <= d - i < len(b)]
            both = pairs[0]
            bulk = jnp.abs(pairs[0])
            for pair in pairs[1:]:
                both = both + pair
                bulk = bulk + jnp.abs(pair)
            value = value + both * moment[d]
            size = size + bulk * jnp.abs(moment[d])
        return value, jnp.where(size <= TRUST * value, good, 0.0)

    def image(a):
        padded = [SHIFT * c for c in a] + [None]
        return [
            (padded[i] if i == 0 else a[i - 1] if i == len(a) else padded[i] + a[i - 1])
            for i in range(len(a) + 1)
        ]

    def plus(a, factor, b):
        longest = max(len(a), len(b))
        made = []
        for i in range(longest):
            if i >= len(a):
                made.append(factor * b[i])
            elif i >= len(b):
                made.append(a[i])
            else:
                made.append(a[i] + factor * b[i])
        return made

    one = jnp.ones((1, 1), jnp.float32)
    residual, direction, answer = [one], [one], []
    gamma, good = product(residual, residual, good)
    for it in range(ITERS):
        curve, good = product(direction, image(direction), good)
        alpha = gamma / curve
        answer = plus(answer, alpha, direction)
        residual = plus(residual, -alpha, image(direction))
        fresh, good = product(residual, residual, good)
        direction = plus(residual, fresh / gamma, direction)
        gamma = fresh
    flag_ref[...] = good

    def combine(z, c):
        for h in range(2):
            cols = slice(h * LANES, (h + 1) * LANES)
            fields = [vs[k, z + 1, :, cols] for k in range(ITERS + 1)]
            x_ref[z, :, cols] = sum(answer[k] * fields[k] for k in range(ITERS))
            r_ref[z, :, cols] = sum(residual[k] * fields[k] for k in range(ITERS + 1))
        return c

    lax.fori_loop(0, CZ, combine, 0, unroll=2)

    def finish(it, c):
        wait_for(row_out.at[it], row_s.at[it])
        wait_for(col_in.at[it], col_s.at[it])
        return c

    lax.fori_loop(0, ITERS, finish, 0)
    wait_for(got_y.at[pl.ds(0, count_y - 1)], y_s)
    wait_for(got_x.at[pl.ds(0, count_x - 1)], x_s)


def blend(acc, count_x, count_y):
    vmem = pl.BlockSpec(memory_space=pltpu.VMEM)
    field = jax.ShapeDtypeStruct((CZ, CX, CY), jnp.float32)

    def kernel(*refs):
        blend_kernel(count_x, count_y, *refs)

    return pl.pallas_call(
        kernel,
        out_shape=(field, field, jax.ShapeDtypeStruct((1, 1), jnp.float32)),
        in_specs=[vmem],
        out_specs=(vmem, vmem, vmem),
        scratch_shapes=[
            pltpu.VMEM((ITERS + 1, CZ + 2, CX, CY), jnp.float32),
            pltpu.VMEM((CZ, CX, CY), jnp.float32),
            pltpu.VMEM((2, 2, CZ, LANES), jnp.float32),
            pltpu.VMEM((2 * ITERS + 1, 8, LANES), jnp.float32),
            pltpu.VMEM((ITERS, 2, CZ, CY), jnp.float32),
            pltpu.VMEM((ITERS, 2, CZ, CY), jnp.float32),
            pltpu.VMEM((ITERS, 2, 8, LANES), jnp.float32),
            pltpu.VMEM((ITERS, 2, 3, 8, LANES), jnp.float32),
            pltpu.VMEM((8, LANES), jnp.float32),
            pltpu.VMEM((8, LANES), jnp.float32),
            pltpu.VMEM((count_y, 8, LANES), jnp.float32),
            pltpu.VMEM((count_x, 8, LANES), jnp.float32),
        ]
        + [pltpu.SemaphoreType.DMA((ITERS,))] * 4
        + [pltpu.SemaphoreType.DMA] * 4,
        compiler_params=pltpu.CompilerParams(
            collective_id=1, has_side_effects=True, vmem_limit_bytes=32 << 20
        ),
    )(acc)


def local(fractions, normals, point_cells, block_owner, block_tile, block_count):
    count_x, count_y = lax.axis_size("gx"), lax.axis_size("gy")
    got = route(
        block_tile,
        block_count,
        block_owner.reshape(1, -1),
        jnp.transpose(fractions, (1, 0, 2)),
        jnp.transpose(normals, (1, 0, 2)),
        point_cells,
        count_x,
        count_y,
    )
    acc = splat(got)
    x, r, flag = blend(acc, count_x, count_y)
    return lax.cond(
        flag[0, 0] > 0.5,
        lambda acc, x, r: (x, r),
        lambda acc, x, r: tuple(solve(acc, count_x, count_y)),
        acc, x, r,
    )


def solution(mesh):
    placed = (
        P(("gx", "gy"), None, None),
        P(("gx", "gy"), None, None),
        P(("gx", "gy"), None),
        P(("gx", "gy"), None),
        P(("gx", "gy")),
        P(("gx", "gy")),
    )
    return jax.shard_map(
        local,
        mesh=mesh,
        in_specs=placed,
        out_specs=(P(None, "gx", "gy"), P(None, "gx", "gy")),
        check_vma=False,
    )
```
